128 devices in a mesh: pipe: 2 (over core), dp: 16 (over x, y), tensor: 4 (over z).
Axes of the slice: x: 4, y: 4, z: 4, core: 2. Of those that a mesh axis runs over, the one named last changes fastest.
Arguments:
- inputs: bfloat16 [2, 8192, 1024], P(None, ('dp', 'tensor')), may hold values from -6 to 6
- upstream: bfloat16 [2, 8192, 1024], P(None, ('dp', 'tensor')), may hold values from -16 to 16
- segments: int32 [2, 8192], P(None, 'dp'), may hold values from 0 to 4, as said below
- joint_weight: bfloat16 [2, 1024, 3, 1024], P('pipe', 'dp', None, 'tensor'), may hold values from -0.1875 to 0.1875
- joint_bias: bfloat16 [2, 3, 4, 256], P('pipe', None, 'tensor', 'dp'), may hold values from -1.25 to 1.25
- output_weight: bfloat16 [2, 1024, 1024], P('pipe', 'tensor', 'dp'), may hold values from -1 to 1
- expand_weight: bfloat16 [2, 1024, 4096], P('pipe', 'dp', 'tensor'), may hold values from -0.1875 to 0.1875
- expand_bias: bfloat16 [2, 4, 1024], P('pipe', 'tensor', 'dp'), may hold values from -1.75 to 1.75
- shrink_weight: bfloat16 [2, 4096, 1024], P('pipe', 'tensor', 'dp'), may hold values from -0.09375 to 0.09375
- norm_gains: bfloat16 [2, 2, 1024], P('pipe', None, 'dp'), may hold values from 0.25 to 1.75
- shift_rows: bfloat16 [2, 4, 1024], P('pipe', None, 'dp'), may hold values from -1.75 to 1.75
Outputs:
- boundary: float32 [2, 2, 8192, 1024], P('pipe', None, ('dp', 'tensor'))
- joint_weight_grad: float32 [2, 1024, 3, 1024], P('pipe', 'dp', None, 'tensor')
- joint_bias_grad: float32 [2, 3, 4, 256], P('pipe', None, 'tensor', 'dp')
- output_weight_grad: float32 [2, 1024, 1024], P('pipe', 'tensor', 'dp')
- expand_weight_grad: float32 [2, 1024, 4096], P('pipe', 'dp', 'tensor')
- expand_bias_grad: float32 [2, 4, 1024], P('pipe', 'tensor', 'dp')
- shrink_weight_grad: float32 [2, 4096, 1024], P('pipe', 'tensor', 'dp')
- norm_gains_grad: float32 [2, 2, 1024], P('pipe', None, 'dp')
- shift_rows_grad: float32 [2, 4, 1024], P('pipe', None, 'dp')
The draws below stay inside these ranges and needn't reach their ends.
Inputs may be any that keep to these rules, and one draw needn't show every extreme that they name: `segments`: within each block of 512 tokens the numbers never fall, and every number from the least to the most occurs.
All inputs are finite; a program needn't handle non-finite values.
Results may differ from the reference program's by a relative error of at most 0.024.
Values may be sent and summed in bfloat16 or wider, within the bound.
No kernel may reach another device: no remote copies, remote signals or barrier semaphores. Data moves between devices by JAX's collectives and lax.ppermute only.
A program may use at most 256 MiB of HBM per device.

```python
import math
import jax
import jax.numpy as jnp
from jax import lax

D = 1024
HEADS = 16
HEAD_DIM = 64
ROTARY = 16
FF = 4096
MICRO = 2
PACK = 512
TOKENS = 8192
N_DP = 16
N_TENSOR = 4


def draw_segments(key, part):
    key = jax.random.fold_in(key, 11)
    pack_count = MICRO * TOKENS // PACK
    quarter = PACK // 4
    key_one, key_two, key_three, key_four = jax.random.split(key, 4)
    start_cut = jax.random.randint(key_one, (pack_count, 1), 2, quarter)
    lead_cut = jax.random.randint(key_two, (pack_count, 1), 1, start_cut)
    long_end = jax.random.randint(key_three, (pack_count, 1), PACK - quarter + 1, PACK - 2)
    tail_cut = jax.random.randint(key_four, (pack_count, 1), long_end + 1, PACK)
    positions = jnp.arange(PACK, dtype=jnp.int32)[None, :]
    numbers = (positions >= lead_cut).astype(jnp.int32) + (positions >= start_cut).astype(jnp.int32)
    numbers = numbers + (positions >= long_end).astype(jnp.int32) + (positions >= tail_cut).astype(jnp.int32)
    return numbers.reshape(MICRO, TOKENS)


def with_spikes(values, stream_key, source, target, shards_of, factor):
    owner, partner = [(jnp.arange(values.shape[position]) // (values.shape[position] // shards_of)).reshape([-1 if axis == position else 1 for axis in range(values.ndim)]) for position in (source, target)]
    chosen = jax.random.permutation(stream_key, shards_of)[partner]
    strong = (owner == chosen) | (owner == (partner + shards_of // 2) % shards_of)
    return jnp.where(strong, factor * values, values)


def levels(own_key, extent, cuts, smallest, high):
    level, own = 1.0, jax.random.fold_in(own_key, 6)
    for position, blocks in cuts:
        steps = jnp.exp(jax.random.uniform(jax.random.fold_in(own, position), (blocks,), jnp.float32, smallest / len(cuts), high / len(cuts)))
        level = level * jnp.repeat(steps, extent[position] // blocks).reshape([-1 if axis == position else 1 for axis in range(len(extent))])
    return level


def normal_values(rng, shape, width, bound, shards=(), kind=jnp.bfloat16):
    array = width * jax.random.normal(rng, shape, jnp.float32)
    if shards:
        array = array * levels(rng, shape, shards, -0.22, 0.18)
    return jnp.clip(array, -bound, bound).astype(kind)


def heavy_noise(own_key, shape, scale, limit, cuts, heavy, held_as=jnp.bfloat16):
    entries = scale * jax.random.normal(own_key, shape, jnp.float32)
    if cuts:
        entries = entries * levels(own_key, shape, cuts, -0.22, 0.18)
    return jnp.clip(with_spikes(entries, jax.random.fold_in(own_key, 3), *heavy), -limit, limit).astype(held_as)


def setup_inputs(seed: int = 0) -> dict:
    keys = jax.random.split(jax.random.key(seed), 12)
    return {
        "inputs": normal_values(keys[0], (MICRO, TOKENS, D), 1.0, 6.0, ((1, 64),)),
        "upstream": heavy_noise(keys[1], (MICRO, TOKENS, D), 1.0, 16.0, ((1, 64),), (1, 2, 64, 4.0)),
        "segments": draw_segments(jax.random.fold_in(keys[11], 71), 0),
        "joint_weight": normal_values(keys[3], (2, D, 3, D), D ** -0.5, 0.1875, ((0, 2), (1, 16), (3, 4))),
        "joint_bias": normal_values(keys[4], (2, 3, N_TENSOR, D // N_TENSOR), 0.2, 1.25, ((0, 2), (2, 4), (3, 16))),
        "output_weight": normal_values(keys[5], (2, D, D), (D // 32) ** -0.5, 1.0, ((0, 2), (1, 4), (2, 16))),
        "expand_weight": normal_values(keys[6], (2, D, FF), D ** -0.5, 0.1875, ((0, 2), (1, 16), (2, 4))),
        "expand_bias": normal_values(keys[7], (2, N_TENSOR, FF // N_TENSOR), 0.3, 1.75, ((0, 2), (1, 4), (2, 16))),
        "shrink_weight": normal_values(keys[8], (2, FF, D), FF ** -0.5, 0.09375, ((0, 2), (1, 4), (2, 16))),
        "norm_gains": jnp.clip(1.0 + 0.15 * jax.random.normal(keys[9], (2, 2, D), jnp.float32), 0.25, 1.75).astype(jnp.bfloat16),
        "shift_rows": normal_values(keys[10], (2, 4, D), 0.3, 1.75, ((0, 2), (2, 16))),
    }


@jax.custom_vjp
def low(v):
    return lax.optimization_barrier(v.astype(jnp.bfloat16)).astype(jnp.float32)

@jax.custom_vjp
def low_back(v):
    return v

def low_keep(v):
    return (low(v), None)

def low_pass(kept, grad):
    return (grad,)

def back_keep(v):
    return (v, None)

def back_low(kept, grad):
    return (low(grad),)
low.defvjp(low_keep, low_pass)
low_back.defvjp(back_keep, back_low)
EPS = 1e-05
HIGH = lax.Precision.HIGHEST
block_rows = 512

def norm_rows(stream, gain_row, shift_row):
    centre = lax.optimization_barrier(jnp.mean(stream, axis=-1, keepdims=True))
    centred = stream - centre
    spread = lax.optimization_barrier(jnp.mean(centred * centred, axis=-1, keepdims=True))
    return centred * lax.rsqrt(spread + EPS) * gain_row + shift_row

def rotary_tables(segment_row):
    row_count = segment_row.shape[0]
    places = jnp.arange(row_count, dtype=jnp.int32)
    before = lax.optimization_barrier(jnp.sum((segment_row[None, :] < segment_row[:, None]).astype(jnp.int32), axis=1))
    positions = (places - before).astype(jnp.float32)
    half_rot = ROTARY // 2
    inverse = 10000.0 ** (-jnp.arange(half_rot, dtype=jnp.float32) * 2.0 / ROTARY)
    angles = positions[:, None] * inverse[None, :]
    angles = jnp.concatenate([angles, angles], axis=1)
    return (jnp.cos(angles), jnp.sin(angles))

def rotate(values, cosine, sine_rows):
    half_rot = ROTARY // 2
    front_part = values[..., :ROTARY]
    turned = jnp.concatenate([-front_part[..., half_rot:], front_part[..., :half_rot]], axis=-1)
    front_part = front_part * cosine[..., None, :] + turned * sine_rows[..., None, :]
    return jnp.concatenate([front_part, values[..., ROTARY:]], axis=-1)

def attend_pack(operands):
    queries, key_rows, value_rows, segment_row = operands
    row_count = queries.shape[0]
    step_rows = min(block_rows, row_count)
    score_scale = 1.0 / math.sqrt(HEAD_DIM)
    key_index = jnp.arange(row_count, dtype=jnp.int32)

    def one_block(block_index):
        begin_row = (block_index * step_rows).astype(jnp.int32)
        query_part = lax.dynamic_slice_in_dim(queries, begin_row, step_rows, 0)
        query_segs = lax.dynamic_slice_in_dim(segment_row, begin_row, step_rows, 0)
        query_index = begin_row + jnp.arange(step_rows, dtype=jnp.int32)
        scores = jnp.einsum('qhd,khd->hqk', query_part, key_rows, precision=HIGH) * score_scale
        scores = low_back(scores)
        allowed = (query_segs[:, None] == segment_row[None, :]) & (key_index[None, :] <= query_index[:, None])
        scores = jnp.where(allowed[None], scores, -1e+30)
        row_top = lax.optimization_barrier(jnp.max(scores, axis=-1, keepdims=True))
        raised = jnp.exp(scores - row_top)
        probs_low = low(raised / lax.optimization_barrier(jnp.sum(raised, axis=-1, keepdims=True)))
        return jnp.einsum('hqk,khd->qhd', probs_low, value_rows, precision=HIGH)
    outputs = lax.map(jax.checkpoint(one_block), jnp.arange(row_count // step_rows, dtype=jnp.int32))
    return outputs.reshape(row_count, queries.shape[1], queries.shape[2])

def layer(stream, weight_set, cosine, sine_rows, seg_rows):
    joint_w, joint_b, output_w, expand_w, expand_b, shrink_w, gain_rows, shift_all = weight_set
    pack_count, row_count, model_width = stream.shape
    total_rows = pack_count * row_count
    normed = low(norm_rows(stream, gain_rows[0], shift_all[0])).reshape(total_rows, model_width)
    mixed_norm = low(norm_rows(stream, gain_rows[1], shift_all[1])).reshape(total_rows, model_width)
    joint = jnp.dot(normed, joint_w.reshape(model_width, 3 * model_width), precision=HIGH) + joint_b.reshape(3 * model_width)
    joint = low_back(joint).reshape(pack_count, row_count, 3, HEADS, HEAD_DIM)
    queries = low(rotate(joint[:, :, 0], cosine, sine_rows))
    key_rows = low(rotate(joint[:, :, 1], cosine, sine_rows))
    value_rows = low(joint[:, :, 2])
    attended = lax.map(attend_pack, (queries, key_rows, value_rows, seg_rows))
    attended = low_back(low(attended)).reshape(total_rows, model_width)
    hidden = low_back(jnp.dot(mixed_norm, expand_w, precision=HIGH) + expand_b.reshape(-1))
    active_rows = low(jax.nn.gelu(hidden, approximate=False))
    branch = jnp.dot(attended, output_w, precision=HIGH) + jnp.dot(active_rows, shrink_w, precision=HIGH)
    branch = low_back(branch).reshape(pack_count, row_count, model_width)
    return stream + branch + shift_all[2] + shift_all[3]

def reference(inputs, upstream, segments, joint_weight, joint_bias, output_weight, expand_weight, expand_bias, shrink_weight, norm_gains, shift_rows):
    pack_count = MICRO * N_DP
    seg_rows = segments.reshape(pack_count, PACK)
    cosine, sine_rows = lax.map(rotary_tables, seg_rows)
    stream = inputs.astype(jnp.float32).reshape(pack_count, PACK, D)
    params = tuple((weight_arg.astype(jnp.float32) for weight_arg in (joint_weight, joint_bias, output_weight, expand_weight, expand_bias, shrink_weight, norm_gains, shift_rows)))

    def forward(stream_in, weight_all):
        middle = layer(stream_in, tuple((weight_arg[0] for weight_arg in weight_all)), cosine, sine_rows, seg_rows)
        middle = low_back(low(middle))
        return layer(middle, tuple((weight_arg[1] for weight_arg in weight_all)), cosine, sine_rows, seg_rows)
    result, pull_back = jax.vjp(forward, stream, params)
    d_stream, d_params = pull_back(upstream.astype(jnp.float32).reshape(pack_count, PACK, D))
    boundary = jnp.stack([d_stream.reshape(MICRO, TOKENS, D), result.reshape(MICRO, TOKENS, D)])
    return (boundary, d_params[0], d_params[1], d_params[2], d_params[3], d_params[4], d_params[5], d_params[6], d_params[7])
```

```python
import functools

import jax
import jax.numpy as jnp
from jax import lax
from jax.experimental import pallas as pl
from jax.experimental.pallas import tpu as pltpu
from jax.sharding import PartitionSpec as P

HEAD_DIM = 64
ROTARY = 16
EPS = 1e-05

MODEL = 1024
ROWS = 512
CHUNK = 256
WIDTH = 128
INNER = 512
HALF = MODEL // 2

QKV = 3 * WIDTH
COL_E = QKV
COL_O = QKV + INNER
COL_S = COL_O + WIDTH
COLS = COL_S + INNER

F32 = jnp.float32
BF16 = jnp.bfloat16


def nn(a, b):
    return lax.dot_general(a, b, (((1,), (0,)), ((), ())), preferred_element_type=F32)


def nt(a, b):
    return lax.dot_general(a, b, (((1,), (1,)), ((), ())), preferred_element_type=F32)


def tn(a, b):
    return lax.dot_general(a, b, (((0,), (0,)), ((), ())), preferred_element_type=F32)


def normalised(x):
    centred = x - jnp.mean(x, axis=1, keepdims=True)
    rstd = lax.rsqrt(jnp.mean(centred * centred, axis=1, keepdims=True) + EPS)
    return centred * rstd, rstd


def gelu_both(h):
    a = jnp.abs(h) * 0.7071067811865476
    t = 1.0 / (1.0 + 0.3275911 * a)
    poly = 1.061405429 * t - 1.453152027
    poly = poly * t + 1.421413741
    poly = poly * t - 0.284496736
    poly = poly * t + 0.254829592
    e = jnp.exp(-0.5 * h * h)
    tail = 0.5 * poly * t * e
    cdf = jnp.where(h >= 0, 1.0 - tail, tail)
    return h * cdf, cdf + h * (e * 0.3989422804014327)


def head_mask(v, head):
    lane = lax.broadcasted_iota(jnp.int32, v.shape, 1)
    return jnp.where((lane >= HEAD_DIM) == (head == 1), v, jnp.zeros_like(v))


def turn(u, c, s1, s2):
    return u * c + pltpu.roll(u, WIDTH - 8, 1) * s1 + pltpu.roll(u, 8, 1) * s2


def turn_back(w, c, s1, s2):
    return w * c + pltpu.roll(w * s2, WIDTH - 8, 1) + pltpu.roll(w * s1, 8, 1)


def allowed(i, seg_col, seg_row):
    keys = (i + 1) * CHUNK
    shape = (CHUNK, keys)
    q_at = lax.broadcasted_iota(jnp.int32, shape, 0) + i * CHUNK
    k_at = lax.broadcasted_iota(jnp.int32, shape, 1)
    same = seg_col[i * CHUNK : keys, :] == seg_row[:, :keys]
    return same & (k_at <= q_at)


def store_parts(first, rows, value, keep, send):
    low, high = value[:, :HALF].astype(BF16), value[:, HALF:].astype(BF16)

    @pl.when(first)
    def _():
        keep[rows, :] = low
        send[rows, :] = high

    @pl.when(jnp.logical_not(first))
    def _():
        keep[rows, :] = high
        send[rows, :] = low


def forward_rows(x_of, w, sm, bq, be, tabs, normed, mixed, q, k, v, active, slope):
    for i in range(ROWS // CHUNK):
        rows = slice(i * CHUNK, (i + 1) * CHUNK)
        xhat, _ = normalised(x_of(rows))
        normed[rows, :] = (xhat * sm[0:1, :] + sm[2:3, :]).astype(BF16)
        mixed[rows, :] = (xhat * sm[1:2, :] + sm[3:4, :]).astype(BF16)
        joint = nn(normed[rows, :], w[:, :QKV]) + bq[...]
        c, s1, s2 = tabs[0, rows, :], tabs[1, rows, :], tabs[2, rows, :]
        q[rows, :] = turn(joint[:, :WIDTH], c, s1, s2).astype(BF16)
        k[rows, :] = turn(joint[:, WIDTH : 2 * WIDTH], c, s1, s2).astype(BF16)
        v[rows, :] = joint[:, 2 * WIDTH :].astype(BF16)
        hidden = nn(mixed[rows, :], w[:, COL_E:COL_O]) + be[...]
        act, dact = gelu_both(hidden)
        active[rows, :] = act.astype(BF16)
        slope[rows, :] = dact.astype(slope.dtype)


def attend(q, k, v, seg_col, seg_row, att, lse):
    for i in range(ROWS // CHUNK):
        rows = slice(i * CHUNK, (i + 1) * CHUNK)
        keys = slice(0, (i + 1) * CHUNK)
        mask = allowed(i, seg_col[...], seg_row[...])
        out, tops = None, []
        for head in range(2):
            s = nt(head_mask(q[rows, :], head) * 0.125, k[keys, :])
            s = jnp.where(mask, s, -1e30)
            top = jnp.max(s, axis=1, keepdims=True)
            e = jnp.exp(s - top)
            total = jnp.sum(e, axis=1, keepdims=True)
            probs = (e * (1.0 / total)).astype(BF16)
            part = nn(probs, head_mask(v[keys, :], head))
            out = part if out is None else out + part
            tops.append(top + jnp.log(total))
        att[rows, :] = out.astype(BF16)
        lane = lax.broadcasted_iota(jnp.int32, (CHUNK, WIDTH), 1)
        lse[rows, :] = jnp.where(lane < HEAD_DIM, tops[0], tops[1])


def branch_out(first, w, att, active, keep, send):
    for i in range(ROWS // CHUNK):
        rows = slice(i * CHUNK, (i + 1) * CHUNK)
        branch = nt(att[rows, :], w[:, COL_O:COL_S]) + nt(active[rows, :], w[:, COL_S:])
        store_parts(first, rows, branch, keep, send)


def backward_rows(
    first, x_of, gy_of, w, sm, tabs, seg_col, seg_row, q, k, v, lse, slope,
    gatt, gk, gv, gq, gjoint, ghid, keep, send, sums,
):
    for i in range(ROWS // CHUNK):
        rows = slice(i * CHUNK, (i + 1) * CHUNK)
        gy = gy_of(rows)
        gatt[rows, :] = nn(gy, w[:, COL_O:COL_S]).astype(BF16)
        gact = nn(gy, w[:, COL_S:])
        ghid[rows, :] = (gact * slope[rows, :].astype(F32)).astype(BF16)
    gk[...] = jnp.zeros_like(gk)
    gv[...] = jnp.zeros_like(gv)
    for i in range(ROWS // CHUNK):
        rows = slice(i * CHUNK, (i + 1) * CHUNK)
        keys = slice(0, (i + 1) * CHUNK)
        mask = allowed(i, seg_col[...], seg_row[...])
        out = None
        for head in range(2):
            qh = head_mask(q[rows, :], head) * 0.125
            gh = head_mask(gatt[rows, :], head)
            s = nt(qh, k[keys, :])
            at = head * HEAD_DIM
            probs = jnp.where(mask, jnp.exp(s - lse[rows, at : at + 1]), 0.0)
            gp = nt(gh, v[keys, :])
            dot = jnp.sum(probs * gp, axis=1, keepdims=True)
            gs = (probs * (gp - dot)).astype(BF16)
            part = nn(gs, head_mask(k[keys, :], head) * 0.125)
            out = part if out is None else out + part
            gk[keys, :] += tn(gs, qh)
            gv[keys, :] += tn(probs.astype(BF16), gh)
        gq[rows, :] = out
    total = [None] * 6
    for i in range(ROWS // CHUNK):
        rows = slice(i * CHUNK, (i + 1) * CHUNK)
        c, s1, s2 = tabs[0, rows, :], tabs[1, rows, :], tabs[2, rows, :]
        gjoint[rows, :WIDTH] = turn_back(gq[rows, :], c, s1, s2).astype(BF16)
        gjoint[rows, WIDTH : 2 * WIDTH] = turn_back(gk[rows, :], c, s1, s2).astype(BF16)
        gjoint[rows, 2 * WIDTH :] = gv[rows, :].astype(BF16)
        gj, gh = gjoint[rows, :], ghid[rows, :]
        gn = nt(gj, w[:, :QKV])
        gm = nt(gh, w[:, COL_E:COL_O])
        xhat, rstd = normalised(x_of(rows))
        h = gn * sm[0:1, :] + gm * sm[1:2, :]
        gx = h - jnp.mean(h, axis=1, keepdims=True)
        gx = (gx - xhat * jnp.mean(h * xhat, axis=1, keepdims=True)) * rstd
        store_parts(first, rows, gx, keep, send)
        found = (
            jnp.sum(gn * xhat, axis=0, keepdims=True),
            jnp.sum(gm * xhat, axis=0, keepdims=True),
            jnp.sum(gn, axis=0, keepdims=True),
            jnp.sum(gm, axis=0, keepdims=True),
            jnp.sum(gy_of(rows).astype(F32), axis=0, keepdims=True),
            jnp.concatenate(
                [
                    jnp.sum(gj.astype(F32), axis=0, keepdims=True),
                    jnp.sum(gh.astype(F32), axis=0, keepdims=True),
                    jnp.zeros((1, MODEL - QKV - INNER), F32),
                ],
                axis=1,
            ),
        )
        total = [a if t is None else t + a for t, a in zip(total, found)]
    for n, t in enumerate(total):
        sums[n : n + 1, :] = t
    sums[6:8, :] = jnp.zeros((2, MODEL), F32)


def joined(first, a, b, rows):
    return jnp.where(
        first,
        jnp.concatenate([a[rows, :], b[rows, :]], axis=1),
        jnp.concatenate([b[rows, :], a[rows, :]], axis=1),
    )


def first_forward(
    core, x, w, sm, bq, be, tabs, seg_col, seg_row,
    keep, send, normed, mixed, q, k, v, att, lse, active, slope,
):
    first = core[0] == 0
    forward_rows(
        lambda rows: x[rows, :].astype(F32), w, sm, bq, be, tabs, normed, mixed, q, k, v, active, slope
    )
    attend(q, k, v, seg_col, seg_row, att, lse)
    branch_out(first, w, att, active, keep, send)


def both_ways(
    core, xa, xb, gy, w, sm, bq, be, tabs, seg_col, seg_row,
    keep_y, send_y, keep_g, send_g, normed, mixed, att, active, gjoint, ghid, sums,
    x, q, k, v, lse, slope, gatt, gk, gv, gq,
):
    first = core[0] == 0
    x[...] = joined(first, xa, xb, slice(None))
    x_of = lambda rows: x[rows, :].astype(F32)
    forward_rows(x_of, w, sm, bq, be, tabs, normed, mixed, q, k, v, active, slope)
    attend(q, k, v, seg_col, seg_row, att, lse)
    backward_rows(
        first, x_of, lambda rows: gy[rows, :], w, sm, tabs, seg_col, seg_row, q, k, v, lse, slope,
        gatt, gk, gv, gq, gjoint, ghid, keep_g, send_g, sums,
    )
    branch_out(first, w, att, active, keep_y, send_y)


def first_backward(
    core, x, ga, gb, w, sm, tabs, seg_col, seg_row, q, k, v, lse, slope,
    keep_g, send_g, gjoint, ghid, gy, sums,
    gatt, gk, gv, gq,
):
    first = core[0] == 0
    gy[...] = joined(first, ga, gb, slice(None))
    backward_rows(
        first, lambda rows: x[rows, :].astype(F32), lambda rows: gy[rows, :], w, sm, tabs,
        seg_col, seg_row, q, k, v, lse, slope, gatt, gk, gv, gq, gjoint, ghid, keep_g, send_g, sums,
    )


def weight_grads(n0, n1, m0, m1, g0, g1, j0, j1, h0, h1, a0, a1, c0, c1, out):
    out[:, :QKV] = (tn(n0[...], j0[...]) + tn(n1[...], j1[...])).astype(BF16)
    out[:, COL_E:COL_O] = (tn(m0[...], h0[...]) + tn(m1[...], h1[...])).astype(BF16)
    out[:, COL_O:COL_S] = (tn(g0[...], a0[...]) + tn(g1[...], a1[...])).astype(BF16)
    out[:, COL_S:] = (tn(g0[...], c0[...]) + tn(g1[...], c1[...])).astype(BF16)


def shaped(*dims, dtype=BF16):
    return jax.ShapeDtypeStruct(dims, dtype)


def call(kernel, n_in, outs, scratch, flops, name):
    whole = pl.BlockSpec(memory_space=pltpu.VMEM)
    return pl.pallas_call(
        kernel,
        in_specs=[pl.BlockSpec(memory_space=pltpu.SMEM)] + [whole] * (n_in - 1),
        out_specs=[whole] * len(outs),
        out_shape=outs,
        scratch_shapes=scratch,
        compiler_params=pltpu.CompilerParams(vmem_limit_bytes=60 * 2**20),
        cost_estimate=pl.CostEstimate(flops=flops, bytes_accessed=8 * 2**20, transcendentals=2**20),
        name=name,
    )


def tall(width, dtype=BF16):
    return shaped(ROWS, width, dtype=dtype)


def forward_call(*args):
    outs = [tall(HALF), tall(HALF), tall(MODEL), tall(MODEL)]
    outs += [tall(WIDTH)] * 4 + [tall(WIDTH, F32), tall(INNER), tall(INNER)]
    return call(first_forward, len(args), outs, [], 2**31, "layer_forward")(*args)


def both_call(*args):
    outs = [tall(HALF)] * 4 + [tall(MODEL)] * 2 + [tall(WIDTH), tall(INNER), tall(QKV), tall(INNER)]
    outs += [shaped(8, MODEL, dtype=F32)]
    scratch = [pltpu.VMEM((ROWS, MODEL), BF16)] + [pltpu.VMEM((ROWS, WIDTH), BF16)] * 3
    scratch += [pltpu.VMEM((ROWS, WIDTH), F32), pltpu.VMEM((ROWS, INNER), F32)]
    scratch += [pltpu.VMEM((ROWS, WIDTH), BF16)] + [pltpu.VMEM((ROWS, WIDTH), F32)] * 3
    return call(both_ways, len(args), outs, scratch, 2**32, "layer_both")(*args)


def backward_call(*args):
    outs = [tall(HALF)] * 2 + [tall(QKV), tall(INNER), tall(MODEL), shaped(8, MODEL, dtype=F32)]
    scratch = [pltpu.VMEM((ROWS, WIDTH), BF16)] + [pltpu.VMEM((ROWS, WIDTH), F32)] * 3
    return call(first_backward, len(args), outs, scratch, 2**31, "layer_backward")(*args)


def grads_call(*args):
    blocks = 4
    step = MODEL // blocks
    cut = pl.BlockSpec((ROWS, step), lambda i: (0, i))
    rest = [pl.BlockSpec(a.shape, lambda i: (0, 0)) for a in args[6:]]
    return pl.pallas_call(
        weight_grads,
        grid=(blocks,),
        in_specs=[cut] * 6 + rest,
        out_specs=pl.BlockSpec((step, COLS), lambda i: (i, 0)),
        out_shape=shaped(MODEL, COLS),
        compiler_params=pltpu.CompilerParams(vmem_limit_bytes=60 * 2**20),
        cost_estimate=pl.CostEstimate(flops=2**32, bytes_accessed=2**23, transcendentals=0),
        name="weight_grads",
    )(*args)


def swap(x):
    return lax.ppermute(x, "pipe", [(0, 1), (1, 0)])


def z_scatter(x):
    return lax.all_to_all(x, "tensor", split_axis=0, concat_axis=0, tiled=True)


def z_gather(x):
    copies = jnp.broadcast_to(x, (lax.axis_size("tensor"), *x.shape))
    arrived = lax.all_to_all(copies, "tensor", split_axis=0, concat_axis=0, tiled=True)
    return arrived.reshape(-1, *x.shape[1:])


def summed_rows(keep, send):
    both = (keep.astype(F32) + swap(send).astype(F32)).astype(BF16)
    tiles = both.reshape(lax.axis_size("tensor"), -1, HALF)
    return z_scatter(tiles).astype(F32).sum(axis=0)


def spread_rows(own):
    mine = z_gather(own)
    return mine, swap(mine)


def rotary_tables(segment_row):
    places = jnp.arange(ROWS, dtype=jnp.int32)
    before = jnp.sum((segment_row[None, :] < segment_row[:, None]).astype(jnp.int32), axis=1)
    positions = (places - before).astype(F32)
    half_rot = ROTARY // 2
    inverse = 10000.0 ** (-jnp.arange(half_rot, dtype=F32) * 2.0 / ROTARY)
    angles = positions[:, None] * inverse[None, :]
    cosine, sine = jnp.cos(angles), jnp.sin(angles)
    rest = HEAD_DIM - ROTARY
    ones, none = jnp.ones((ROWS, rest), F32), jnp.zeros((ROWS, rest), F32)
    zero = jnp.zeros_like(sine)
    c = jnp.concatenate([cosine, cosine, ones] * 2, axis=1)
    s1 = jnp.concatenate([-sine, zero, none] * 2, axis=1)
    s2 = jnp.concatenate([zero, sine, none] * 2, axis=1)
    return jnp.stack([c, s1, s2])


def shards(
    inputs, upstream, segments, joint_weight, joint_bias, output_weight, expand_weight,
    expand_bias, shrink_weight, norm_gains, shift_rows,
):
    dp = lax.axis_size("dp")
    tensor = lax.axis_size("tensor")
    core = lax.axis_index("pipe")
    first = core == 0
    core_arg = core.astype(jnp.int32).reshape(1)
    micros = inputs.shape[0]
    own_d = MODEL // dp

    def pick(a, b):
        return jnp.where(first, a, b)

    def packed(h):
        return jnp.concatenate(
            [
                joint_weight[0][:, :, h * WIDTH : (h + 1) * WIDTH].reshape(own_d, QKV),
                expand_weight[0][:, h * INNER : (h + 1) * INNER],
                output_weight[0][h * WIDTH : (h + 1) * WIDTH].T,
                shrink_weight[0][h * INNER : (h + 1) * INNER].T,
            ],
            axis=1,
        )

    with jax.named_scope("weights"):
        pack_a, pack_b = packed(0), packed(1)
        stay = pick(pack_a, pack_b)
        came = swap(pick(pack_b, pack_a))
        w0 = lax.all_gather(pick(stay, came), "dp", axis=0, tiled=True)
        w1 = lax.all_gather(pick(came, stay), "dp", axis=0, tiled=True)

    with jax.named_scope("small_parameters"):
        bias_row = jnp.pad(joint_bias[0, :, 0, :].reshape(1, -1), ((0, 0), (0, own_d - 3 * 16)))
        small = jnp.concatenate([norm_gains[0], shift_rows[0], expand_bias[0], bias_row], axis=0)
        copies = jnp.broadcast_to(small, (2 * dp, *small.shape))
        small = lax.all_to_all(copies, ("pipe", "dp"), split_axis=0, concat_axis=0, tiled=True)
        small = small.reshape(2, dp, 8, own_d).astype(F32)
        rows = small.transpose(0, 2, 1, 3).reshape(2, 8, MODEL)
        be = [pick(rows[n, 6:7, :INNER], rows[n, 6:7, INNER:]) for n in range(2)]
        bq_all = small[:, :, 7, :48].reshape(2, dp, 3, 16).transpose(0, 2, 1, 3).reshape(2, 3, 256)
        bq = [
            pick(bq_all[n, :, :WIDTH], bq_all[n, :, WIDTH:]).reshape(1, QKV) for n in range(2)
        ]
        shift_own = [pick(rows[n, :, :HALF], rows[n, :, HALF:]) for n in range(2)]

    with jax.named_scope("activations_in"):

        def everywhere(a):
            mine = z_gather(pick(a[0], a[1]))
            other = swap(mine)
            return [pick(mine, other), pick(other, mine)]

        x0 = everywhere(inputs)
        gy1 = everywhere(upstream)
        x0_own = [pick(inputs[m, :, :HALF], inputs[m, :, HALF:]).astype(F32) for m in range(micros)]
        g1_own = [
            pick(upstream[m, :, :HALF], upstream[m, :, HALF:]).astype(F32) for m in range(micros)
        ]

    with jax.named_scope("tables"):
        tabs = [rotary_tables(segments[m]) for m in range(micros)]
        seg_col = [segments[m].reshape(ROWS, 1) for m in range(micros)]
        seg_row = [segments[m].reshape(1, ROWS) for m in range(micros)]

    kept, x1_own, x1 = [], [], []
    for m in range(micros):
        with jax.named_scope("first_layer"):
            keep, send, *saved = forward_call(
                core_arg, x0[m], w0, rows[0], bq[0], be[0], tabs[m], seg_col[m], seg_row[m]
            )
            total = summed_rows(keep, send)
            total = x0_own[m] + total + shift_own[0][4:5] + shift_own[0][5:6]
            x1_own.append(total.astype(BF16))
            x1.append(spread_rows(x1_own[m]))
            kept.append(saved)

    made1, y_own, g0_own, g0 = [], [], [], []
    for m in range(micros):
        with jax.named_scope("second_layer"):
            keep_y, send_y, keep_g, send_g, *made = both_call(
                core_arg, *x1[m], gy1[m], w1, rows[1], bq[1], be[1], tabs[m], seg_col[m], seg_row[m]
            )
            g0_own.append((g1_own[m] + summed_rows(keep_g, send_g)).astype(BF16))
            g0.append(spread_rows(g0_own[m]))
            total = x1_own[m].astype(F32) + summed_rows(keep_y, send_y)
            y_own.append(total + shift_own[1][4:5] + shift_own[1][5:6])
            made1.append(made)

    def weight_sum(grads):
        tiles = grads.reshape(dp, own_d, COLS)
        arrived = lax.all_to_all(tiles, "dp", split_axis=0, concat_axis=0, tiled=True)
        return arrived.astype(F32).sum(axis=0)

    def pairs(made, n):
        return [made[m][n] for m in range(micros)]

    with jax.named_scope("second_layer_grads"):
        order = (0, 1, None, 4, 5, 2, 3)
        args = []
        for n in order:
            args += gy1 if n is None else pairs(made1, n)
        sum1 = weight_sum(grads_call(*args))

    made0, gx_own = [], []
    for m in range(micros):
        with jax.named_scope("first_layer_back"):
            normed, mixed, q, k, v, att, lse, active, slope = kept[m]
            keep_g, send_g, gjoint, ghid, gy, sums = backward_call(
                core_arg, x0[m], *g0[m], w0, rows[0], tabs[m], seg_col[m], seg_row[m],
                q, k, v, lse, slope,
            )
            gx_own.append(g0_own[m].astype(F32) + summed_rows(keep_g, send_g))
            made0.append((normed, mixed, att, active, gjoint, ghid, sums, gy))

    with jax.named_scope("first_layer_grads"):
        args = []
        for n in (0, 1, 7, 4, 5, 2, 3):
            args += pairs(made0, n)
        sum0 = weight_sum(grads_call(*args))

    with jax.named_scope("boundary"):
        y_all, gx_all = jnp.stack(y_own), jnp.stack(gx_own)
        other = swap(pick(y_all, gx_all))
        boundary = pick(
            jnp.concatenate([gx_all, other], axis=2), jnp.concatenate([other, y_all], axis=2)
        )[None]

    with jax.named_scope("small_grads"):
        sums = jnp.stack([made0[0][6] + made0[1][6], made1[0][6] + made1[1][6]])
        by_owner = sums[:, :5].reshape(2, 5, dp, own_d).transpose(2, 0, 1, 3)
        zero = jnp.zeros((2, HALF), F32)
        hid = sums[:, 5, QKV : QKV + INNER]
        hid = pick(jnp.concatenate([hid, zero], 1), jnp.concatenate([zero, hid], 1))
        hid = hid.reshape(2, 1, dp, own_d).transpose(2, 0, 1, 3)
        jb = sums[:, 5, :QKV].reshape(2, 3, WIDTH)
        zero = jnp.zeros_like(jb)
        jb = pick(jnp.concatenate([jb, zero], 2), jnp.concatenate([zero, jb], 2))
        jb = jb.reshape(2, 3, dp, 16).transpose(2, 0, 1, 3).reshape(dp, 2, 1, 48)
        jb = jnp.pad(jb, ((0, 0), (0, 0), (0, 0), (0, own_d - 48)))
        sent = jnp.concatenate([by_owner, hid, jb], axis=2)
        sent = lax.all_to_all(sent, "dp", split_axis=0, concat_axis=0, tiled=True).sum(axis=0)
        sent = jnp.broadcast_to(sent, (2 * tensor, *sent.shape))
        got = lax.all_to_all(sent, ("pipe", "tensor"), split_axis=0, concat_axis=0, tiled=True)
        got = jnp.where(first, got[:, 0], got[:, 1])
        every = got.sum(axis=0)
        z = lax.axis_index("tensor")
        here = got.reshape(2, tensor, *got.shape[1:]).sum(axis=0)
        here = lax.dynamic_index_in_dim(here, z, 0, keepdims=False)
        gains = every[None, 0:2]
        shift = jnp.stack([every[2], every[3], here[4] * 0.5, here[4] * 0.5])[None]
        expand_bias_grad = here[5].reshape(1, 1, own_d)
        joint_bias_grad = here[6, :48].reshape(1, 3, 1, 16)

    with jax.named_scope("outputs"):
        other = swap(pick(sum1, sum0))
        low = pick(sum0, other)
        high = pick(other, sum1)
        joint = jnp.concatenate(
            [low[:, :QKV].reshape(own_d, 3, WIDTH), high[:, :QKV].reshape(own_d, 3, WIDTH)], axis=2
        )[None]
        expand = jnp.concatenate([low[:, COL_E:COL_O], high[:, COL_E:COL_O]], axis=1)[None]
        output = jnp.concatenate([low[:, COL_O:COL_S], high[:, COL_O:COL_S]], axis=1).T[None]
        shrink = jnp.concatenate([low[:, COL_S:], high[:, COL_S:]], axis=1).T[None]

    return (
        boundary,
        joint,
        joint_bias_grad,
        output,
        expand,
        expand_bias_grad,
        shrink,
        gains,
        shift,
    )


def solution(mesh):
    placed = (
        P(None, ("dp", "tensor"), None),
        P(None, ("dp", "tensor"), None),
        P(None, "dp"),
        P("pipe", "dp", None, "tensor"),
        P("pipe", None, "tensor", "dp"),
        P("pipe", "tensor", "dp"),
        P("pipe", "dp", "tensor"),
        P("pipe", "tensor", "dp"),
        P("pipe", "tensor", "dp"),
        P("pipe", None, "dp"),
        P("pipe", None, "dp"),
    )
    return jax.shard_map(
        shards,
        mesh=mesh,
        in_specs=placed,
        out_specs=(
            P("pipe", None, ("dp", "tensor"), None),
            P("pipe", "dp", None, "tensor"),
            P("pipe", None, "tensor", "dp"),
            P("pipe", "tensor", "dp"),
            P("pipe", "dp", "tensor"),
            P("pipe", "tensor", "dp"),
            P("pipe", "tensor", "dp"),
            P("pipe", None, "dp"),
            P("pipe", None, "dp"),
        ),
        check_vma=False,
    )
```

```python
import functools

import jax
import jax.numpy as jnp
from jax import lax
from jax.experimental import pallas as pl
from jax.experimental.pallas import tpu as pltpu
from jax.sharding import PartitionSpec as P

HEAD_DIM = 64
ROTARY = 16
EPS = 1e-05

MODEL = 1024
ROWS = 512
CHUNK = 256
WIDTH = 128
INNER = 512
HALF = MODEL // 2

QKV = 3 * WIDTH
COL_E = QKV
COL_O = QKV + INNER
COL_S = COL_O + WIDTH
COLS = COL_S + INNER

F32 = jnp.float32
BF16 = jnp.bfloat16


def nn(a, b):
    return lax.dot_general(a, b, (((1,), (0,)), ((), ())), preferred_element_type=F32)


def nt(a, b):
    return lax.dot_general(a, b, (((1,), (1,)), ((), ())), preferred_element_type=F32)


def tn(a, b):
    return lax.dot_general(a, b, (((0,), (0,)), ((), ())), preferred_element_type=F32)


def normalised(x):
    centred = x - jnp.mean(x, axis=1, keepdims=True)
    rstd = lax.rsqrt(jnp.mean(centred * centred, axis=1, keepdims=True) + EPS)
    return centred * rstd, rstd


def gelu_both(h):
    a = jnp.abs(h) * 0.7071067811865476
    t = 1.0 / (1.0 + 0.3275911 * a)
    poly = 1.061405429 * t - 1.453152027
    poly = poly * t + 1.421413741
    poly = poly * t - 0.284496736
    poly = poly * t + 0.254829592
    e = jnp.exp(-0.5 * h * h)
    tail = 0.5 * poly * t * e
    cdf = jnp.where(h >= 0, 1.0 - tail, tail)
    return h * cdf, cdf + h * (e * 0.3989422804014327)


def head_mask(v, head):
    lane = lax.broadcasted_iota(jnp.int32, v.shape, 1)
    return jnp.where((lane >= HEAD_DIM) == (head == 1), v, jnp.zeros_like(v))


def turn(u, c, s1, s2):
    return u * c + pltpu.roll(u, WIDTH - 8, 1) * s1 + pltpu.roll(u, 8, 1) * s2


def turn_back(w, c, s1, s2):
    return w * c + pltpu.roll(w * s2, WIDTH - 8, 1) + pltpu.roll(w * s1, 8, 1)


def allowed(i, seg_col, seg_row):
    keys = (i + 1) * CHUNK
    shape = (CHUNK, keys)
    q_at = lax.broadcasted_iota(jnp.int32, shape, 0) + i * CHUNK
    k_at = lax.broadcasted_iota(jnp.int32, shape, 1)
    same = seg_col[i * CHUNK : keys, :] == seg_row[:, :keys]
    return same & (k_at <= q_at)


def placed_half(first, row):
    none = jnp.zeros_like(row)
    return jnp.where(
        first, jnp.concatenate([row, none], axis=1), jnp.concatenate([none, row], axis=1)
    )


def store_parts(first, rows, value, keep, send):
    low, high = value[:, :HALF].astype(BF16), value[:, HALF:].astype(BF16)

    @pl.when(first)
    def _():
        keep[rows, :] = low
        send[rows, :] = high

    @pl.when(jnp.logical_not(first))
    def _():
        keep[rows, :] = high
        send[rows, :] = low


def forward_rows(x_of, w, sm, bq, be, tabs, normed, mixed, q, k, v, active, slope):
    for i in range(ROWS // CHUNK):
        rows = slice(i * CHUNK, (i + 1) * CHUNK)
        xhat, _ = normalised(x_of(rows))
        normed[rows, :] = (xhat * sm[0:1, :] + sm[2:3, :]).astype(BF16)
        mixed[rows, :] = (xhat * sm[1:2, :] + sm[3:4, :]).astype(BF16)
        joint = nn(normed[rows, :], w[:, :QKV]) + bq[...]
        c, s1, s2 = tabs[0, rows, :], tabs[1, rows, :], tabs[2, rows, :]
        q[rows, :] = turn(joint[:, :WIDTH], c, s1, s2).astype(BF16)
        k[rows, :] = turn(joint[:, WIDTH : 2 * WIDTH], c, s1, s2).astype(BF16)
        v[rows, :] = joint[:, 2 * WIDTH :].astype(BF16)
        hidden = nn(mixed[rows, :], w[:, COL_E:COL_O]) + be[...]
        act, dact = gelu_both(hidden)
        active[rows, :] = act.astype(BF16)
        slope[rows, :] = dact.astype(slope.dtype)


def attend(q, k, v, seg_col, seg_row, att, lse):
    for i in range(ROWS // CHUNK):
        rows = slice(i * CHUNK, (i + 1) * CHUNK)
        keys = slice(0, (i + 1) * CHUNK)
        mask = allowed(i, seg_col[...], seg_row[...])
        out, tops = None, []
        for head in range(2):
            s = nt(head_mask(q[rows, :], head) * 0.125, k[keys, :])
            s = jnp.where(mask, s, -1e30)
            top = jnp.max(s, axis=1, keepdims=True)
            e = jnp.exp(s - top)
            total = jnp.sum(e, axis=1, keepdims=True)
            probs = (e * (1.0 / total)).astype(BF16)
            part = nn(probs, head_mask(v[keys, :], head))
            out = part if out is None else out + part
            tops.append(top + jnp.log(total))
        att[rows, :] = out.astype(BF16)
        lane = lax.broadcasted_iota(jnp.int32, (CHUNK, WIDTH), 1)
        lse[rows, :] = jnp.where(lane < HEAD_DIM, tops[0], tops[1])


def branch_out(first, w, att, active, keep, send):
    for i in range(ROWS // CHUNK):
        rows = slice(i * CHUNK, (i + 1) * CHUNK)
        branch = nt(att[rows, :], w[:, COL_O:COL_S]) + nt(active[rows, :], w[:, COL_S:])
        store_parts(first, rows, branch, keep, send)


def backward_rows(
    first, x_of, gy_of, w, sm, tabs, seg_col, seg_row, q, k, v, lse, slope,
    gatt, gk, gv, gq, gjoint, ghid, keep, send, sums,
):
    for i in range(ROWS // CHUNK):
        rows = slice(i * CHUNK, (i + 1) * CHUNK)
        gy = gy_of(rows)
        gatt[rows, :] = nn(gy, w[:, COL_O:COL_S]).astype(BF16)
        gact = nn(gy, w[:, COL_S:])
        ghid[rows, :] = (gact * slope[rows, :].astype(F32)).astype(BF16)
    gk[...] = jnp.zeros_like(gk)
    gv[...] = jnp.zeros_like(gv)
    for i in range(ROWS // CHUNK):
        rows = slice(i * CHUNK, (i + 1) * CHUNK)
        keys = slice(0, (i + 1) * CHUNK)
        mask = allowed(i, seg_col[...], seg_row[...])
        out = None
        for head in range(2):
            qh = head_mask(q[rows, :], head) * 0.125
            gh = head_mask(gatt[rows, :], head)
            s = nt(qh, k[keys, :])
            at = head * HEAD_DIM
            probs = jnp.where(mask, jnp.exp(s - lse[rows, at : at + 1]), 0.0)
            gp = nt(gh, v[keys, :])
            dot = jnp.sum(probs * gp, axis=1, keepdims=True)
            gs = (probs * (gp - dot)).astype(BF16)
            part = nn(gs, head_mask(k[keys, :], head) * 0.125)
            out = part if out is None else out + part
            gk[keys, :] += tn(gs, qh)
            gv[keys, :] += tn(probs.astype(BF16), gh)
        gq[rows, :] = out
    total = [None] * 7
    for i in range(ROWS // CHUNK):
        rows = slice(i * CHUNK, (i + 1) * CHUNK)
        c, s1, s2 = tabs[0, rows, :], tabs[1, rows, :], tabs[2, rows, :]
        gjoint[rows, :WIDTH] = turn_back(gq[rows, :], c, s1, s2).astype(BF16)
        gjoint[rows, WIDTH : 2 * WIDTH] = turn_back(gk[rows, :], c, s1, s2).astype(BF16)
        gjoint[rows, 2 * WIDTH :] = gv[rows, :].astype(BF16)
        gj, gh = gjoint[rows, :], ghid[rows, :]
        gn = nt(gj, w[:, :QKV])
        gm = nt(gh, w[:, COL_E:COL_O])
        xhat, rstd = normalised(x_of(rows))
        h = gn * sm[0:1, :] + gm * sm[1:2, :]
        gx = h - jnp.mean(h, axis=1, keepdims=True)
        gx = (gx - xhat * jnp.mean(h * xhat, axis=1, keepdims=True)) * rstd
        store_parts(first, rows, gx, keep, send)
        found = (
            jnp.sum(gn * xhat, axis=0, keepdims=True),
            jnp.sum(gm * xhat, axis=0, keepdims=True),
            jnp.sum(gn, axis=0, keepdims=True),
            jnp.sum(gm, axis=0, keepdims=True),
            jnp.sum(gy_of(rows).astype(F32), axis=0, keepdims=True),
            placed_half(first, jnp.sum(gh.astype(F32), axis=0, keepdims=True)),
            jnp.concatenate(
                [jnp.sum(gj.astype(F32), axis=0, keepdims=True), jnp.zeros((1, MODEL - QKV), F32)],
                axis=1,
            ),
        )
        total = [a if t is None else t + a for t, a in zip(total, found)]
    for n, t in enumerate(total):
        sums[n : n + 1, :] = t
    sums[7:8, :] = jnp.zeros((1, MODEL), F32)


def joined(first, a, b, rows):
    return jnp.where(
        first,
        jnp.concatenate([a[rows, :], b[rows, :]], axis=1),
        jnp.concatenate([b[rows, :], a[rows, :]], axis=1),
    )


def first_forward(
    core, x, w, sm, bq, be, tabs, seg_col, seg_row,
    keep, send, normed, mixed, q, k, v, att, lse, active, slope,
):
    first = core[0] == 0
    forward_rows(
        lambda rows: x[rows, :].astype(F32), w, sm, bq, be, tabs, normed, mixed, q, k, v, active, slope
    )
    attend(q, k, v, seg_col, seg_row, att, lse)
    branch_out(first, w, att, active, keep, send)


def both_ways(
    core, xa, xb, gy, w, sm, bq, be, tabs, seg_col, seg_row,
    keep_y, send_y, keep_g, send_g, normed, mixed, att, active, gjoint, ghid, sums,
    x, q, k, v, lse, slope, gatt, gk, gv, gq,
):
    first = core[0] == 0
    x[...] = joined(first, xa, xb, slice(None))
    x_of = lambda rows: x[rows, :].astype(F32)
    forward_rows(x_of, w, sm, bq, be, tabs, normed, mixed, q, k, v, active, slope)
    attend(q, k, v, seg_col, seg_row, att, lse)
    backward_rows(
        first, x_of, lambda rows: gy[rows, :], w, sm, tabs, seg_col, seg_row, q, k, v, lse, slope,
        gatt, gk, gv, gq, gjoint, ghid, keep_g, send_g, sums,
    )
    branch_out(first, w, att, active, keep_y, send_y)


def first_backward(
    core, x, ga, gb, w, sm, tabs, seg_col, seg_row, q, k, v, lse, slope,
    keep_g, send_g, gjoint, ghid, gy, sums,
    gatt, gk, gv, gq,
):
    first = core[0] == 0
    gy[...] = joined(first, ga, gb, slice(None))
    backward_rows(
        first, lambda rows: x[rows, :].astype(F32), lambda rows: gy[rows, :], w, sm, tabs,
        seg_col, seg_row, q, k, v, lse, slope, gatt, gk, gv, gq, gjoint, ghid, keep_g, send_g, sums,
    )


def weight_grads(n0, n1, m0, m1, g0, g1, j0, j1, h0, h1, a0, a1, c0, c1, out):
    out[:, :QKV] = (tn(n0[...], j0[...]) + tn(n1[...], j1[...])).astype(BF16)
    out[:, COL_E:COL_O] = (tn(m0[...], h0[...]) + tn(m1[...], h1[...])).astype(BF16)
    out[:, COL_O:COL_S] = (tn(g0[...], a0[...]) + tn(g1[...], a1[...])).astype(BF16)
    out[:, COL_S:COLS] = (tn(g0[...], c0[...]) + tn(g1[...], c1[...])).astype(BF16)


def owner_order(first, row):
    shape = (QKV, HALF)
    at = lax.broadcasted_iota(jnp.int32, shape, 0)
    col = lax.broadcasted_iota(jnp.int32, shape, 1)
    part = (col // 16) % 4
    wanted = jnp.where(part < 3, part * WIDTH + (col // 64) * 16 + col % 16, -1)
    moved = nn(row.astype(BF16), jnp.where(at == wanted, 1.0, 0.0).astype(BF16))
    return placed_half(first, moved)


def weight_and_row_grads(core, *refs):
    *big, s00, s01, s10, s11, out, rows = refs
    step = out.shape[0]
    weight_grads(*big, out)

    @pl.when(pl.program_id(0) == 0)
    def _():
        rows[...] = jnp.zeros_like(rows)
        for n, (a, b) in enumerate(((s00, s01), (s10, s11))):
            total = a[...] + b[...]
            rows[8 * n : 8 * n + 8, :] = total
            moved = owner_order(core[0] == 0, total[:, :QKV])
            rows[8 * n + 6 : 8 * n + 7, :] = moved[6:7, :]

    at = pl.multiple_of(pl.program_id(0) * step, step)
    out[:, COLS:] = rows[:, pl.ds(at, step)].T.astype(BF16)


def shaped(*dims, dtype=BF16):
    return jax.ShapeDtypeStruct(dims, dtype)


def call(kernel, n_in, outs, scratch, flops, name, after=()):
    whole = pl.BlockSpec(memory_space=pltpu.VMEM)

    def body(*refs):
        kernel(*refs[:n_in], *refs[n_in + len(after) :])

    made = pl.pallas_call(
        body,
        in_specs=[pl.BlockSpec(memory_space=pltpu.SMEM)]
        + [whole] * (n_in - 1)
        + [pl.BlockSpec(memory_space=pl.ANY)] * len(after),
        out_specs=[whole] * len(outs),
        out_shape=outs,
        scratch_shapes=scratch,
        compiler_params=pltpu.CompilerParams(vmem_limit_bytes=60 * 2**20),
        cost_estimate=pl.CostEstimate(flops=flops, bytes_accessed=8 * 2**20, transcendentals=2**20),
        name=name,
    )
    return lambda *args: made(*args, *after)


def tall(width, dtype=BF16):
    return shaped(ROWS, width, dtype=dtype)


def forward_call(*args, after=()):
    outs = [tall(HALF), tall(HALF), tall(MODEL), tall(MODEL)]
    outs += [tall(WIDTH)] * 4 + [tall(WIDTH, F32), tall(INNER), tall(INNER)]
    return call(first_forward, len(args), outs, [], 2**31, "layer_forward", after)(*args)


def both_call(*args, after=()):
    outs = [tall(HALF)] * 4 + [tall(MODEL)] * 2 + [tall(WIDTH), tall(INNER), tall(QKV), tall(INNER)]
    outs += [shaped(8, MODEL, dtype=F32)]
    scratch = [pltpu.VMEM((ROWS, MODEL), BF16)] + [pltpu.VMEM((ROWS, WIDTH), BF16)] * 3
    scratch += [pltpu.VMEM((ROWS, WIDTH), F32), pltpu.VMEM((ROWS, INNER), F32)]
    scratch += [pltpu.VMEM((ROWS, WIDTH), BF16)] + [pltpu.VMEM((ROWS, WIDTH), F32)] * 3
    return call(both_ways, len(args), outs, scratch, 2**32, "layer_both", after)(*args)


def backward_call(*args, after=()):
    outs = [tall(HALF)] * 2 + [tall(QKV), tall(INNER), tall(MODEL), shaped(8, MODEL, dtype=F32)]
    scratch = [pltpu.VMEM((ROWS, WIDTH), BF16)] + [pltpu.VMEM((ROWS, WIDTH), F32)] * 3
    return call(first_backward, len(args), outs, scratch, 2**31, "layer_backward", after)(*args)


def grads_call(*args, core_arg=None, sums=(), after=()):
    blocks = 4
    step = MODEL // blocks
    cut = pl.BlockSpec((ROWS, step), lambda i: (0, i))
    rest = [pl.BlockSpec(a.shape, lambda i: (0, 0)) for a in (*args[6:], *sums)]
    n_in = len(args) + len(sums)
    width = COLS + (128 if sums else 0)

    def body(*refs):
        refs = (*refs[:n_in], *refs[n_in + len(after) :])
        weight_grads(*refs)

    def body_rows(core, *refs):
        weight_and_row_grads(core, *refs[:n_in], *refs[n_in + len(after) :])

    specs = [cut] * 6 + rest + [pl.BlockSpec(memory_space=pl.ANY)] * len(after)
    return pl.pallas_call(
        body_rows if sums else body,
        grid=(blocks,),
        in_specs=([pl.BlockSpec(memory_space=pltpu.SMEM)] if sums else []) + specs,
        out_specs=pl.BlockSpec((step, width), lambda i: (i, 0)),
        out_shape=shaped(MODEL, width),
        scratch_shapes=[pltpu.VMEM((128, MODEL), F32)] if sums else [],
        compiler_params=pltpu.CompilerParams(vmem_limit_bytes=60 * 2**20),
        cost_estimate=pl.CostEstimate(flops=2**32, bytes_accessed=2**23, transcendentals=0),
        name="weight_grads",
    )(*([core_arg] if sums else []), *args, *sums, *after)


def spread(core, a, out):
    for n in range(out.shape[0]):
        out[n] = jnp.where(core[0] == 0, a[0], a[1])


def spread_call(a, core_arg, after):
    outs = [shaped(lax.axis_size("tensor"), *a.shape[1:])]
    return call(spread, 2, outs, [], 2**20, "spread_rows", after)(core_arg, a)[0]


def add_around(place, k0, g0, k1, g1, *outs):
    step = ROWS // len(outs)
    for n, out in enumerate(outs):
        at = lax.rem(place[0] + n, len(outs)) * step
        rows = pl.ds(pl.multiple_of(at, step), step)
        out[0] = (k0[rows, :].astype(F32) + g0[rows, :].astype(F32)).astype(BF16)
        out[1] = (k1[rows, :].astype(F32) + g1[rows, :].astype(F32)).astype(BF16)


def add_around_call(place, keeps, gots, after):
    tensor = lax.axis_size("tensor")
    outs = [shaped(2, ROWS // tensor, HALF)] * tensor
    args = (place, keeps[0], gots[0], keeps[1], gots[1])
    return call(add_around, 5, outs, [], 2**20, "add_around", after)(*args)


def swap(x):
    return lax.ppermute(x, "pipe", [(0, 1), (1, 0)])


def z_scatter(x):
    return lax.all_to_all(x, "tensor", split_axis=0, concat_axis=0, tiled=True)


def along_ring(x, axis, offset, stride=1, side=4):
    pairs = []
    for g in range(lax.axis_size(axis)):
        at = (g // stride) % side
        to = (at + 1) % side if at % 2 == offset else (at - 1) % side
        pairs.append((g, g + (to - at) * stride))
    return lax.ppermute(x, axis, pairs)


def added(a, b):
    return (a.astype(F32) + b.astype(F32)).astype(BF16)


class SumOverTensor:
    def __init__(self, keep, send):
        both = added(keep, swap(send))
        self.chip = [both[:, : HALF // 2], both[:, HALF // 2 :]]
        self.pair = [added(a, along_ring(a, "tensor", n)) for n, a in enumerate(self.chip)]

    def finish(self, base, shift):
        whole = [added(a, along_ring(a, "tensor", 1 - n)) for n, a in enumerate(self.pair)]
        total = jnp.concatenate(whole, axis=1).astype(F32) + base.astype(F32)
        mine = (total if shift is None else total + shift).astype(BF16)
        return mine, swap(mine)


def around(keeps, sends, place, after):
    return add_around_call(place, keeps, [swap(s) for s in sends], after)


def summed_around(parts):
    tensor = lax.axis_size("tensor")
    total = parts[0].astype(F32)
    for n, other in enumerate(parts[1:]):
        pairs = [(i, (i + n + 1) % tensor) for i in range(tensor)]
        total = total + lax.ppermute(other, "tensor", pairs).astype(F32)
    return total


def rotary_tables(segment_row):
    places = jnp.arange(ROWS, dtype=jnp.int32)
    before = jnp.sum((segment_row[None, :] < segment_row[:, None]).astype(jnp.int32), axis=1)
    positions = (places - before).astype(F32)
    half_rot = ROTARY // 2
    lane = jnp.arange(WIDTH, dtype=jnp.int32)[None, :] % HEAD_DIM
    inverse = 10000.0 ** (-(lane % half_rot).astype(F32) * 2.0 / ROTARY)
    angles = positions[:, None] * inverse
    cosine, sine = jnp.cos(angles), jnp.sin(angles)
    c = jnp.where(lane < ROTARY, cosine, 1.0)
    s1 = jnp.where(lane < half_rot, -sine, 0.0)
    s2 = jnp.where((lane >= half_rot) & (lane < ROTARY), sine, 0.0)
    return jnp.stack([c, s1, s2])


def shards(
    inputs, upstream, segments, joint_weight, joint_bias, output_weight, expand_weight,
    expand_bias, shrink_weight, norm_gains, shift_rows,
):
    dp = lax.axis_size("dp")
    tensor = lax.axis_size("tensor")
    core = lax.axis_index("pipe")
    first = core == 0
    core_arg = core.astype(jnp.int32).reshape(1)
    micros = inputs.shape[0]
    own_d = MODEL // dp

    def pick(a, b):
        return jnp.where(first, a, b)

    def packed(h):
        return jnp.concatenate(
            [
                joint_weight[0][:, :, h * WIDTH : (h + 1) * WIDTH].reshape(own_d, QKV),
                expand_weight[0][:, h * INNER : (h + 1) * INNER],
                output_weight[0][h * WIDTH : (h + 1) * WIDTH].T,
                shrink_weight[0][h * INNER : (h + 1) * INNER].T,
            ],
            axis=1,
        )

    with jax.named_scope("weights"):
        pack_a, pack_b = packed(0), packed(1)
        stay = pick(pack_a, pack_b)
        came = swap(pick(pack_b, pack_a))
        w0 = lax.all_gather(pick(stay, came), "dp", axis=0, tiled=True)
        w1 = lax.all_gather(pick(came, stay), "dp", axis=0, tiled=True)

    with jax.named_scope("small_parameters"):
        bias_row = jnp.pad(joint_bias[0, :, 0, :].reshape(1, -1), ((0, 0), (0, own_d - 3 * 16)))
        small = jnp.concatenate([norm_gains[0], shift_rows[0], expand_bias[0], bias_row], axis=0)
        copies = jnp.broadcast_to(small, (2 * dp, *small.shape))
        small = lax.all_to_all(copies, ("pipe", "dp"), split_axis=0, concat_axis=0, tiled=True)
        small = small.reshape(2, dp, 8, own_d).astype(F32)
        rows = small.transpose(0, 2, 1, 3).reshape(2, 8, MODEL)
        be = [pick(rows[n, 6:7, :INNER], rows[n, 6:7, INNER:]) for n in range(2)]
        bq_all = small[:, :, 7, :48].reshape(2, dp, 3, 16).transpose(0, 2, 1, 3).reshape(2, 3, 256)
        bq = [
            pick(bq_all[n, :, :WIDTH], bq_all[n, :, WIDTH:]).reshape(1, QKV) for n in range(2)
        ]
        shift_own = [pick(rows[n, :, :HALF], rows[n, :, HALF:]) for n in range(2)]

    with jax.named_scope("activations_in"):

        def everywhere(copies):
            mine = z_scatter(copies).reshape(ROWS, MODEL)
            other = swap(mine)
            return [pick(mine, other), pick(other, mine)]

        x0 = everywhere(spread_call(inputs, core_arg, (came,)))

    with jax.named_scope("tables"):
        tabs = [rotary_tables(segments[m]) for m in range(micros)]
        seg_col = [segments[m].reshape(ROWS, 1) for m in range(micros)]
        seg_row = [segments[m].reshape(1, ROWS) for m in range(micros)]

    place = lax.axis_index("tensor").astype(jnp.int32).reshape(1)

    def half_of(a):
        return pick(a[:, :HALF], a[:, HALF:])

    kept, sums0 = [], []
    after = tuple(tabs)
    for m in range(micros):
        with jax.named_scope("first_layer"):
            keep, send, *saved = forward_call(
                core_arg, x0[m], w0, rows[0], bq[0], be[0], tabs[m], seg_col[m], seg_row[m], after=after
            )
            sums0.append(SumOverTensor(keep, send))
            after = tuple(sums0[m].chip)
            kept.append(saved)

    with jax.named_scope("upstream_in"):
        gy1 = everywhere(spread_call(upstream, core_arg, (kept[0][0],)))

    x1, made1, y_parts, sums1 = [], [], [], []
    shift = shift_own[0][4:5] + shift_own[0][5:6]
    after = ()
    for m in range(micros):
        with jax.named_scope("second_layer"):
            x1.append(sums0[m].finish(half_of(x0[m]), shift))
            keep_y, send_y, keep_g, send_g, *made = both_call(
                core_arg, *x1[m], gy1[m], w1, rows[1], bq[1], be[1], tabs[m], seg_col[m], seg_row[m],
                after=after,
            )
            sums1.append(SumOverTensor(keep_g, send_g))
            after = tuple(sums1[m].chip)
            y_parts.append((keep_y, send_y))
            made1.append(made)

    def pairs(made, n):
        return [made[m][n] for m in range(micros)]

    with jax.named_scope("second_layer_grads"):
        args = []
        for n in (0, 1, None, 4, 5, 2, 3):
            args += gy1 if n is None else pairs(made1, n)
        grads1 = grads_call(*args, after=(*sums1[0].pair, *sums1[1].chip))
        sum1 = lax.psum_scatter(grads1, "dp", scatter_dimension=0, tiled=True).astype(F32)

    g0, made0, g_parts = [], [], []
    after = (grads1,)
    for m in range(micros):
        with jax.named_scope("first_layer_back"):
            normed, mixed, q, k, v, att, lse, active, slope = kept[m]
            g0.append(sums1[m].finish(half_of(gy1[m]), None))
            keep_g, send_g, gjoint, ghid, gy, sums = backward_call(
                core_arg, x0[m], *g0[m], w0, rows[0], tabs[m], seg_col[m], seg_row[m],
                q, k, v, lse, slope, after=after,
            )
            g_parts.append((keep_g, send_g))
            made0.append((normed, mixed, att, active, gjoint, ghid, sums, gy))
        if m == 0:
            with jax.named_scope("boundary"):
                y_around = around(*zip(*y_parts), place, (keep_g,))
                after = tuple(y_around)

    with jax.named_scope("boundary"):
        g_around = around(*zip(*g_parts), place, ())

    with jax.named_scope("first_layer_grads"):
        args = []
        for n in (0, 1, 7, 4, 5, 2, 3):
            args += pairs(made0, n)
        sums = (made0[0][6], made0[1][6], made1[0][6], made1[1][6])
        grads0 = grads_call(*args, core_arg=core_arg, sums=sums, after=tuple(g_around))
        tiles = grads0.reshape(dp, own_d, -1)
        arrived = lax.all_to_all(tiles, "dp", split_axis=0, concat_axis=0, tiled=True)
        sum0 = arrived.astype(F32).sum(axis=0)

    with jax.named_scope("boundary"):

        def own_rows(parts):
            step = ROWS // tensor
            return jnp.stack(
                [lax.dynamic_slice_in_dim(a, place[0] * step, step, 0) for a, _ in parts]
            ).astype(F32)

        gx_all = summed_around(g_around) + own_rows(g0)
        y_all = summed_around(y_around) + own_rows(x1)
        y_all = y_all + (shift_own[1][4:5] + shift_own[1][5:6])
        other = swap(pick(y_all, gx_all))
        boundary = pick(
            jnp.concatenate([gx_all, other], axis=2), jnp.concatenate([other, y_all], axis=2)
        )[None]

    with jax.named_scope("small_grads"):
        own = sum0[:, COLS : COLS + 16].T.reshape(2, 8, own_d)
        total, rest = own[:, :4], own[:, 4:]
        for offset in (0, 1):
            total = total + along_ring(total, "tensor", offset)
        both = jnp.concatenate([total, rest], axis=1)
        both = pick(both[0], both[1]) + swap(pick(both[1], both[0]))
        gains = both[None, 0:2]
        gy_sum = both[4] * 0.5
        shift = jnp.stack([both[2], both[3], gy_sum, gy_sum])[None]
        expand_bias_grad = both[5].reshape(1, 1, own_d)
        joint_bias_grad = both[6, :48].reshape(1, 3, 1, 16)
        sum0 = sum0[:, :COLS]

    with jax.named_scope("outputs"):
        other = swap(pick(sum1, sum0))
        low = pick(sum0, other)
        high = pick(other, sum1)
        joint = jnp.concatenate(
            [low[:, :QKV].reshape(own_d, 3, WIDTH), high[:, :QKV].reshape(own_d, 3, WIDTH)], axis=2
        )[None]
        expand = jnp.concatenate([low[:, COL_E:COL_O], high[:, COL_E:COL_O]], axis=1)[None]
        output = jnp.concatenate([low[:, COL_O:COL_S], high[:, COL_O:COL_S]], axis=1).T[None]
        shrink = jnp.concatenate([low[:, COL_S:], high[:, COL_S:]], axis=1).T[None]

    return (
        boundary,
        joint,
        joint_bias_grad,
        output,
        expand,
        expand_bias_grad,
        shrink,
        gains,
        shift,
    )


def solution(mesh):
    placed = (
        P(None, ("dp", "tensor"), None),
        P(None, ("dp", "tensor"), None),
        P(None, "dp"),
        P("pipe", "dp", None, "tensor"),
        P("pipe", None, "tensor", "dp"),
        P("pipe", "tensor", "dp"),
        P("pipe", "dp", "tensor"),
        P("pipe", "tensor", "dp"),
        P("pipe", "tensor", "dp"),
        P("pipe", None, "dp"),
        P("pipe", None, "dp"),
    )
    return jax.shard_map(
        shards,
        mesh=mesh,
        in_specs=placed,
        out_specs=(
            P("pipe", None, ("dp", "tensor"), None),
            P("pipe", "dp", None, "tensor"),
            P("pipe", None, "tensor", "dp"),
            P("pipe", "tensor", "dp"),
            P("pipe", "dp", "tensor"),
            P("pipe", "tensor", "dp"),
            P("pipe", "tensor", "dp"),
            P("pipe", None, "dp"),
            P("pipe", None, "dp"),
        ),
        check_vma=False,
    )
```

```python
import functools

import jax
import jax.numpy as jnp
from jax import lax
from jax.experimental import pallas as pl
from jax.experimental.pallas import tpu as pltpu
from jax.sharding import PartitionSpec as P

HEAD_DIM = 64
ROTARY = 16
EPS = 1e-05

MODEL = 1024
ROWS = 512
CHUNK = 256
WIDTH = 128
INNER = 512
HALF = MODEL // 2

QKV = 3 * WIDTH
COL_E = QKV
COL_O = QKV + INNER
COL_S = COL_O + WIDTH
COLS = COL_S + INNER

F32 = jnp.float32
BF16 = jnp.bfloat16


def nn(a, b):
    return lax.dot_general(a, b, (((1,), (0,)), ((), ())), preferred_element_type=F32)


def nt(a, b):
    return lax.dot_general(a, b, (((1,), (1,)), ((), ())), preferred_element_type=F32)


def tn(a, b):
    return lax.dot_general(a, b, (((0,), (0,)), ((), ())), preferred_element_type=F32)


def normalised(x):
    centred = x - jnp.mean(x, axis=1, keepdims=True)
    rstd = lax.rsqrt(jnp.mean(centred * centred, axis=1, keepdims=True) + EPS)
    return centred * rstd, rstd


def gelu_both(h):
    a = jnp.abs(h) * 0.7071067811865476
    t = 1.0 / (1.0 + 0.3275911 * a)
    poly = 1.061405429 * t - 1.453152027
    poly = poly * t + 1.421413741
    poly = poly * t - 0.284496736
    poly = poly * t + 0.254829592
    e = jnp.exp(-0.5 * h * h)
    tail = 0.5 * poly * t * e
    cdf = jnp.where(h >= 0, 1.0 - tail, tail)
    return h * cdf, cdf + h * (e * 0.3989422804014327)


def head_mask(v, head):
    lane = lax.broadcasted_iota(jnp.int32, v.shape, 1)
    return jnp.where((lane >= HEAD_DIM) == (head == 1), v, jnp.zeros_like(v))


def turn(u, c, s1, s2):
    return u * c + pltpu.roll(u, WIDTH - 8, 1) * s1 + pltpu.roll(u, 8, 1) * s2


def turn_back(w, c, s1, s2):
    return w * c + pltpu.roll(w * s2, WIDTH - 8, 1) + pltpu.roll(w * s1, 8, 1)


def allowed(i, seg_col, seg_row):
    keys = (i + 1) * CHUNK
    shape = (CHUNK, keys)
    q_at = lax.broadcasted_iota(jnp.int32, shape, 0) + i * CHUNK
    k_at = lax.broadcasted_iota(jnp.int32, shape, 1)
    same = seg_col[i * CHUNK : keys, :] == seg_row[:, :keys]
    return same & (k_at <= q_at)


def placed_half(first, row):
    none = jnp.zeros_like(row)
    return jnp.where(
        first, jnp.concatenate([row, none], axis=1), jnp.concatenate([none, row], axis=1)
    )


def store_parts(first, rows, value, keep, send):
    low, high = value[:, :HALF].astype(BF16), value[:, HALF:].astype(BF16)

    @pl.when(first)
    def _():
        keep[rows, :] = low
        send[rows, :] = high

    @pl.when(jnp.logical_not(first))
    def _():
        keep[rows, :] = high
        send[rows, :] = low


def forward_rows(x_of, w, sm, bq, be, tabs, normed, mixed, q, k, v, active, slope):
    for i in range(ROWS // CHUNK):
        rows = slice(i * CHUNK, (i + 1) * CHUNK)
        xhat, _ = normalised(x_of(rows))
        normed[rows, :] = (xhat * sm[0:1, :] + sm[2:3, :]).astype(BF16)
        mixed[rows, :] = (xhat * sm[1:2, :] + sm[3:4, :]).astype(BF16)
        joint = nn(normed[rows, :], w[:, :QKV]) + bq[...]
        c, s1, s2 = tabs[0, rows, :], tabs[1, rows, :], tabs[2, rows, :]
        q[rows, :] = turn(joint[:, :WIDTH], c, s1, s2).astype(BF16)
        k[rows, :] = turn(joint[:, WIDTH : 2 * WIDTH], c, s1, s2).astype(BF16)
        v[rows, :] = joint[:, 2 * WIDTH :].astype(BF16)
        hidden = nn(mixed[rows, :], w[:, COL_E:COL_O]) + be[...]
        act, dact = gelu_both(hidden)
        active[rows, :] = act.astype(BF16)
        slope[rows, :] = dact.astype(slope.dtype)


def attend(q, k, v, seg_col, seg_row, att, lse):
    for i in range(ROWS // CHUNK):
        rows = slice(i * CHUNK, (i + 1) * CHUNK)
        keys = slice(0, (i + 1) * CHUNK)
        mask = allowed(i, seg_col[...], seg_row[...])
        out, tops = None, []
        for head in range(2):
            s = nt(head_mask(q[rows, :], head) * 0.125, k[keys, :])
            s = jnp.where(mask, s, -1e30)
            top = jnp.max(s, axis=1, keepdims=True)
            e = jnp.exp(s - top)
            total = jnp.sum(e, axis=1, keepdims=True)
            probs = (e * (1.0 / total)).astype(BF16)
            part = nn(probs, head_mask(v[keys, :], head))
            out = part if out is None else out + part
            tops.append(top + jnp.log(total))
        att[rows, :] = out.astype(BF16)
        lane = lax.broadcasted_iota(jnp.int32, (CHUNK, WIDTH), 1)
        lse[rows, :] = jnp.where(lane < HEAD_DIM, tops[0], tops[1])


def branch_out(first, w, att, active, keep, send):
    for i in range(ROWS // CHUNK):
        rows = slice(i * CHUNK, (i + 1) * CHUNK)
        branch = nt(att[rows, :], w[:, COL_O:COL_S]) + nt(active[rows, :], w[:, COL_S:])
        store_parts(first, rows, branch, keep, send)


def backward_rows(
    first, x_of, gy_of, w, sm, tabs, seg_col, seg_row, q, k, v, lse, slope,
    gatt, gk, gv, gq, gjoint, ghid, keep, send, sums,
):
    for i in range(ROWS // CHUNK):
        rows = slice(i * CHUNK, (i + 1) * CHUNK)
        gy = gy_of(rows)
        gatt[rows, :] = nn(gy, w[:, COL_O:COL_S]).astype(BF16)
        gact = nn(gy, w[:, COL_S:])
        ghid[rows, :] = (gact * slope[rows, :].astype(F32)).astype(BF16)
    gk[...] = jnp.zeros_like(gk)
    gv[...] = jnp.zeros_like(gv)
    for i in range(ROWS // CHUNK):
        rows = slice(i * CHUNK, (i + 1) * CHUNK)
        keys = slice(0, (i + 1) * CHUNK)
        mask = allowed(i, seg_col[...], seg_row[...])
        out = None
        for head in range(2):
            qh = head_mask(q[rows, :], head) * 0.125
            gh = head_mask(gatt[rows, :], head)
            s = nt(qh, k[keys, :])
            at = head * HEAD_DIM
            probs = jnp.where(mask, jnp.exp(s - lse[rows, at : at + 1]), 0.0)
            gp = nt(gh, v[keys, :])
            dot = jnp.sum(probs * gp, axis=1, keepdims=True)
            gs = (probs * (gp - dot)).astype(BF16)
            part = nn(gs, head_mask(k[keys, :], head) * 0.125)
            out = part if out is None else out + part
            gk[keys, :] += tn(gs, qh)
            gv[keys, :] += tn(probs.astype(BF16), gh)
        gq[rows, :] = out
    total = [None] * 7
    for i in range(ROWS // CHUNK):
        rows = slice(i * CHUNK, (i + 1) * CHUNK)
        c, s1, s2 = tabs[0, rows, :], tabs[1, rows, :], tabs[2, rows, :]
        gjoint[rows, :WIDTH] = turn_back(gq[rows, :], c, s1, s2).astype(BF16)
        gjoint[rows, WIDTH : 2 * WIDTH] = turn_back(gk[rows, :], c, s1, s2).astype(BF16)
        gjoint[rows, 2 * WIDTH :] = gv[rows, :].astype(BF16)
        gj, gh = gjoint[rows, :], ghid[rows, :]
        gn = nt(gj, w[:, :QKV])
        gm = nt(gh, w[:, COL_E:COL_O])
        xhat, rstd = normalised(x_of(rows))
        h = gn * sm[0:1, :] + gm * sm[1:2, :]
        gx = h - jnp.mean(h, axis=1, keepdims=True)
        gx = (gx - xhat * jnp.mean(h * xhat, axis=1, keepdims=True)) * rstd
        store_parts(first, rows, gx, keep, send)
        found = (
            jnp.sum(gn * xhat, axis=0, keepdims=True),
            jnp.sum(gm * xhat, axis=0, keepdims=True),
            jnp.sum(gn, axis=0, keepdims=True),
            jnp.sum(gm, axis=0, keepdims=True),
            jnp.sum(gy_of(rows).astype(F32), axis=0, keepdims=True),
            placed_half(first, jnp.sum(gh.astype(F32), axis=0, keepdims=True)),
            jnp.concatenate(
                [jnp.sum(gj.astype(F32), axis=0, keepdims=True), jnp.zeros((1, MODEL - QKV), F32)],
                axis=1,
            ),
        )
        total = [a if t is None else t + a for t, a in zip(total, found)]
    for n, t in enumerate(total):
        sums[n : n + 1, :] = t
    sums[7:8, :] = jnp.zeros((1, MODEL), F32)


def join(first, out, a0, a1, b0, b1):
    step = HALF // 2

    @pl.when(first)
    def _():
        for n, part in enumerate((a0, a1, b0, b1)):
            out[:, n * step : (n + 1) * step] = part[...]

    @pl.when(jnp.logical_not(first))
    def _():
        for n, part in enumerate((b0, b1, a0, a1)):
            out[:, n * step : (n + 1) * step] = part[...]


def first_forward(
    core, x, w, sm, bq, be, tabs, seg_col, seg_row,
    keep, send, normed, mixed, q, k, v, att, lse, active, slope,
):
    first = core[0] == 0
    forward_rows(
        lambda rows: x[rows, :].astype(F32), w, sm, bq, be, tabs, normed, mixed, q, k, v, active, slope
    )
    attend(q, k, v, seg_col, seg_row, att, lse)
    branch_out(first, w, att, active, keep, send)


def both_ways(
    core, xa0, xa1, xb0, xb1, gy, w, sm, bq, be, tabs, seg_col, seg_row,
    keep_y, send_y, keep_g, send_g, normed, mixed, att, active, gjoint, ghid, sums,
    x, q, k, v, lse, slope, gatt, gk, gv, gq,
):
    first = core[0] == 0
    join(first, x, xa0, xa1, xb0, xb1)
    x_of = lambda rows: x[rows, :].astype(F32)
    forward_rows(x_of, w, sm, bq, be, tabs, normed, mixed, q, k, v, active, slope)
    attend(q, k, v, seg_col, seg_row, att, lse)
    backward_rows(
        first, x_of, lambda rows: gy[rows, :], w, sm, tabs, seg_col, seg_row, q, k, v, lse, slope,
        gatt, gk, gv, gq, gjoint, ghid, keep_g, send_g, sums,
    )
    branch_out(first, w, att, active, keep_y, send_y)


def first_backward(
    core, x, ga0, ga1, gb0, gb1, w, sm, tabs, seg_col, seg_row, q, k, v, lse, slope,
    keep_g, send_g, gjoint, ghid, gy, sums,
    gatt, gk, gv, gq,
):
    first = core[0] == 0
    join(first, gy, ga0, ga1, gb0, gb1)
    backward_rows(
        first, lambda rows: x[rows, :].astype(F32), lambda rows: gy[rows, :], w, sm, tabs,
        seg_col, seg_row, q, k, v, lse, slope, gatt, gk, gv, gq, gjoint, ghid, keep_g, send_g, sums,
    )


def weight_grads(n0, n1, m0, m1, g0, g1, j0, j1, h0, h1, a0, a1, c0, c1, out):
    out[:, :QKV] = (tn(n0[...], j0[...]) + tn(n1[...], j1[...])).astype(BF16)
    out[:, COL_E:COL_O] = (tn(m0[...], h0[...]) + tn(m1[...], h1[...])).astype(BF16)
    out[:, COL_O:COL_S] = (tn(g0[...], a0[...]) + tn(g1[...], a1[...])).astype(BF16)
    out[:, COL_S:COLS] = (tn(g0[...], c0[...]) + tn(g1[...], c1[...])).astype(BF16)


def owner_order(first, row):
    shape = (QKV, HALF)
    at = lax.broadcasted_iota(jnp.int32, shape, 0)
    col = lax.broadcasted_iota(jnp.int32, shape, 1)
    part = (col // 16) % 4
    wanted = jnp.where(part < 3, part * WIDTH + (col // 64) * 16 + col % 16, -1)
    moved = nn(row.astype(BF16), jnp.where(at == wanted, 1.0, 0.0).astype(BF16))
    return placed_half(first, moved)


def weight_and_row_grads(core, *refs):
    *big, s00, s01, s10, s11, out, rows = refs
    step = out.shape[0]
    weight_grads(*big, out)

    @pl.when(pl.program_id(0) == 0)
    def _():
        rows[...] = jnp.zeros_like(rows)
        for n, (a, b) in enumerate(((s00, s01), (s10, s11))):
            total = a[...] + b[...]
            rows[8 * n : 8 * n + 8, :] = total
            moved = owner_order(core[0] == 0, total[:, :QKV])
            rows[8 * n + 6 : 8 * n + 7, :] = moved[6:7, :]

    at = pl.multiple_of(pl.program_id(0) * step, step)
    out[:, COLS:] = rows[:, pl.ds(at, step)].T.astype(BF16)


def shaped(*dims, dtype=BF16):
    return jax.ShapeDtypeStruct(dims, dtype)


def call(kernel, n_in, outs, scratch, flops, name, after=()):
    whole = pl.BlockSpec(memory_space=pltpu.VMEM)

    def body(*refs):
        kernel(*refs[:n_in], *refs[n_in + len(after) :])

    made = pl.pallas_call(
        body,
        in_specs=[pl.BlockSpec(memory_space=pltpu.SMEM)]
        + [whole] * (n_in - 1)
        + [pl.BlockSpec(memory_space=pl.ANY)] * len(after),
        out_specs=[whole] * len(outs),
        out_shape=outs,
        scratch_shapes=scratch,
        compiler_params=pltpu.CompilerParams(vmem_limit_bytes=60 * 2**20),
        cost_estimate=pl.CostEstimate(flops=flops, bytes_accessed=8 * 2**20, transcendentals=2**20),
        name=name,
    )
    return lambda *args: made(*args, *after)


def tall(width, dtype=BF16):
    return shaped(ROWS, width, dtype=dtype)


def forward_call(*args, after=()):
    outs = [tall(HALF), tall(HALF), tall(MODEL), tall(MODEL)]
    outs += [tall(WIDTH)] * 4 + [tall(WIDTH, F32), tall(INNER), tall(INNER)]
    return call(first_forward, len(args), outs, [], 2**31, "layer_forward", after)(*args)


def both_call(*args, after=()):
    outs = [tall(HALF)] * 4 + [tall(MODEL)] * 2 + [tall(WIDTH), tall(INNER), tall(QKV), tall(INNER)]
    outs += [shaped(8, MODEL, dtype=F32)]
    scratch = [pltpu.VMEM((ROWS, MODEL), BF16)] + [pltpu.VMEM((ROWS, WIDTH), BF16)] * 3
    scratch += [pltpu.VMEM((ROWS, WIDTH), F32), pltpu.VMEM((ROWS, INNER), F32)]
    scratch += [pltpu.VMEM((ROWS, WIDTH), BF16)] + [pltpu.VMEM((ROWS, WIDTH), F32)] * 3
    return call(both_ways, len(args), outs, scratch, 2**32, "layer_both", after)(*args)


def backward_call(*args, after=()):
    outs = [tall(HALF)] * 2 + [tall(QKV), tall(INNER), tall(MODEL), shaped(8, MODEL, dtype=F32)]
    scratch = [pltpu.VMEM((ROWS, WIDTH), BF16)] + [pltpu.VMEM((ROWS, WIDTH), F32)] * 3
    return call(first_backward, len(args), outs, scratch, 2**31, "layer_backward", after)(*args)


def grads_call(*args, core_arg=None, sums=(), after=()):
    blocks = 4
    step = MODEL // blocks
    cut = pl.BlockSpec((ROWS, step), lambda i: (0, i))
    rest = [pl.BlockSpec(a.shape, lambda i: (0, 0)) for a in (*args[6:], *sums)]
    n_in = len(args) + len(sums)
    width = COLS + (128 if sums else 0)

    def body(*refs):
        *outs, token = refs[n_in + len(after) :]
        weight_grads(*refs[:n_in], *outs)
        token[...] = jnp.zeros_like(token)

    def body_rows(core, *refs):
        weight_and_row_grads(core, *refs[:n_in], *refs[n_in + len(after) :])

    specs = [cut] * 6 + rest + [pl.BlockSpec(memory_space=pl.ANY)] * len(after)
    return pl.pallas_call(
        body_rows if sums else body,
        grid=(blocks,),
        in_specs=([pl.BlockSpec(memory_space=pltpu.SMEM)] if sums else []) + specs,
        out_specs=[pl.BlockSpec((step, width), lambda i: (i, 0))]
        + ([] if sums else [pl.BlockSpec((8, 128), lambda i: (0, 0))]),
        out_shape=[shaped(MODEL, width)] + ([] if sums else [shaped(8, 128, dtype=F32)]),
        scratch_shapes=[pltpu.VMEM((128, MODEL), F32)] if sums else [],
        compiler_params=pltpu.CompilerParams(vmem_limit_bytes=60 * 2**20),
        cost_estimate=pl.CostEstimate(flops=2**32, bytes_accessed=2**23, transcendentals=0),
        name="weight_grads",
    )(*([core_arg] if sums else []), *args, *sums, *after)


def gate(x, *after):
    anywhere = pl.BlockSpec(memory_space=pl.ANY)
    return pl.pallas_call(
        lambda *refs: None,
        in_specs=[anywhere] * (1 + len(after)),
        out_specs=anywhere,
        out_shape=shaped(*x.shape, dtype=x.dtype),
        input_output_aliases={0: 0},
        name="gate",
    )(x, *after)


def assemble(place, own, before, behind, far0, far1, out0, out1):
    step = own.shape[1]
    ring = ROWS // step

    def put(out, value, distance):
        at = lax.rem(place[0] + distance, ring) * step
        out[pl.ds(pl.multiple_of(at, step), step), :] = value

    for n, (out, far) in enumerate(((out0, far0), (out1, far1))):
        put(out, own[n], 0)
        put(out, before[n], ring - 1)
        put(out, behind[n], 1)
        put(out, far[...], 2)


def around_ring(x, by):
    ring = lax.axis_size("tensor")
    return lax.ppermute(x, "tensor", [(i, (i + by) % ring) for i in range(ring)])


def gathered_rows(x, place):
    before, behind = around_ring(x, 1), around_ring(x, -1)
    far0, far1 = around_ring(before[0], 1), around_ring(behind[1], -1)
    outs = [tall(MODEL)] * 2
    return call(assemble, 6, outs, [], 2**20, "assemble")(place, x, before, behind, far0, far1)


def add_around(place, k0, g0, k1, g1, *outs):
    step = ROWS // len(outs)
    for n, out in enumerate(outs):
        at = lax.rem(place[0] + n, len(outs)) * step
        rows = pl.ds(pl.multiple_of(at, step), step)
        out[0] = (k0[rows, :].astype(F32) + g0[rows, :].astype(F32)).astype(BF16)
        out[1] = (k1[rows, :].astype(F32) + g1[rows, :].astype(F32)).astype(BF16)


def add_around_call(place, keeps, gots, after):
    tensor = lax.axis_size("tensor")
    outs = [shaped(2, ROWS // tensor, HALF)] * tensor
    args = (place, keeps[0], gots[0], keeps[1], gots[1])
    return call(add_around, 5, outs, [], 2**20, "add_around", after)(*args)


def swap(x):
    return lax.ppermute(x, "pipe", [(0, 1), (1, 0)])


def along_ring(x, axis, offset, stride=1, side=4):
    pairs = []
    for g in range(lax.axis_size(axis)):
        at = (g // stride) % side
        to = (at + 1) % side if at % 2 == offset else (at - 1) % side
        pairs.append((g, g + (to - at) * stride))
    return lax.ppermute(x, axis, pairs)


def added(a, b, row=None):
    total = a.astype(F32) + b.astype(F32)
    return (total if row is None else total + row).astype(BF16)


def halves(a):
    return [a[:, : HALF // 2], a[:, HALF // 2 :]]


class SumOverTensor:
    def __init__(self, keep, send):
        self.chip = halves(added(keep, swap(send)))

    def second(self, after=()):
        row = gate(jnp.zeros((1, HALF // 2), F32), *after) if after else None
        self.pair = [added(a, along_ring(a, "tensor", n), row) for n, a in enumerate(self.chip)]

    def finish(self, base, shift, after=()):
        shift = gate(shift, *after) if after else shift
        mine = []
        for n, (a, b, row) in enumerate(zip(self.pair, halves(base), halves(shift))):
            total = a.astype(F32) + along_ring(a, "tensor", 1 - n).astype(F32)
            mine.append((total + b.astype(F32) + row).astype(BF16))
        return (*mine, *[swap(a) for a in mine])


def around(keeps, sends, place, after):
    return add_around_call(place, keeps, [swap(gate(s, after)) for s in sends], ())


def summed_around(parts):
    tensor = lax.axis_size("tensor")
    total = parts[0].astype(F32)
    for n, other in enumerate(parts[1:]):
        pairs = [(i, (i + n + 1) % tensor) for i in range(tensor)]
        total = total + lax.ppermute(other, "tensor", pairs).astype(F32)
    return total


def rotary_tables(segment_row):
    places = jnp.arange(ROWS, dtype=jnp.int32)
    before = jnp.sum((segment_row[None, :] < segment_row[:, None]).astype(jnp.int32), axis=1)
    positions = (places - before).astype(F32)
    half_rot = ROTARY // 2
    lane = jnp.arange(WIDTH, dtype=jnp.int32)[None, :] % HEAD_DIM
    inverse = 10000.0 ** (-(lane % half_rot).astype(F32) * 2.0 / ROTARY)
    angles = positions[:, None] * inverse
    cosine, sine = jnp.cos(angles), jnp.sin(angles)
    c = jnp.where(lane < ROTARY, cosine, 1.0)
    s1 = jnp.where(lane < half_rot, -sine, 0.0)
    s2 = jnp.where((lane >= half_rot) & (lane < ROTARY), sine, 0.0)
    return jnp.stack([c, s1, s2])


def shards(
    inputs, upstream, segments, joint_weight, joint_bias, output_weight, expand_weight,
    expand_bias, shrink_weight, norm_gains, shift_rows,
):
    dp = lax.axis_size("dp")
    tensor = lax.axis_size("tensor")
    core = lax.axis_index("pipe")
    first = core == 0
    core_arg = core.astype(jnp.int32).reshape(1)
    micros = inputs.shape[0]
    own_d = MODEL // dp

    def pick(a, b):
        return jnp.where(first, a, b)

    def packed(h):
        return jnp.concatenate(
            [
                joint_weight[0][:, :, h * WIDTH : (h + 1) * WIDTH].reshape(own_d, QKV),
                expand_weight[0][:, h * INNER : (h + 1) * INNER],
                output_weight[0][h * WIDTH : (h + 1) * WIDTH].T,
                shrink_weight[0][h * INNER : (h + 1) * INNER].T,
            ],
            axis=1,
        )

    with jax.named_scope("weights"):
        pack_a, pack_b = packed(0), packed(1)
        stay = pick(pack_a, pack_b)
        came = swap(pick(pack_b, pack_a))
        w0 = lax.all_gather(pick(stay, came), "dp", axis=0, tiled=True)
        w1 = lax.all_gather(pick(came, stay), "dp", axis=0, tiled=True)

    with jax.named_scope("small_parameters"):
        bias_row = jnp.pad(joint_bias[0, :, 0, :].reshape(1, -1), ((0, 0), (0, own_d - 3 * 16)))
        small = jnp.concatenate([norm_gains[0], shift_rows[0], expand_bias[0], bias_row], axis=0)
        copies = jnp.broadcast_to(small, (2 * dp, *small.shape))
        small = lax.all_to_all(copies, ("pipe", "dp"), split_axis=0, concat_axis=0, tiled=True)
        small = small.reshape(2, dp, 8, own_d).astype(F32)
        rows = small.transpose(0, 2, 1, 3).reshape(2, 8, MODEL)
        be = [pick(rows[n, 6:7, :INNER], rows[n, 6:7, INNER:]) for n in range(2)]
        bq_all = small[:, :, 7, :48].reshape(2, dp, 3, 16).transpose(0, 2, 1, 3).reshape(2, 3, 256)
        bq = [
            pick(bq_all[n, :, :WIDTH], bq_all[n, :, WIDTH:]).reshape(1, QKV) for n in range(2)
        ]
        shift_own = [pick(rows[n, :, :HALF], rows[n, :, HALF:]) for n in range(2)]

    place = lax.axis_index("tensor").astype(jnp.int32).reshape(1)
    with jax.named_scope("activations_in"):
        x0 = gathered_rows(inputs, place)
        gy1 = gathered_rows(upstream, place)

    with jax.named_scope("tables"):
        tabs = [rotary_tables(segments[m]) for m in range(micros)]
        seg_col = [segments[m].reshape(ROWS, 1) for m in range(micros)]
        seg_row = [segments[m].reshape(1, ROWS) for m in range(micros)]

    def half_of(a):
        return pick(a[:, :HALF], a[:, HALF:])

    kept, sums0 = [], []
    after = (*tabs, *gy1)
    for m in range(micros):
        with jax.named_scope("first_layer"):
            keep, send, *saved = forward_call(
                core_arg, x0[m], w0, rows[0], bq[0], be[0], tabs[m], seg_col[m], seg_row[m], after=after
            )
            if m:
                sums0[0].second((saved[0],))
                send = gate(send, *sums0[0].pair)
            sums0.append(SumOverTensor(keep, send))
            after = tuple(sums0[m].chip)
            kept.append(saved)
    sums0[1].second()

    x1, made1, y_parts, sums1 = [], [], [], []
    shift = shift_own[0][4:5] + shift_own[0][5:6]
    for m in range(micros):
        with jax.named_scope("second_layer"):
            if m == 0:
                x1.append(sums0[0].finish(half_of(x0[0]), shift))
                after = tuple(sums0[1].pair)
            else:
                after = tuple(sums1[0].chip)
            keep_y, send_y, keep_g, send_g, *made = both_call(
                core_arg, *x1[m], gy1[m], w1, rows[1], bq[1], be[1], tabs[m], seg_col[m], seg_row[m],
                after=after,
            )
            if m == 0:
                x1.append(sums0[1].finish(half_of(x0[1]), shift, (made[-1],)))
            else:
                sums1[0].second((made[-1],))
                send_g = gate(send_g, *sums1[0].pair)
            sums1.append(SumOverTensor(keep_g, send_g))
            y_parts.append((keep_y, send_y))
            made1.append(made)

    def pairs(made, n):
        return [made[m][n] for m in range(micros)]

    with jax.named_scope("second_layer_grads"):
        args = []
        for n in (0, 1, None, 4, 5, 2, 3):
            args += gy1 if n is None else pairs(made1, n)
        grads1, token = grads_call(*args, after=(*sums1[1].chip, *sums1[0].pair))
        none = jnp.zeros((1, HALF), F32)
        g0 = [sums1[0].finish(half_of(gy1[0]), none, (token,))]
        sums1[1].second((token,))
        tiles1 = gate(grads1.reshape(dp, own_d, -1), *g0[0][:2], *sums1[1].pair)
        arrived1 = lax.all_to_all(tiles1, "dp", split_axis=0, concat_axis=0, tiled=True)

    made0, g_parts = [], []
    after = tuple(sums1[1].pair)
    for m in range(micros):
        with jax.named_scope("first_layer_back"):
            if m:
                g0.append(sums1[m].finish(half_of(gy1[m]), none, after))
            normed, mixed, q, k, v, att, lse, active, slope = kept[m]
            keep_g, send_g, gjoint, ghid, gy, sums = backward_call(
                core_arg, x0[m], *g0[m], w0, rows[0], tabs[m], seg_col[m], seg_row[m],
                q, k, v, lse, slope, after=after,
            )
            after = (sums,)
            g_parts.append((keep_g, send_g))
            made0.append((normed, mixed, att, active, gjoint, ghid, sums, gy))

    with jax.named_scope("first_layer_grads"):
        args = []
        for n in (0, 1, 7, 4, 5, 2, 3):
            args += pairs(made0, n)
        sums = (made0[0][6], made0[1][6], made1[0][6], made1[1][6])
        tiles0 = grads_call(*args, core_arg=core_arg, sums=sums)[0].reshape(dp, own_d, -1)
        tiles0 = gate(tiles0, arrived1)
        arrived = lax.all_to_all(tiles0, "dp", split_axis=0, concat_axis=0, tiled=True)
        sum0 = arrived.astype(F32).sum(axis=0)
        sum1 = gate(arrived1, tiles0).astype(F32).sum(axis=0)

    with jax.named_scope("boundary"):

        def own_rows(parts):
            step = ROWS // tensor
            return jnp.stack(
                [
                    lax.dynamic_slice_in_dim(jnp.concatenate(a[:2], axis=1), place[0] * step, step, 0)
                    for a in parts
                ]
            ).astype(F32)

        g_around = around(*zip(*g_parts), place, tiles0)
        gx_all = summed_around(g_around) + own_rows(g0)
        y_around = around(*zip(*y_parts), place, g_around[0])
        y_all = summed_around(y_around) + own_rows(x1)
        y_all = y_all + (shift_own[1][4:5] + shift_own[1][5:6])
        other = swap(pick(y_all, gx_all))
        boundary = pick(
            jnp.concatenate([gx_all, other], axis=2), jnp.concatenate([other, y_all], axis=2)
        )[None]

    with jax.named_scope("small_grads"):
        own = sum0[:, COLS : COLS + 16].T.reshape(2, 8, own_d)
        total, rest = own[:, :4], own[:, 4:]
        for offset in (0, 1):
            total = total + along_ring(total, "tensor", offset)
        both = jnp.concatenate([total, rest], axis=1)
        both = pick(both[0], both[1]) + swap(pick(both[1], both[0]))
        gains = both[None, 0:2]
        gy_sum = both[4] * 0.5
        shift = jnp.stack([both[2], both[3], gy_sum, gy_sum])[None]
        expand_bias_grad = both[5].reshape(1, 1, own_d)
        joint_bias_grad = both[6, :48].reshape(1, 3, 1, 16)
        sum0 = sum0[:, :COLS]

    with jax.named_scope("outputs"):
        other = swap(pick(sum1, sum0))
        low = pick(sum0, other)
        high = pick(other, sum1)
        joint = jnp.concatenate(
            [low[:, :QKV].reshape(own_d, 3, WIDTH), high[:, :QKV].reshape(own_d, 3, WIDTH)], axis=2
        )[None]
        expand = jnp.concatenate([low[:, COL_E:COL_O], high[:, COL_E:COL_O]], axis=1)[None]
        output = jnp.concatenate([low[:, COL_O:COL_S], high[:, COL_O:COL_S]], axis=1).T[None]
        shrink = jnp.concatenate([low[:, COL_S:], high[:, COL_S:]], axis=1).T[None]

    return (
        boundary,
        joint,
        joint_bias_grad,
        output,
        expand,
        expand_bias_grad,
        shrink,
        gains,
        shift,
    )


def solution(mesh):
    placed = (
        P(None, ("dp", "tensor"), None),
        P(None, ("dp", "tensor"), None),
        P(None, "dp"),
        P("pipe", "dp", None, "tensor"),
        P("pipe", None, "tensor", "dp"),
        P("pipe", "tensor", "dp"),
        P("pipe", "dp", "tensor"),
        P("pipe", "tensor", "dp"),
        P("pipe", "tensor", "dp"),
        P("pipe", None, "dp"),
        P("pipe", None, "dp"),
    )
    return jax.shard_map(
        shards,
        mesh=mesh,
        in_specs=placed,
        out_specs=(
            P("pipe", None, ("dp", "tensor"), None),
            P("pipe", "dp", None, "tensor"),
            P("pipe", None, "tensor", "dp"),
            P("pipe", "tensor", "dp"),
            P("pipe", "dp", "tensor"),
            P("pipe", "tensor", "dp"),
            P("pipe", "tensor", "dp"),
            P("pipe", None, "dp"),
            P("pipe", None, "dp"),
        ),
        check_vma=False,
    )
```

```python
import functools

import jax
import jax.numpy as jnp
from jax import lax
from jax.experimental import pallas as pl
from jax.experimental.pallas import tpu as pltpu
from jax.sharding import PartitionSpec as P

HEAD_DIM = 64
ROTARY = 16
EPS = 1e-05

MODEL = 1024
ROWS = 512
CHUNK = 256
WIDTH = 128
INNER = 512
HALF = MODEL // 2

QKV = 3 * WIDTH
COL_E = QKV
COL_O = QKV + INNER
COL_S = COL_O + WIDTH
COLS = COL_S + INNER

F32 = jnp.float32
BF16 = jnp.bfloat16


def nn(a, b):
    return lax.dot_general(a, b, (((1,), (0,)), ((), ())), preferred_element_type=F32)


def nt(a, b):
    return lax.dot_general(a, b, (((1,), (1,)), ((), ())), preferred_element_type=F32)


def tn(a, b):
    return lax.dot_general(a, b, (((0,), (0,)), ((), ())), preferred_element_type=F32)


def normalised(x):
    centred = x - jnp.mean(x, axis=1, keepdims=True)
    rstd = lax.rsqrt(jnp.mean(centred * centred, axis=1, keepdims=True) + EPS)
    return centred * rstd, rstd


def gelu_both(h):
    a = jnp.abs(h) * 0.7071067811865476
    t = 1.0 / (1.0 + 0.3275911 * a)
    poly = 1.061405429 * t - 1.453152027
    poly = poly * t + 1.421413741
    poly = poly * t - 0.284496736
    poly = poly * t + 0.254829592
    e = jnp.exp(-0.5 * h * h)
    tail = 0.5 * poly * t * e
    cdf = jnp.where(h >= 0, 1.0 - tail, tail)
    return h * cdf, cdf + h * (e * 0.3989422804014327)


def head_mask(v, head):
    lane = lax.broadcasted_iota(jnp.int32, v.shape, 1)
    return jnp.where((lane >= HEAD_DIM) == (head == 1), v, jnp.zeros_like(v))


def turn(u, c, s1, s2):
    return u * c + pltpu.roll(u, WIDTH - 8, 1) * s1 + pltpu.roll(u, 8, 1) * s2


def turn_back(w, c, s1, s2):
    return w * c + pltpu.roll(w * s2, WIDTH - 8, 1) + pltpu.roll(w * s1, 8, 1)


def allowed(i, seg_col, seg_row):
    keys = (i + 1) * CHUNK
    shape = (CHUNK, keys)
    q_at = lax.broadcasted_iota(jnp.int32, shape, 0) + i * CHUNK
    k_at = lax.broadcasted_iota(jnp.int32, shape, 1)
    same = seg_col[i * CHUNK : keys, :] == seg_row[:, :keys]
    return same & (k_at <= q_at)


def placed_half(first, row):
    none = jnp.zeros_like(row)
    return jnp.where(
        first, jnp.concatenate([row, none], axis=1), jnp.concatenate([none, row], axis=1)
    )


def store_parts(first, rows, value, keep, send):
    low, high = value[:, :HALF].astype(BF16), value[:, HALF:].astype(BF16)

    @pl.when(first)
    def _():
        keep[rows, :] = low
        send[rows, :] = high

    @pl.when(jnp.logical_not(first))
    def _():
        keep[rows, :] = high
        send[rows, :] = low


def forward_rows(x_of, w, sm, bq, be, tabs, normed, mixed, q, k, v, active, slope, stats=None):
    for i in range(ROWS // CHUNK):
        rows = slice(i * CHUNK, (i + 1) * CHUNK)
        xhat, rstd = normalised(x_of(rows))
        if stats:
            stats[0][rows, :], stats[1][rows, :] = xhat, rstd
        normed[rows, :] = (xhat * sm[0:1, :] + sm[2:3, :]).astype(BF16)
        mixed[rows, :] = (xhat * sm[1:2, :] + sm[3:4, :]).astype(BF16)
        joint = nn(normed[rows, :], w[:, :QKV]) + bq[...]
        c, s1, s2 = tabs[0, rows, :], tabs[1, rows, :], tabs[2, rows, :]
        q[rows, :] = turn(joint[:, :WIDTH], c, s1, s2).astype(BF16)
        k[rows, :] = turn(joint[:, WIDTH : 2 * WIDTH], c, s1, s2).astype(BF16)
        v[rows, :] = joint[:, 2 * WIDTH :].astype(BF16)
        hidden = nn(mixed[rows, :], w[:, COL_E:COL_O]) + be[...]
        act, dact = gelu_both(hidden)
        active[rows, :] = act.astype(BF16)
        slope[rows, :] = dact.astype(slope.dtype)


def attend(q, k, v, seg_col, seg_row, att, lse):
    for i in range(ROWS // CHUNK):
        rows = slice(i * CHUNK, (i + 1) * CHUNK)
        keys = slice(0, (i + 1) * CHUNK)
        mask = allowed(i, seg_col[...], seg_row[...])
        out, tops = None, []
        for head in range(2):
            s = nt(head_mask(q[rows, :], head) * 0.125, k[keys, :])
            s = jnp.where(mask, s, -1e30)
            top = jnp.max(s, axis=1, keepdims=True)
            e = jnp.exp(s - top)
            total = jnp.sum(e, axis=1, keepdims=True)
            probs = (e * (1.0 / total)).astype(BF16)
            part = nn(probs, head_mask(v[keys, :], head))
            out = part if out is None else out + part
            tops.append(top + jnp.log(total))
        att[rows, :] = out.astype(BF16)
        lane = lax.broadcasted_iota(jnp.int32, (CHUNK, WIDTH), 1)
        lse[rows, :] = jnp.where(lane < HEAD_DIM, tops[0], tops[1])


def branch_out(first, w, att, active, keep, send):
    for i in range(ROWS // CHUNK):
        rows = slice(i * CHUNK, (i + 1) * CHUNK)
        branch = nt(att[rows, :], w[:, COL_O:COL_S]) + nt(active[rows, :], w[:, COL_S:])
        store_parts(first, rows, branch, keep, send)


def backward_rows(
    first, stats_of, gy_of, w, sm, tabs, seg_col, seg_row, q, k, v, lse, slope,
    gatt, gk, gv, gq, gjoint, ghid, keep, send, sums,
):
    for i in range(ROWS // CHUNK):
        rows = slice(i * CHUNK, (i + 1) * CHUNK)
        gy = gy_of(rows)
        gatt[rows, :] = nn(gy, w[:, COL_O:COL_S]).astype(BF16)
        gact = nn(gy, w[:, COL_S:])
        ghid[rows, :] = (gact * slope[rows, :].astype(F32)).astype(BF16)
    gk[...] = jnp.zeros_like(gk)
    gv[...] = jnp.zeros_like(gv)
    for i in range(ROWS // CHUNK):
        rows = slice(i * CHUNK, (i + 1) * CHUNK)
        keys = slice(0, (i + 1) * CHUNK)
        mask = allowed(i, seg_col[...], seg_row[...])
        out = None
        for head in range(2):
            qh = head_mask(q[rows, :], head) * 0.125
            gh = head_mask(gatt[rows, :], head)
            s = nt(qh, k[keys, :])
            at = head * HEAD_DIM
            probs = jnp.where(mask, jnp.exp(s - lse[rows, at : at + 1]), 0.0)
            gp = nt(gh, v[keys, :])
            dot = jnp.sum(probs * gp, axis=1, keepdims=True)
            gs = (probs * (gp - dot)).astype(BF16)
            part = nn(gs, head_mask(k[keys, :], head) * 0.125)
            out = part if out is None else out + part
            gk[keys, :] += tn(gs, qh)
            gv[keys, :] += tn(probs.astype(BF16), gh)
        gq[rows, :] = out
    total = [None] * 7
    for i in range(ROWS // CHUNK):
        rows = slice(i * CHUNK, (i + 1) * CHUNK)
        c, s1, s2 = tabs[0, rows, :], tabs[1, rows, :], tabs[2, rows, :]
        gjoint[rows, :WIDTH] = turn_back(gq[rows, :], c, s1, s2).astype(BF16)
        gjoint[rows, WIDTH : 2 * WIDTH] = turn_back(gk[rows, :], c, s1, s2).astype(BF16)
        gjoint[rows, 2 * WIDTH :] = gv[rows, :].astype(BF16)
        gj, gh = gjoint[rows, :], ghid[rows, :]
        gn = nt(gj, w[:, :QKV])
        gm = nt(gh, w[:, COL_E:COL_O])
        xhat, rstd = stats_of(rows)
        h = gn * sm[0:1, :] + gm * sm[1:2, :]
        gx = h - jnp.mean(h, axis=1, keepdims=True)
        gx = (gx - xhat * jnp.mean(h * xhat, axis=1, keepdims=True)) * rstd
        store_parts(first, rows, gx, keep, send)
        found = (
            jnp.sum(gn * xhat, axis=0, keepdims=True),
            jnp.sum(gm * xhat, axis=0, keepdims=True),
            jnp.sum(gn, axis=0, keepdims=True),
            jnp.sum(gm, axis=0, keepdims=True),
            jnp.sum(gy_of(rows).astype(F32), axis=0, keepdims=True),
            placed_half(first, jnp.sum(gh.astype(F32), axis=0, keepdims=True)),
            jnp.concatenate(
                [jnp.sum(gj.astype(F32), axis=0, keepdims=True), jnp.zeros((1, MODEL - QKV), F32)],
                axis=1,
            ),
        )
        total = [a if t is None else t + a for t, a in zip(total, found)]
    for n, t in enumerate(total):
        sums[n : n + 1, :] = t
    sums[7:8, :] = jnp.zeros((1, MODEL), F32)


def join(first, out, a0, a1, b0, b1):
    step = HALF // 2

    @pl.when(first)
    def _():
        for n, part in enumerate((a0, a1, b0, b1)):
            out[:, n * step : (n + 1) * step] = part[...]

    @pl.when(jnp.logical_not(first))
    def _():
        for n, part in enumerate((b0, b1, a0, a1)):
            out[:, n * step : (n + 1) * step] = part[...]


def first_forward(
    core, x, w, sm, bq, be, tabs, seg_col, seg_row,
    keep, send, normed, mixed, q, k, v, att, lse, active, slope, zero,
):
    first = core[0] == 0
    zero[...] = jnp.zeros_like(zero)
    forward_rows(
        lambda rows: x[rows, :].astype(F32), w, sm, bq, be, tabs, normed, mixed, q, k, v, active, slope
    )
    attend(q, k, v, seg_col, seg_row, att, lse)
    branch_out(first, w, att, active, keep, send)


def both_ways(
    core, xa0, xa1, xb0, xb1, gy, w, sm, bq, be, tabs, seg_col, seg_row,
    keep_y, send_y, keep_g, send_g, normed, mixed, att, active, gjoint, ghid, sums, zero,
    x, q, k, v, lse, slope, gatt, gk, gv, gq, xhat, rstd,
):
    first = core[0] == 0
    zero[...] = jnp.zeros_like(zero)
    join(first, x, xa0, xa1, xb0, xb1)
    x_of = lambda rows: x[rows, :].astype(F32)
    stats = (xhat, rstd)
    forward_rows(x_of, w, sm, bq, be, tabs, normed, mixed, q, k, v, active, slope, stats)
    attend(q, k, v, seg_col, seg_row, att, lse)
    backward_rows(
        first, lambda rows: (xhat[rows, :], rstd[rows, :]), lambda rows: gy[rows, :], w, sm, tabs,
        seg_col, seg_row, q, k, v, lse, slope, gatt, gk, gv, gq, gjoint, ghid, keep_g, send_g, sums,
    )
    branch_out(first, w, att, active, keep_y, send_y)


def first_backward(
    core, x, ga0, ga1, gb0, gb1, w, sm, tabs, seg_col, seg_row, q, k, v, lse, slope,
    keep_g, send_g, gjoint, ghid, gy, sums, zero,
    gatt, gk, gv, gq,
):
    first = core[0] == 0
    zero[...] = jnp.zeros_like(zero)
    join(first, gy, ga0, ga1, gb0, gb1)
    backward_rows(
        first, lambda rows: normalised(x[rows, :].astype(F32)), lambda rows: gy[rows, :], w, sm, tabs,
        seg_col, seg_row, q, k, v, lse, slope, gatt, gk, gv, gq, gjoint, ghid, keep_g, send_g, sums,
    )


def weight_grads(n0, n1, m0, m1, g0, g1, j0, j1, h0, h1, a0, a1, c0, c1, out):
    out[:, :QKV] = (tn(n0[...], j0[...]) + tn(n1[...], j1[...])).astype(BF16)
    out[:, COL_E:COL_O] = (tn(m0[...], h0[...]) + tn(m1[...], h1[...])).astype(BF16)
    out[:, COL_O:COL_S] = (tn(g0[...], a0[...]) + tn(g1[...], a1[...])).astype(BF16)
    out[:, COL_S:COLS] = (tn(g0[...], c0[...]) + tn(g1[...], c1[...])).astype(BF16)


def owner_order(first, row):
    shape = (QKV, HALF)
    at = lax.broadcasted_iota(jnp.int32, shape, 0)
    col = lax.broadcasted_iota(jnp.int32, shape, 1)
    part = (col // 16) % 4
    wanted = jnp.where(part < 3, part * WIDTH + (col // 64) * 16 + col % 16, -1)
    moved = nn(row.astype(BF16), jnp.where(at == wanted, 1.0, 0.0).astype(BF16))
    return placed_half(first, moved)


def row_grads(core, s00, s01, s10, s11, rows):
    for n, (a, b) in enumerate(((s00, s01), (s10, s11))):
        total = a[...] + b[...]
        rows[8 * n : 8 * n + 8, :] = total
        moved = owner_order(core[0] == 0, total[:, :QKV])
        rows[8 * n + 6 : 8 * n + 7, :] = moved[6:7, :]


def write_out(core, sum0, got0, sum1, got1, rows, joint, expand, output, shrink, gains, shift, hid, bias):
    def write(low, high, at):
        for t in range(3):
            joint[t, :, :WIDTH] = low[:, t * WIDTH : (t + 1) * WIDTH]
            joint[t, :, WIDTH:] = high[:, t * WIDTH : (t + 1) * WIDTH]
        for out, start, end in ((expand, COL_E, COL_O), (output, COL_O, COL_S), (shrink, COL_S, COLS)):
            out[:, : end - start] = low[:, start:end]
            out[:, end - start :] = high[:, start:end]
        gains[...] = rows[at : at + 2, :]
        shift[...] = rows[at + 2 : at + 6, :]
        shift[3:4, :] = rows[at + 4 : at + 5, :]
        hid[...] = rows[at + 5 : at + 6, :]
        for t in range(3):
            bias[t : t + 1, :] = rows[at + 6 : at + 7, 16 * t : 16 * t + 16]

    @pl.when(core[0] == 0)
    def _():
        write(sum0, got0, 0)

    @pl.when(core[0] != 0)
    def _():
        write(got1, sum1, 8)


def write_boundary(core, gx, y, other, out):
    @pl.when(core[0] == 0)
    def _():
        out[:, :, :HALF] = gx[...]
        out[:, :, HALF:] = other[...]

    @pl.when(core[0] != 0)
    def _():
        out[:, :, :HALF] = other[...]
        out[:, :, HALF:] = y[...]


def shaped(*dims, dtype=BF16):
    return jax.ShapeDtypeStruct(dims, dtype)


def call(kernel, n_in, outs, scratch, flops, name, after=()):
    whole = pl.BlockSpec(memory_space=pltpu.VMEM)

    def body(*refs):
        kernel(*refs[:n_in], *refs[n_in + len(after) :])

    made = pl.pallas_call(
        body,
        in_specs=[pl.BlockSpec(memory_space=pltpu.SMEM)]
        + [whole] * (n_in - 1)
        + [pl.BlockSpec(memory_space=pl.ANY)] * len(after),
        out_specs=[whole] * len(outs),
        out_shape=outs,
        scratch_shapes=scratch,
        compiler_params=pltpu.CompilerParams(vmem_limit_bytes=60 * 2**20),
        cost_estimate=pl.CostEstimate(flops=flops, bytes_accessed=8 * 2**20, transcendentals=2**20),
        name=name,
    )
    return lambda *args: made(*args, *after)


ZERO = shaped(1, HALF // 2, dtype=F32)


def tall(width, dtype=BF16):
    return shaped(ROWS, width, dtype=dtype)


def forward_call(*args, after=()):
    outs = [tall(HALF), tall(HALF), tall(MODEL), tall(MODEL)]
    outs += [tall(WIDTH)] * 4 + [tall(WIDTH, F32), tall(INNER), tall(INNER), ZERO]
    return call(first_forward, len(args), outs, [], 2**31, "layer_forward", after)(*args)


def both_call(*args, after=()):
    outs = [tall(HALF)] * 4 + [tall(MODEL)] * 2 + [tall(WIDTH), tall(INNER), tall(QKV), tall(INNER)]
    outs += [shaped(8, MODEL, dtype=F32), ZERO]
    scratch = [pltpu.VMEM((ROWS, MODEL), BF16)] + [pltpu.VMEM((ROWS, WIDTH), BF16)] * 3
    scratch += [pltpu.VMEM((ROWS, WIDTH), F32), pltpu.VMEM((ROWS, INNER), F32)]
    scratch += [pltpu.VMEM((ROWS, WIDTH), BF16)] + [pltpu.VMEM((ROWS, WIDTH), F32)] * 3
    scratch += [pltpu.VMEM((ROWS, MODEL), F32), pltpu.VMEM((ROWS, 1), F32)]
    return call(both_ways, len(args), outs, scratch, 2**32, "layer_both", after)(*args)


def backward_call(*args, after=()):
    outs = [tall(HALF)] * 2 + [tall(QKV), tall(INNER), tall(MODEL), shaped(8, MODEL, dtype=F32), ZERO]
    scratch = [pltpu.VMEM((ROWS, WIDTH), BF16)] + [pltpu.VMEM((ROWS, WIDTH), F32)] * 3
    return call(first_backward, len(args), outs, scratch, 2**31, "layer_backward", after)(*args)


def grads_call(*args, sums=(), after=()):
    blocks = 4
    step = MODEL // blocks
    extra = 128 if sums else 0
    cut = pl.BlockSpec((ROWS, step), lambda i: (0, i))
    rest = [pl.BlockSpec(a.shape, lambda i: (0, 0)) for a in (*args[6:], *sums[1:])]
    n_in = len(args)
    n_all = n_in + len(sums) + len(after)

    def body(*refs):
        first = len(sums[:1])
        out, token, *rows = refs[n_all:]
        weight_grads(*refs[first : first + n_in], out)
        token[...] = jnp.zeros_like(token)
        if sums:
            rows = rows[0]

            @pl.when(pl.program_id(0) == 0)
            def _():
                rows[...] = jnp.zeros_like(rows)
                row_grads(refs[0], *refs[1 + n_in : 5 + n_in], rows)

            at = pl.multiple_of(pl.program_id(0) * step, step)
            out[:, COLS:] = rows[:, pl.ds(at, step)].T.astype(BF16)

    return pl.pallas_call(
        body,
        grid=(blocks,),
        in_specs=[pl.BlockSpec(memory_space=pltpu.SMEM)] * len(sums[:1])
        + [cut] * 6
        + rest
        + [pl.BlockSpec(memory_space=pl.ANY)] * len(after),
        out_specs=[
            pl.BlockSpec((step, COLS + extra), lambda i: (i, 0)),
            pl.BlockSpec(ZERO.shape, lambda i: (0, 0)),
        ],
        out_shape=[shaped(MODEL, COLS + extra), ZERO],
        scratch_shapes=[pltpu.VMEM((128, MODEL), F32)] if sums else [],
        compiler_params=pltpu.CompilerParams(vmem_limit_bytes=60 * 2**20),
        cost_estimate=pl.CostEstimate(flops=2**32, bytes_accessed=2**23, transcendentals=0),
        name="weight_grads",
    )(*sums[:1], *args, *sums[1:], *after)


def gate(x, *after):
    anywhere = pl.BlockSpec(memory_space=pl.ANY)
    return pl.pallas_call(
        lambda *refs: None,
        in_specs=[anywhere] * (1 + len(after)),
        out_specs=anywhere,
        out_shape=shaped(*x.shape, dtype=x.dtype),
        input_output_aliases={0: 0},
        name="gate",
    )(x, *after)


def assemble(place, own, before, behind, far0, far1, out0, out1, *parts):
    step = own.shape[1]
    ring = ROWS // step

    def put(out, value, distance):
        at = lax.rem(place[0] + distance, ring) * step
        out[pl.ds(pl.multiple_of(at, step), step), :] = value

    for n, (out, far) in enumerate(((out0, far0), (out1, far1))):
        put(out, own[n], 0)
        put(out, before[n], ring - 1)
        put(out, behind[n], 1)
        put(out, far[...], 2)

    quarter = HALF // 2
    for core in range(2):

        @pl.when(place[1] == core)
        def _():
            for n, part in enumerate(parts):
                at = core * HALF + (n % 2) * quarter
                part[...] = (out0 if n < 2 else out1)[:, at : at + quarter]


def around_ring(x, by):
    ring = lax.axis_size("tensor")
    return lax.ppermute(x, "tensor", [(i, (i + by) % ring) for i in range(ring)])


def gathered_rows(x, place):
    before, behind = around_ring(x, 1), around_ring(x, -1)
    far0, far1 = around_ring(before[0], 1), around_ring(behind[1], -1)
    outs = [tall(MODEL)] * 2 + [tall(HALF // 2)] * 4
    args = (place, x, before, behind, far0, far1)
    out0, out1, *parts = call(assemble, 6, outs, [], 2**20, "assemble")(*args)
    return [out0, out1], [parts[:2], parts[2:]]


def add_blocks(offset, place, k0, g0, k1, g1, keep, send):
    step = keep.shape[2]
    ring = ROWS // step
    first = jnp.where(place[0] % 2 == offset, 1, ring - 1)
    for out, which in ((keep, (0, ring - first)), (send, (first, 2))):
        for n, distance in enumerate(which):
            at = lax.rem(place[0] + distance, ring) * step
            rows = pl.ds(pl.multiple_of(at, step), step)
            out[n, 0] = (k0[rows, :].astype(F32) + g0[rows, :].astype(F32)).astype(BF16)
            out[n, 1] = (k1[rows, :].astype(F32) + g1[rows, :].astype(F32)).astype(BF16)


def add_blocks_call(offset, place, keeps, gots):
    outs = [shaped(2, 2, ROWS // lax.axis_size("tensor"), HALF)] * 2
    args = (place, keeps[0], gots[0], keeps[1], gots[1])
    return call(functools.partial(add_blocks, offset), 5, outs, [], 2**20, "add_blocks")(*args)


def swap(x):
    return lax.ppermute(x, "pipe", [(0, 1), (1, 0)])


def along_ring(x, axis, offset, stride=1, side=4):
    pairs = []
    for g in range(lax.axis_size(axis)):
        at = (g // stride) % side
        to = (at + 1) % side if at % 2 == offset else (at - 1) % side
        pairs.append((g, g + (to - at) * stride))
    return lax.ppermute(x, axis, pairs)


def added(a, b, row=None):
    total = a.astype(F32) + b.astype(F32)
    return (total if row is None else total + row).astype(BF16)


def halves(a):
    return [a[:, : HALF // 2], a[:, HALF // 2 :]]


class SumOverTensor:
    def __init__(self, keep, send):
        self.chip = halves(added(keep, swap(send)))

    def second(self, zero=None):
        self.pair = [added(a, along_ring(a, "tensor", n), zero) for n, a in enumerate(self.chip)]

    def finish(self, base, rows, zero=None):
        mine = []
        for n, (a, b) in enumerate(zip(self.pair, base)):
            total = a.astype(F32) + along_ring(a, "tensor", 1 - n).astype(F32) + b.astype(F32)
            for row in (rows and rows[n], zero):
                total = total if row is None else total + row
            mine.append(total.astype(BF16))
        return (*mine, *[swap(a) for a in mine])


def summed_blocks(keeps, sends, place, offset, after):
    gots = [swap(gate(s, after)) for s in sends]
    keep, send = add_blocks_call(offset, place, keeps, gots)
    half = added(keep, along_ring(send, "tensor", offset))
    return half[0].astype(F32) + along_ring(half[1], "tensor", 1 - offset).astype(F32)


def rotary_tables(segment_row):
    places = jnp.arange(ROWS, dtype=jnp.int32)
    before = jnp.sum((segment_row[None, :] < segment_row[:, None]).astype(jnp.int32), axis=1)
    positions = (places - before).astype(F32)
    half_rot = ROTARY // 2
    lane = jnp.arange(WIDTH, dtype=jnp.int32)[None, :] % HEAD_DIM
    inverse = 10000.0 ** (-(lane % half_rot).astype(F32) * 2.0 / ROTARY)
    angles = positions[:, None] * inverse
    cosine, sine = jnp.cos(angles), jnp.sin(angles)
    c = jnp.where(lane < ROTARY, cosine, 1.0)
    s1 = jnp.where(lane < half_rot, -sine, 0.0)
    s2 = jnp.where((lane >= half_rot) & (lane < ROTARY), sine, 0.0)
    return jnp.stack([c, s1, s2])


def shards(
    inputs, upstream, segments, joint_weight, joint_bias, output_weight, expand_weight,
    expand_bias, shrink_weight, norm_gains, shift_rows,
):
    dp = lax.axis_size("dp")
    tensor = lax.axis_size("tensor")
    core = lax.axis_index("pipe")
    first = core == 0
    core_arg = core.astype(jnp.int32).reshape(1)
    micros = inputs.shape[0]
    own_d = MODEL // dp

    def pick(a, b):
        return jnp.where(first, a, b)

    def packed(h):
        return jnp.concatenate(
            [
                joint_weight[0][:, :, h * WIDTH : (h + 1) * WIDTH].reshape(own_d, QKV),
                expand_weight[0][:, h * INNER : (h + 1) * INNER],
                output_weight[0][h * WIDTH : (h + 1) * WIDTH].T,
                shrink_weight[0][h * INNER : (h + 1) * INNER].T,
            ],
            axis=1,
        )

    with jax.named_scope("weights"):
        pack_a, pack_b = packed(0), packed(1)
        stay = pick(pack_a, pack_b)
        came = swap(pick(pack_b, pack_a))
        w0 = lax.all_gather(pick(stay, came), "dp", axis=0, tiled=True)
        w1 = lax.all_gather(pick(came, stay), "dp", axis=0, tiled=True)

    with jax.named_scope("small_parameters"):
        bias_row = jnp.pad(joint_bias[0, :, 0, :].reshape(1, -1), ((0, 0), (0, own_d - 3 * 16)))
        small = jnp.concatenate([norm_gains[0], shift_rows[0], expand_bias[0], bias_row], axis=0)
        copies = jnp.broadcast_to(small, (2 * dp, *small.shape))
        small = lax.all_to_all(copies, ("pipe", "dp"), split_axis=0, concat_axis=0, tiled=True)
        small = small.reshape(2, dp, 8, own_d).astype(F32)
        rows = small.transpose(0, 2, 1, 3).reshape(2, 8, MODEL)
        be = [pick(rows[n, 6:7, :INNER], rows[n, 6:7, INNER:]) for n in range(2)]
        bq_all = small[:, :, 7, :48].reshape(2, dp, 3, 16).transpose(0, 2, 1, 3).reshape(2, 3, 256)
        bq = [
            pick(bq_all[n, :, :WIDTH], bq_all[n, :, WIDTH:]).reshape(1, QKV) for n in range(2)
        ]
        shift_own = [pick(rows[n, :, :HALF], rows[n, :, HALF:]) for n in range(2)]

    place = lax.axis_index("tensor").astype(jnp.int32).reshape(1)
    with jax.named_scope("activations_in"):
        both_places = jnp.concatenate([place, core_arg])
        x0, x0_half = gathered_rows(inputs, both_places)
        gy1, gy1_half = gathered_rows(upstream, both_places)

    with jax.named_scope("tables"):
        tabs = [rotary_tables(segments[m]) for m in range(micros)]
        seg_col = [segments[m].reshape(ROWS, 1) for m in range(micros)]
        seg_row = [segments[m].reshape(1, ROWS) for m in range(micros)]

    kept, sums0 = [], []
    after = (*tabs, *gy1)
    for m in range(micros):
        with jax.named_scope("first_layer"):
            keep, send, *saved, zero = forward_call(
                core_arg, x0[m], w0, rows[0], bq[0], be[0], tabs[m], seg_col[m], seg_row[m], after=after
            )
            if m:
                sums0[0].second(zero)
                send = gate(send, *sums0[0].pair)
            sums0.append(SumOverTensor(keep, send))
            after = tuple(sums0[m].chip)
            kept.append(saved)
    sums0[1].second()

    x1, made1, y_parts, sums1 = [], [], [], []
    shift = halves(shift_own[0][4:5] + shift_own[0][5:6])
    for m in range(micros):
        with jax.named_scope("second_layer"):
            if m == 0:
                x1.append(sums0[0].finish(x0_half[0], shift))
                after = tuple(sums0[1].pair)
            else:
                after = tuple(sums1[0].chip)
            keep_y, send_y, keep_g, send_g, *made, zero = both_call(
                core_arg, *x1[m], gy1[m], w1, rows[1], bq[1], be[1], tabs[m], seg_col[m], seg_row[m],
                after=after,
            )
            if m == 0:
                x1.append(sums0[1].finish(x0_half[1], shift, zero))
            else:
                sums1[0].second(zero)
                send_g = gate(send_g, *sums1[0].pair)
            sums1.append(SumOverTensor(keep_g, send_g))
            y_parts.append((keep_y, send_y))
            made1.append(made)

    def pairs(made, n):
        return [made[m][n] for m in range(micros)]

    with jax.named_scope("second_layer_grads"):
        args = []
        for n in (0, 1, None, 4, 5, 2, 3):
            args += gy1 if n is None else pairs(made1, n)
        grads1, zero = grads_call(*args, after=(*sums1[1].chip, *sums1[0].pair))
        g0 = [sums1[0].finish(gy1_half[0], None, zero)]
        sums1[1].second(zero)
        tiles1 = gate(grads1.reshape(dp, own_d, -1), *g0[0][:2], *sums1[1].pair)
        arrived1 = lax.all_to_all(tiles1, "dp", split_axis=0, concat_axis=0, tiled=True)

    made0, g_parts = [], []
    after = tuple(sums1[1].pair)
    for m in range(micros):
        with jax.named_scope("first_layer_back"):
            if m:
                g0.append(sums1[m].finish(gy1_half[m], None, zero))
            normed, mixed, q, k, v, att, lse, active, slope = kept[m]
            keep_g, send_g, gjoint, ghid, gy, sums, zero = backward_call(
                core_arg, x0[m], *g0[m], w0, rows[0], tabs[m], seg_col[m], seg_row[m],
                q, k, v, lse, slope, after=after,
            )
            after = (sums,)
            g_parts.append((keep_g, send_g))
            made0.append((normed, mixed, att, active, gjoint, ghid, sums, gy))

    with jax.named_scope("first_layer_grads"):
        args = []
        for n in (0, 1, 7, 4, 5, 2, 3):
            args += pairs(made0, n)
        sums = (core_arg, made0[0][6], made0[1][6], made1[0][6], made1[1][6])
        grads0, _ = grads_call(*args, sums=sums)
        tiles0 = gate(grads0.reshape(dp, own_d, -1), arrived1)
        arrived0 = lax.all_to_all(tiles0, "dp", split_axis=0, concat_axis=0, tiled=True)

    with jax.named_scope("boundary"):

        def own_rows(parts):
            step = ROWS // tensor
            return jnp.stack(
                [
                    lax.dynamic_slice_in_dim(jnp.concatenate(a[:2], axis=1), place[0] * step, step, 0)
                    for a in parts
                ]
            ).astype(F32)

        gx_all = summed_blocks(*zip(*g_parts), place, 0, tiles0) + own_rows(g0)
        y_all = summed_blocks(*zip(*y_parts), place, 1, tiles0) + own_rows(x1)
        y_all = y_all + (shift_own[1][4:5] + shift_own[1][5:6])
        other = swap(pick(y_all, gx_all))
        outs = [shaped(2, ROWS // tensor, MODEL, dtype=F32)]
        args = (core_arg, gx_all, y_all, other)
        boundary = call(write_boundary, 4, outs, [], 2**20, "write_boundary")(*args)[0][None]

    with jax.named_scope("outputs"):
        sum1 = gate(arrived1, tiles0).astype(F32).sum(axis=0)
        got1 = lax.ppermute(sum1, "pipe", [(0, 1)])
        sum0 = arrived0.astype(F32).sum(axis=0)
        got0 = lax.ppermute(sum0[:, :COLS], "pipe", [(1, 0)])
        rows = sum0[:, COLS : COLS + 16].T
        total = rows
        for by in range(1, tensor):
            total = total + around_ring(rows, by)
        at = jnp.arange(16, dtype=jnp.int32)[:, None] % 8
        total = jnp.where(at < 4, total, rows)
        total = jnp.where(at == 4, total, total + swap(total))
        outs = [(3, own_d, 2 * WIDTH), (own_d, 2 * INNER), (own_d, 2 * WIDTH), (own_d, 2 * INNER)]
        outs += [(2, own_d), (4, own_d), (1, own_d), (3, 16)]
        outs = [shaped(*dims, dtype=F32) for dims in outs]
        args = (core_arg, sum0, got0, sum1, got1, total)
        made = call(write_out, 6, outs, [], 2**20, "write_out")(*args)
        joint = made[0].transpose(1, 0, 2)[None]
        expand, gains, shift = [made[n][None] for n in (1, 4, 5)]
        output, shrink = made[2].T[None], made[3].T[None]
        expand_bias_grad = made[6].reshape(1, 1, own_d)
        joint_bias_grad = made[7].reshape(1, 3, 1, 16)

    return (
        boundary,
        joint,
        joint_bias_grad,
        output,
        expand,
        expand_bias_grad,
        shrink,
        gains,
        shift,
    )


def solution(mesh):
    placed = (
        P(None, ("dp", "tensor"), None),
        P(None, ("dp", "tensor"), None),
        P(None, "dp"),
        P("pipe", "dp", None, "tensor"),
        P("pipe", None, "tensor", "dp"),
        P("pipe", "tensor", "dp"),
        P("pipe", "dp", "tensor"),
        P("pipe", "tensor", "dp"),
        P("pipe", "tensor", "dp"),
        P("pipe", None, "dp"),
        P("pipe", None, "dp"),
    )
    return jax.shard_map(
        shards,
        mesh=mesh,
        in_specs=placed,
        out_specs=(
            P("pipe", None, ("dp", "tensor"), None),
            P("pipe", "dp", None, "tensor"),
            P("pipe", None, "tensor", "dp"),
            P("pipe", "tensor", "dp"),
            P("pipe", "dp", "tensor"),
            P("pipe", "tensor", "dp"),
            P("pipe", "tensor", "dp"),
            P("pipe", None, "dp"),
            P("pipe", None, "dp"),
        ),
        check_vma=False,
    )
```

```python
import functools

import jax
import jax.numpy as jnp
from jax import lax
from jax.experimental import pallas as pl
from jax.experimental.pallas import tpu as pltpu
from jax.sharding import PartitionSpec as P

HEAD_DIM = 64
ROTARY = 16
EPS = 1e-05

MODEL = 1024
ROWS = 512
CHUNK = 256
WIDTH = 128
INNER = 512
HALF = MODEL // 2

QKV = 3 * WIDTH
COL_E = QKV
COL_O = QKV + INNER
COL_S = COL_O + WIDTH
COLS = COL_S + INNER

F32 = jnp.float32
BF16 = jnp.bfloat16


def nn(a, b):
    return lax.dot_general(a, b, (((1,), (0,)), ((), ())), preferred_element_type=F32)


def nt(a, b):
    return lax.dot_general(a, b, (((1,), (1,)), ((), ())), preferred_element_type=F32)


def tn(a, b):
    return lax.dot_general(a, b, (((0,), (0,)), ((), ())), preferred_element_type=F32)


def normalised(x):
    centred = x - jnp.mean(x, axis=1, keepdims=True)
    rstd = lax.rsqrt(jnp.mean(centred * centred, axis=1, keepdims=True) + EPS)
    return centred * rstd, rstd


def gelu_both(h):
    a = jnp.abs(h) * 0.7071067811865476
    t = 1.0 / (1.0 + 0.3275911 * a)
    poly = 1.061405429 * t - 1.453152027
    poly = poly * t + 1.421413741
    poly = poly * t - 0.284496736
    poly = poly * t + 0.254829592
    e = jnp.exp(-0.5 * h * h)
    tail = 0.5 * poly * t * e
    cdf = jnp.where(h >= 0, 1.0 - tail, tail)
    return h * cdf, cdf + h * (e * 0.3989422804014327)


def head_mask(v, head):
    lane = lax.broadcasted_iota(jnp.int32, v.shape, 1)
    return jnp.where((lane >= HEAD_DIM) == (head == 1), v, jnp.zeros_like(v))


def turn(u, c, s1, s2):
    return u * c + pltpu.roll(u, WIDTH - 8, 1) * s1 + pltpu.roll(u, 8, 1) * s2


def turn_back(w, c, s1, s2):
    return w * c + pltpu.roll(w * s2, WIDTH - 8, 1) + pltpu.roll(w * s1, 8, 1)


def allowed(i, seg_col, seg_row):
    keys = (i + 1) * CHUNK
    shape = (CHUNK, keys)
    q_at = lax.broadcasted_iota(jnp.int32, shape, 0) + i * CHUNK
    k_at = lax.broadcasted_iota(jnp.int32, shape, 1)
    same = seg_col[i * CHUNK : keys, :] == seg_row[:, :keys]
    return same & (k_at <= q_at)


def placed_half(first, row):
    none = jnp.zeros_like(row)
    return jnp.where(
        first, jnp.concatenate([row, none], axis=1), jnp.concatenate([none, row], axis=1)
    )


def store_parts(first, rows, value, keep, send):
    low, high = value[:, :HALF].astype(BF16), value[:, HALF:].astype(BF16)

    @pl.when(first)
    def _():
        keep[rows, :] = low
        send[rows, :] = high

    @pl.when(jnp.logical_not(first))
    def _():
        keep[rows, :] = high
        send[rows, :] = low


def forward_rows(x_of, w, sm, bq, be, tabs, normed, mixed, q, k, v, active, slope, stats=None):
    for i in range(ROWS // CHUNK):
        rows = slice(i * CHUNK, (i + 1) * CHUNK)
        xhat, rstd = normalised(x_of(rows))
        if stats:
            stats[0][rows, :], stats[1][rows, :] = xhat, rstd
        normed[rows, :] = (xhat * sm[0:1, :] + sm[2:3, :]).astype(BF16)
        mixed[rows, :] = (xhat * sm[1:2, :] + sm[3:4, :]).astype(BF16)
        joint = nn(normed[rows, :], w[:, :QKV]) + bq[...]
        c, s1, s2 = tabs[0, rows, :], tabs[1, rows, :], tabs[2, rows, :]
        q[rows, :] = turn(joint[:, :WIDTH], c, s1, s2).astype(BF16)
        k[rows, :] = turn(joint[:, WIDTH : 2 * WIDTH], c, s1, s2).astype(BF16)
        v[rows, :] = joint[:, 2 * WIDTH :].astype(BF16)
        hidden = nn(mixed[rows, :], w[:, COL_E:COL_O]) + be[...]
        act, dact = gelu_both(hidden)
        active[rows, :] = act.astype(BF16)
        slope[rows, :] = dact.astype(slope.dtype)


def attend(q, k, v, seg_col, seg_row, att, lse):
    for i in range(ROWS // CHUNK):
        rows = slice(i * CHUNK, (i + 1) * CHUNK)
        keys = slice(0, (i + 1) * CHUNK)
        mask = allowed(i, seg_col[...], seg_row[...])
        out, tops = None, []
        for head in range(2):
            s = nt(head_mask(q[rows, :], head) * 0.125, k[keys, :])
            s = jnp.where(mask, s, -1e30)
            top = jnp.max(s, axis=1, keepdims=True)
            e = jnp.exp(s - top)
            total = jnp.sum(e, axis=1, keepdims=True)
            probs = (e * (1.0 / total)).astype(BF16)
            part = nn(probs, head_mask(v[keys, :], head))
            out = part if out is None else out + part
            tops.append(top + jnp.log(total))
        att[rows, :] = out.astype(BF16)
        lane = lax.broadcasted_iota(jnp.int32, (CHUNK, WIDTH), 1)
        lse[rows, :] = jnp.where(lane < HEAD_DIM, tops[0], tops[1])


def branch_out(first, w, att, active, keep, send):
    for i in range(ROWS // CHUNK):
        rows = slice(i * CHUNK, (i + 1) * CHUNK)
        branch = nt(att[rows, :], w[:, COL_O:COL_S]) + nt(active[rows, :], w[:, COL_S:])
        store_parts(first, rows, branch, keep, send)


def backward_rows(
    first, stats_of, gy_of, w, sm, tabs, seg_col, seg_row, q, k, v, lse, slope,
    gatt, gk, gv, gq, gjoint, ghid, keep, send, sums,
):
    for i in range(ROWS // CHUNK):
        rows = slice(i * CHUNK, (i + 1) * CHUNK)
        gy = gy_of(rows)
        gatt[rows, :] = nn(gy, w[:, COL_O:COL_S]).astype(BF16)
        gact = nn(gy, w[:, COL_S:])
        ghid[rows, :] = (gact * slope[rows, :].astype(F32)).astype(BF16)
    gk[...] = jnp.zeros_like(gk)
    gv[...] = jnp.zeros_like(gv)
    for i in range(ROWS // CHUNK):
        rows = slice(i * CHUNK, (i + 1) * CHUNK)
        keys = slice(0, (i + 1) * CHUNK)
        mask = allowed(i, seg_col[...], seg_row[...])
        out = None
        for head in range(2):
            qh = head_mask(q[rows, :], head) * 0.125
            gh = head_mask(gatt[rows, :], head)
            s = nt(qh, k[keys, :])
            at = head * HEAD_DIM
            probs = jnp.where(mask, jnp.exp(s - lse[rows, at : at + 1]), 0.0)
            gp = nt(gh, v[keys, :])
            dot = jnp.sum(probs * gp, axis=1, keepdims=True)
            gs = (probs * (gp - dot)).astype(BF16)
            part = nn(gs, head_mask(k[keys, :], head) * 0.125)
            out = part if out is None else out + part
            gk[keys, :] += tn(gs, qh)
            gv[keys, :] += tn(probs.astype(BF16), gh)
        gq[rows, :] = out
    total = [None] * 7
    for i in range(ROWS // CHUNK):
        rows = slice(i * CHUNK, (i + 1) * CHUNK)
        c, s1, s2 = tabs[0, rows, :], tabs[1, rows, :], tabs[2, rows, :]
        gjoint[rows, :WIDTH] = turn_back(gq[rows, :], c, s1, s2).astype(BF16)
        gjoint[rows, WIDTH : 2 * WIDTH] = turn_back(gk[rows, :], c, s1, s2).astype(BF16)
        gjoint[rows, 2 * WIDTH :] = gv[rows, :].astype(BF16)
        gj, gh = gjoint[rows, :], ghid[rows, :]
        gn = nt(gj, w[:, :QKV])
        gm = nt(gh, w[:, COL_E:COL_O])
        xhat, rstd = stats_of(rows)
        h = gn * sm[0:1, :] + gm * sm[1:2, :]
        gx = h - jnp.mean(h, axis=1, keepdims=True)
        gx = (gx - xhat * jnp.mean(h * xhat, axis=1, keepdims=True)) * rstd
        store_parts(first, rows, gx, keep, send)
        found = (
            jnp.sum(gn * xhat, axis=0, keepdims=True),
            jnp.sum(gm * xhat, axis=0, keepdims=True),
            jnp.sum(gn, axis=0, keepdims=True),
            jnp.sum(gm, axis=0, keepdims=True),
            jnp.sum(gy_of(rows).astype(F32), axis=0, keepdims=True),
            placed_half(first, jnp.sum(gh.astype(F32), axis=0, keepdims=True)),
            jnp.concatenate(
                [jnp.sum(gj.astype(F32), axis=0, keepdims=True), jnp.zeros((1, MODEL - QKV), F32)],
                axis=1,
            ),
        )
        total = [a if t is None else t + a for t, a in zip(total, found)]
    for n, t in enumerate(total):
        sums[n : n + 1, :] = t
    sums[7:8, :] = jnp.zeros((1, MODEL), F32)


def join(first, out, a0, a1, b0, b1):
    step = HALF // 2

    @pl.when(first)
    def _():
        for n, part in enumerate((a0, a1, b0, b1)):
            out[:, n * step : (n + 1) * step] = part[...]

    @pl.when(jnp.logical_not(first))
    def _():
        for n, part in enumerate((b0, b1, a0, a1)):
            out[:, n * step : (n + 1) * step] = part[...]


def first_forward(
    core, x, w, sm, bq, be, tabs, seg_col, seg_row,
    keep, send, normed, mixed, q, k, v, att, lse, active, slope, zero,
):
    first = core[0] == 0
    zero[...] = jnp.zeros_like(zero)
    forward_rows(
        lambda rows: x[rows, :].astype(F32), w, sm, bq, be, tabs, normed, mixed, q, k, v, active, slope
    )
    attend(q, k, v, seg_col, seg_row, att, lse)
    branch_out(first, w, att, active, keep, send)


def both_ways(
    core, xa0, xa1, xb0, xb1, gy, w, sm, bq, be, tabs, seg_col, seg_row,
    keep_y, send_y, keep_g, send_g, normed, mixed, att, active, gjoint, ghid, sums, zero,
    x, q, k, v, lse, slope, gatt, gk, gv, gq, xhat, rstd,
):
    first = core[0] == 0
    zero[...] = jnp.zeros_like(zero)
    join(first, x, xa0, xa1, xb0, xb1)
    x_of = lambda rows: x[rows, :].astype(F32)
    stats = (xhat, rstd)
    forward_rows(x_of, w, sm, bq, be, tabs, normed, mixed, q, k, v, active, slope, stats)
    attend(q, k, v, seg_col, seg_row, att, lse)
    backward_rows(
        first, lambda rows: (xhat[rows, :], rstd[rows, :]), lambda rows: gy[rows, :], w, sm, tabs,
        seg_col, seg_row, q, k, v, lse, slope, gatt, gk, gv, gq, gjoint, ghid, keep_g, send_g, sums,
    )
    branch_out(first, w, att, active, keep_y, send_y)


def first_backward(
    core, x, ga0, ga1, gb0, gb1, w, sm, tabs, seg_col, seg_row, q, k, v, lse, slope,
    keep_g, send_g, gjoint, ghid, gy, sums, zero,
    gatt, gk, gv, gq,
):
    first = core[0] == 0
    zero[...] = jnp.zeros_like(zero)
    join(first, gy, ga0, ga1, gb0, gb1)
    backward_rows(
        first, lambda rows: normalised(x[rows, :].astype(F32)), lambda rows: gy[rows, :], w, sm, tabs,
        seg_col, seg_row, q, k, v, lse, slope, gatt, gk, gv, gq, gjoint, ghid, keep_g, send_g, sums,
    )


def weight_grads(n0, n1, m0, m1, g0, g1, j0, j1, h0, h1, a0, a1, c0, c1, out):
    out[:, :QKV] = (tn(n0[...], j0[...]) + tn(n1[...], j1[...])).astype(BF16)
    out[:, COL_E:COL_O] = (tn(m0[...], h0[...]) + tn(m1[...], h1[...])).astype(BF16)
    sides = [jnp.concatenate([a[...], c[...]], axis=1) for a, c in ((a0, c0), (a1, c1))]
    out[:, COL_O:COLS] = (tn(g0[...], sides[0]) + tn(g1[...], sides[1])).astype(BF16)


def owner_order(first, row):
    shape = (QKV, HALF)
    at = lax.broadcasted_iota(jnp.int32, shape, 0)
    col = lax.broadcasted_iota(jnp.int32, shape, 1)
    part = (col // 16) % 4
    wanted = jnp.where(part < 3, part * WIDTH + (col // 64) * 16 + col % 16, -1)
    moved = nn(row.astype(BF16), jnp.where(at == wanted, 1.0, 0.0).astype(BF16))
    return placed_half(first, moved)


def row_grads(core, s00, s01, s10, s11, rows):
    for n, (a, b) in enumerate(((s00, s01), (s10, s11))):
        total = a[...] + b[...]
        rows[8 * n : 8 * n + 8, :] = total
        moved = owner_order(core[0] == 0, total[:, :QKV])
        rows[8 * n + 6 : 8 * n + 7, :] = moved[6:7, :]


def sum_tiles(arrived, *refs):
    out, held, sems = refs[-3:]
    parts = held.shape[0]
    step = held.shape[2]
    copies = []
    for i in range(parts):
        rows = pl.ds(i * step, step)
        copies.append(pltpu.make_async_copy(arrived.at[:, rows, :], held.at[i], sems.at[i]))
        copies[i].start()
    for i in range(parts):
        copies[i].wait()
        total = held[i, 0].astype(F32)
        for n in range(1, held.shape[1]):
            total = total + held[i, n].astype(F32)
        out[i * step : (i + 1) * step, :] = total


def sum_tiles_call(arrived, after=()):
    peers, rows, cols = arrived.shape
    parts = 4
    return pl.pallas_call(
        sum_tiles,
        in_specs=[pl.BlockSpec(memory_space=pltpu.HBM)]
        + [pl.BlockSpec(memory_space=pl.ANY)] * len(after),
        out_specs=pl.BlockSpec(memory_space=pltpu.VMEM),
        out_shape=shaped(rows, cols, dtype=F32),
        scratch_shapes=[
            pltpu.VMEM((parts, peers, rows // parts, cols), BF16),
            pltpu.SemaphoreType.DMA((parts,)),
        ],
        compiler_params=pltpu.CompilerParams(vmem_limit_bytes=60 * 2**20),
        name="sum_tiles",
    )(arrived, *after)


def write_out(core, sum0, got0, sum1, got1, joint, expand, output, shrink, hid, bias):
    def write(low, high, at):
        for t in range(3):
            joint[t, :, :WIDTH] = low[:, t * WIDTH : (t + 1) * WIDTH]
            joint[t, :, WIDTH:] = high[:, t * WIDTH : (t + 1) * WIDTH]
        for out, start, end in ((expand, COL_E, COL_O), (output, COL_O, COL_S), (shrink, COL_S, COLS)):
            out[:, : end - start] = low[:, start:end]
            out[:, end - start :] = high[:, start:end]
        rows = (sum0[:, COLS:] + got0[:, COLS:]).T
        hid[...] = rows[at + 5 : at + 6, :]
        for t in range(3):
            bias[t : t + 1, :] = rows[at + 6 : at + 7, 16 * t : 16 * t + 16]

    @pl.when(core[0] == 0)
    def _():
        write(sum0, got0, 0)

    @pl.when(core[0] != 0)
    def _():
        write(got1, sum1, 8)


def write_boundary(core, gx, y, other, out):
    @pl.when(core[0] == 0)
    def _():
        out[:, :, :HALF] = gx[...]
        out[:, :, HALF:] = other[...]

    @pl.when(core[0] != 0)
    def _():
        out[:, :, :HALF] = other[...]
        out[:, :, HALF:] = y[...]


def shaped(*dims, dtype=BF16):
    return jax.ShapeDtypeStruct(dims, dtype)


def call(kernel, n_in, outs, scratch, flops, name, after=()):
    whole = pl.BlockSpec(memory_space=pltpu.VMEM)

    def body(*refs):
        kernel(*refs[:n_in], *refs[n_in + len(after) :])

    made = pl.pallas_call(
        body,
        in_specs=[pl.BlockSpec(memory_space=pltpu.SMEM)]
        + [whole] * (n_in - 1)
        + [pl.BlockSpec(memory_space=pl.ANY)] * len(after),
        out_specs=[whole] * len(outs),
        out_shape=outs,
        scratch_shapes=scratch,
        compiler_params=pltpu.CompilerParams(vmem_limit_bytes=60 * 2**20),
        cost_estimate=pl.CostEstimate(flops=flops, bytes_accessed=8 * 2**20, transcendentals=2**20),
        name=name,
    )
    return lambda *args: made(*args, *after)


ZERO = shaped(1, HALF // 2, dtype=F32)


def tall(width, dtype=BF16):
    return shaped(ROWS, width, dtype=dtype)


def forward_call(*args, after=()):
    outs = [tall(HALF), tall(HALF), tall(MODEL), tall(MODEL)]
    outs += [tall(WIDTH)] * 4 + [tall(WIDTH, F32), tall(INNER), tall(INNER), ZERO]
    return call(first_forward, len(args), outs, [], 2**31, "layer_forward", after)(*args)


def both_call(*args, after=()):
    outs = [tall(HALF)] * 4 + [tall(MODEL)] * 2 + [tall(WIDTH), tall(INNER), tall(QKV), tall(INNER)]
    outs += [shaped(8, MODEL, dtype=F32), ZERO]
    scratch = [pltpu.VMEM((ROWS, MODEL), BF16)] + [pltpu.VMEM((ROWS, WIDTH), BF16)] * 3
    scratch += [pltpu.VMEM((ROWS, WIDTH), F32), pltpu.VMEM((ROWS, INNER), F32)]
    scratch += [pltpu.VMEM((ROWS, WIDTH), BF16)] + [pltpu.VMEM((ROWS, WIDTH), F32)] * 3
    scratch += [pltpu.VMEM((ROWS, MODEL), F32), pltpu.VMEM((ROWS, 1), F32)]
    return call(both_ways, len(args), outs, scratch, 2**32, "layer_both", after)(*args)


def backward_call(*args, after=()):
    outs = [tall(HALF)] * 2 + [tall(QKV), tall(INNER), tall(MODEL), shaped(8, MODEL, dtype=F32), ZERO]
    scratch = [pltpu.VMEM((ROWS, WIDTH), BF16)] + [pltpu.VMEM((ROWS, WIDTH), F32)] * 3
    return call(first_backward, len(args), outs, scratch, 2**31, "layer_backward", after)(*args)


def grads_call(*args, sums=(), after=()):
    blocks = 4
    step = MODEL // blocks
    extra = 128 if sums else 0
    cut = pl.BlockSpec((ROWS, step), lambda i: (0, i))
    rest = [pl.BlockSpec(a.shape, lambda i: (0, 0)) for a in (*args[6:], *sums[1:])]
    n_in = len(args)
    n_all = n_in + len(sums) + len(after)

    def body(*refs):
        first = len(sums[:1])
        out, token, *rows = refs[n_all:]
        weight_grads(*refs[first : first + n_in], out)
        token[...] = jnp.zeros_like(token)
        if sums:
            rows = rows[0]

            @pl.when(pl.program_id(0) == 0)
            def _():
                rows[...] = jnp.zeros_like(rows)
                row_grads(refs[0], *refs[1 + n_in : 5 + n_in], rows)

            at = pl.multiple_of(pl.program_id(0) * step, step)
            out[:, COLS:] = rows[:, pl.ds(at, step)].T.astype(BF16)

    return pl.pallas_call(
        body,
        grid=(blocks,),
        in_specs=[pl.BlockSpec(memory_space=pltpu.SMEM)] * len(sums[:1])
        + [cut] * 6
        + rest
        + [pl.BlockSpec(memory_space=pl.ANY)] * len(after),
        out_specs=[
            pl.BlockSpec((step, COLS + extra), lambda i: (i, 0)),
            pl.BlockSpec(ZERO.shape, lambda i: (0, 0)),
        ],
        out_shape=[pltpu.HBM((MODEL, COLS + extra), BF16), ZERO],
        scratch_shapes=[pltpu.VMEM((128, MODEL), F32)] if sums else [],
        compiler_params=pltpu.CompilerParams(vmem_limit_bytes=60 * 2**20),
        cost_estimate=pl.CostEstimate(flops=2**32, bytes_accessed=2**23, transcendentals=0),
        name="weight_grads",
    )(*sums[:1], *args, *sums[1:], *after)


def gate(x, *after):
    anywhere = pl.BlockSpec(memory_space=pl.ANY)
    return pl.pallas_call(
        lambda *refs: None,
        in_specs=[anywhere] * (1 + len(after)),
        out_specs=anywhere,
        out_shape=shaped(*x.shape, dtype=x.dtype),
        input_output_aliases={0: 0},
        name="gate",
    )(x, *after)


def assemble(place, own, before, behind, far0, far1, out0, out1, *parts):
    step = own.shape[1]
    ring = ROWS // step

    def put(out, value, distance):
        at = lax.rem(place[0] + distance, ring) * step
        out[pl.ds(pl.multiple_of(at, step), step), :] = value

    for n, (out, far) in enumerate(((out0, far0), (out1, far1))):
        put(out, own[n], 0)
        put(out, before[n], ring - 1)
        put(out, behind[n], 1)
        put(out, far[...], 2)

    quarter = HALF // 2
    for core in range(2):

        @pl.when(place[1] == core)
        def _():
            for n, part in enumerate(parts):
                at = core * HALF + (n % 2) * quarter
                part[...] = (out0 if n < 2 else out1)[:, at : at + quarter]


def around_ring(x, by):
    ring = lax.axis_size("tensor")
    return lax.ppermute(x, "tensor", [(i, (i + by) % ring) for i in range(ring)])


def gathered_rows(x, place):
    before, behind = around_ring(x, 1), around_ring(x, -1)
    far0, far1 = around_ring(before[0], 1), around_ring(behind[1], -1)
    outs = [tall(MODEL)] * 2 + [tall(HALF // 2)] * 4
    args = (place, x, before, behind, far0, far1)
    out0, out1, *parts = call(assemble, 6, outs, [], 2**20, "assemble")(*args)
    return [out0, out1], [parts[:2], parts[2:]]


def add_blocks(offset, place, k0, g0, k1, g1, keep, send):
    step = keep.shape[2]
    ring = ROWS // step
    first = jnp.where(place[0] % 2 == offset, 1, ring - 1)
    for out, which in ((keep, (0, ring - first)), (send, (first, 2))):
        for n, distance in enumerate(which):
            at = lax.rem(place[0] + distance, ring) * step
            rows = pl.ds(pl.multiple_of(at, step), step)
            out[n, 0] = (k0[rows, :].astype(F32) + g0[rows, :].astype(F32)).astype(BF16)
            out[n, 1] = (k1[rows, :].astype(F32) + g1[rows, :].astype(F32)).astype(BF16)


def add_blocks_call(offset, place, keeps, gots):
    outs = [shaped(2, 2, ROWS // lax.axis_size("tensor"), HALF)] * 2
    args = (place, keeps[0], gots[0], keeps[1], gots[1])
    return call(functools.partial(add_blocks, offset), 5, outs, [], 2**20, "add_blocks")(*args)


def swap(x):
    return lax.ppermute(x, "pipe", [(0, 1), (1, 0)])


def along_ring(x, axis, offset, stride=1, side=4):
    pairs = []
    for g in range(lax.axis_size(axis)):
        at = (g // stride) % side
        to = (at + 1) % side if at % 2 == offset else (at - 1) % side
        pairs.append((g, g + (to - at) * stride))
    return lax.ppermute(x, axis, pairs)


def added(a, b, row=None):
    total = a.astype(F32) + b.astype(F32)
    return (total if row is None else total + row).astype(BF16)


def halves(a):
    return [a[:, : HALF // 2], a[:, HALF // 2 :]]


class SumOverTensor:
    def __init__(self, keep, send):
        self.chip = halves(added(keep, swap(send)))

    def second(self, zero=None):
        self.pair = [added(a, along_ring(a, "tensor", n), zero) for n, a in enumerate(self.chip)]

    def finish(self, base, rows, zero=None):
        mine = []
        for n, (a, b) in enumerate(zip(self.pair, base)):
            total = a.astype(F32) + along_ring(a, "tensor", 1 - n).astype(F32) + b.astype(F32)
            for row in (rows and rows[n], zero):
                total = total if row is None else total + row
            mine.append(total.astype(BF16))
        return (*mine, *[swap(a) for a in mine])


def summed_blocks(keeps, sends, place, offset, after):
    gots = [swap(gate(s, after)) for s in sends]
    keep, send = add_blocks_call(offset, place, keeps, gots)
    half = added(keep, along_ring(send, "tensor", offset))
    return half[0].astype(F32) + along_ring(half[1], "tensor", 1 - offset).astype(F32)


def rotary_tables(segment_row):
    places = jnp.arange(ROWS, dtype=jnp.int32)
    before = jnp.sum((segment_row[None, :] < segment_row[:, None]).astype(jnp.int32), axis=1)
    positions = (places - before).astype(F32)
    half_rot = ROTARY // 2
    lane = jnp.arange(WIDTH, dtype=jnp.int32)[None, :] % HEAD_DIM
    inverse = 10000.0 ** (-(lane % half_rot).astype(F32) * 2.0 / ROTARY)
    angles = positions[:, None] * inverse
    cosine, sine = jnp.cos(angles), jnp.sin(angles)
    c = jnp.where(lane < ROTARY, cosine, 1.0)
    s1 = jnp.where(lane < half_rot, -sine, 0.0)
    s2 = jnp.where((lane >= half_rot) & (lane < ROTARY), sine, 0.0)
    return jnp.stack([c, s1, s2])


def shards(
    inputs, upstream, segments, joint_weight, joint_bias, output_weight, expand_weight,
    expand_bias, shrink_weight, norm_gains, shift_rows,
):
    dp = lax.axis_size("dp")
    tensor = lax.axis_size("tensor")
    core = lax.axis_index("pipe")
    first = core == 0
    core_arg = core.astype(jnp.int32).reshape(1)
    micros = inputs.shape[0]
    own_d = MODEL // dp

    def pick(a, b):
        return jnp.where(first, a, b)

    def packed(h):
        return jnp.concatenate(
            [
                joint_weight[0][:, :, h * WIDTH : (h + 1) * WIDTH].reshape(own_d, QKV),
                expand_weight[0][:, h * INNER : (h + 1) * INNER],
                output_weight[0][h * WIDTH : (h + 1) * WIDTH].T,
                shrink_weight[0][h * INNER : (h + 1) * INNER].T,
            ],
            axis=1,
        )

    with jax.named_scope("weights"):
        pack_a, pack_b = packed(0), packed(1)
        stay = pick(pack_a, pack_b)
        came = swap(pick(pack_b, pack_a))
        w0 = lax.all_gather(pick(stay, came), "dp", axis=0, tiled=True)
        w1 = lax.all_gather(pick(came, stay), "dp", axis=0, tiled=True)

    with jax.named_scope("small_parameters"):
        bias_row = jnp.pad(joint_bias[0, :, 0, :].reshape(1, -1), ((0, 0), (0, own_d - 3 * 16)))
        small = jnp.concatenate([norm_gains[0], shift_rows[0], expand_bias[0], bias_row], axis=0)
        copies = jnp.broadcast_to(small, (2 * dp, *small.shape))
        small = lax.all_to_all(copies, ("pipe", "dp"), split_axis=0, concat_axis=0, tiled=True)
        small = small.reshape(2, dp, 8, own_d).astype(F32)
        rows = small.transpose(0, 2, 1, 3).reshape(2, 8, MODEL)
        be = [pick(rows[n, 6:7, :INNER], rows[n, 6:7, INNER:]) for n in range(2)]
        bq_all = small[:, :, 7, :48].reshape(2, dp, 3, 16).transpose(0, 2, 1, 3).reshape(2, 3, 256)
        bq = [
            pick(bq_all[n, :, :WIDTH], bq_all[n, :, WIDTH:]).reshape(1, QKV) for n in range(2)
        ]
        shift_own = [pick(rows[n, :, :HALF], rows[n, :, HALF:]) for n in range(2)]

    place = lax.axis_index("tensor").astype(jnp.int32).reshape(1)
    with jax.named_scope("activations_in"):
        both_places = jnp.concatenate([place, core_arg])
        x0, x0_half = gathered_rows(inputs, both_places)
        gy1, gy1_half = gathered_rows(upstream, both_places)

    with jax.named_scope("tables"):
        tabs = [rotary_tables(segments[m]) for m in range(micros)]
        seg_col = [segments[m].reshape(ROWS, 1) for m in range(micros)]
        seg_row = [segments[m].reshape(1, ROWS) for m in range(micros)]

    kept, sums0 = [], []
    after = (*tabs, *gy1)
    for m in range(micros):
        with jax.named_scope("first_layer"):
            keep, send, *saved, zero = forward_call(
                core_arg, x0[m], w0, rows[0], bq[0], be[0], tabs[m], seg_col[m], seg_row[m], after=after
            )
            if m:
                sums0[0].second(zero)
                send = gate(send, *sums0[0].pair)
            sums0.append(SumOverTensor(keep, send))
            after = tuple(sums0[m].chip)
            kept.append(saved)
    sums0[1].second()

    x1, made1, y_parts, sums1 = [], [], [], []
    shift = halves(shift_own[0][4:5] + shift_own[0][5:6])
    for m in range(micros):
        with jax.named_scope("second_layer"):
            if m == 0:
                x1.append(sums0[0].finish(x0_half[0], shift))
                after = tuple(sums0[1].pair)
            else:
                after = tuple(sums1[0].chip)
            keep_y, send_y, keep_g, send_g, *made, zero = both_call(
                core_arg, *x1[m], gy1[m], w1, rows[1], bq[1], be[1], tabs[m], seg_col[m], seg_row[m],
                after=after,
            )
            if m == 0:
                x1.append(sums0[1].finish(x0_half[1], shift, zero))
            else:
                sums1[0].second(zero)
                send_g = gate(send_g, *sums1[0].pair)
            sums1.append(SumOverTensor(keep_g, send_g))
            y_parts.append((keep_y, send_y))
            made1.append(made)

    def pairs(made, n):
        return [made[m][n] for m in range(micros)]

    with jax.named_scope("second_layer_grads"):
        args = []
        for n in (0, 1, None, 4, 5, 2, 3):
            args += gy1 if n is None else pairs(made1, n)
        grads1, zero = grads_call(*args, after=(*sums1[1].chip, *sums1[0].pair))
        g0 = [sums1[0].finish(gy1_half[0], None, zero)]
        sums1[1].second(zero)
        tiles1 = gate(grads1.reshape(dp, own_d, -1), *g0[0][:2])
        arrived1 = lax.all_to_all(tiles1, "dp", split_axis=0, concat_axis=0, tiled=True)

    made0, g_parts = [], []
    after = tuple(sums1[1].pair)
    for m in range(micros):
        with jax.named_scope("first_layer_back"):
            if m:
                g0.append(sums1[m].finish(gy1_half[m], None, zero))
            normed, mixed, q, k, v, att, lse, active, slope = kept[m]
            keep_g, send_g, gjoint, ghid, gy, sums, zero = backward_call(
                core_arg, x0[m], *g0[m], w0, rows[0], tabs[m], seg_col[m], seg_row[m],
                q, k, v, lse, slope, after=after,
            )
            after = (sums,)
            g_parts.append((keep_g, send_g))
            made0.append((normed, mixed, att, active, gjoint, ghid, sums, gy))

    with jax.named_scope("first_layer_grads"):
        args = []
        for n in (0, 1, 7, 4, 5, 2, 3):
            args += pairs(made0, n)
        sums = (core_arg, made0[0][6], made0[1][6], made1[0][6], made1[1][6])
        grads0, _ = grads_call(*args, sums=sums)
        tiles0 = gate(grads0.reshape(dp, own_d, -1), arrived1)
        arrived0 = lax.all_to_all(tiles0, "dp", split_axis=0, concat_axis=0, tiled=True)

    with jax.named_scope("boundary"):

        def own_rows(parts):
            step = ROWS // tensor
            return jnp.stack(
                [
                    lax.dynamic_slice_in_dim(jnp.concatenate(a[:2], axis=1), place[0] * step, step, 0)
                    for a in parts
                ]
            ).astype(F32)

        gx_all = summed_blocks(*zip(*g_parts), place, 0, tiles0) + own_rows(g0)
        y_all = summed_blocks(*zip(*y_parts), place, 1, tiles0) + own_rows(x1)
        y_all = y_all + (shift_own[1][4:5] + shift_own[1][5:6])
        other = swap(pick(y_all, gx_all))
        outs = [shaped(2, ROWS // tensor, MODEL, dtype=F32)]
        args = (core_arg, gx_all, y_all, other)
        boundary = call(write_boundary, 4, outs, [], 2**20, "write_boundary")(*args)[0][None]

    with jax.named_scope("outputs"):
        sum1 = gate(arrived1, tiles0).astype(F32).sum(axis=0)
        got1 = lax.ppermute(sum1, "pipe", [(0, 1)])
        sum0 = sum_tiles_call(arrived0, (boundary, got1))
        got0 = swap(sum0)
        both = sum0[:, COLS:] + got0[:, COLS:]
        total = pick(both[:, :4], both[:, 8:12]).T
        for offset in (0, 1):
            total = total + along_ring(total, "tensor", offset)
        gy_sum = pick(sum0[:, COLS + 4], sum0[:, COLS + 12])
        outs = [(3, own_d, 2 * WIDTH), (own_d, 2 * INNER), (own_d, 2 * WIDTH), (own_d, 2 * INNER)]
        outs += [(1, own_d), (3, 16)]
        outs = [shaped(*dims, dtype=F32) for dims in outs]
        args = (core_arg, sum0, got0, sum1, got1)
        made = call(write_out, 5, outs, [], 2**20, "write_out")(*args)
        gains = total[None, 0:2]
        shift = jnp.stack([total[2], total[3], gy_sum, gy_sum])[None]
        joint = made[0].transpose(1, 0, 2)[None]
        expand = made[1][None]
        output, shrink = made[2].T[None], made[3].T[None]
        expand_bias_grad = made[4].reshape(1, 1, own_d)
        joint_bias_grad = made[5].reshape(1, 3, 1, 16)

    return (
        boundary,
        joint,
        joint_bias_grad,
        output,
        expand,
        expand_bias_grad,
        shrink,
        gains,
        shift,
    )


def solution(mesh):
    placed = (
        P(None, ("dp", "tensor"), None),
        P(None, ("dp", "tensor"), None),
        P(None, "dp"),
        P("pipe", "dp", None, "tensor"),
        P("pipe", None, "tensor", "dp"),
        P("pipe", "tensor", "dp"),
        P("pipe", "dp", "tensor"),
        P("pipe", "tensor", "dp"),
        P("pipe", "tensor", "dp"),
        P("pipe", None, "dp"),
        P("pipe", None, "dp"),
    )
    return jax.shard_map(
        shards,
        mesh=mesh,
        in_specs=placed,
        out_specs=(
            P("pipe", None, ("dp", "tensor"), None),
            P("pipe", "dp", None, "tensor"),
            P("pipe", None, "tensor", "dp"),
            P("pipe", "tensor", "dp"),
            P("pipe", "dp", "tensor"),
            P("pipe", "tensor", "dp"),
            P("pipe", "tensor", "dp"),
            P("pipe", None, "dp"),
            P("pipe", None, "dp"),
        ),
        check_vma=False,
    )
```

```python
import functools

import jax
import jax.numpy as jnp
from jax import lax
from jax.experimental import pallas as pl
from jax.experimental.pallas import tpu as pltpu
from jax.sharding import PartitionSpec as P

HEAD_DIM = 64
ROTARY = 16
EPS = 1e-05

MODEL = 1024
ROWS = 512
CHUNK = 256
WIDTH = 128
INNER = 512
HALF = MODEL // 2

QKV = 3 * WIDTH
COL_E = QKV
COL_O = QKV + INNER
COL_S = COL_O + WIDTH
COLS = COL_S + INNER

F32 = jnp.float32
BF16 = jnp.bfloat16


def nn(a, b):
    return lax.dot_general(a, b, (((1,), (0,)), ((), ())), preferred_element_type=F32)


def nt(a, b):
    return lax.dot_general(a, b, (((1,), (1,)), ((), ())), preferred_element_type=F32)


def tn(a, b):
    return lax.dot_general(a, b, (((0,), (0,)), ((), ())), preferred_element_type=F32)


def normalised(x):
    centred = x - jnp.mean(x, axis=1, keepdims=True)
    rstd = lax.rsqrt(jnp.mean(centred * centred, axis=1, keepdims=True) + EPS)
    return centred * rstd, rstd


def gelu_both(h):
    a = jnp.abs(h) * 0.7071067811865476
    t = 1.0 / (1.0 + 0.3275911 * a)
    poly = 1.061405429 * t - 1.453152027
    poly = poly * t + 1.421413741
    poly = poly * t - 0.284496736
    poly = poly * t + 0.254829592
    e = jnp.exp(-0.5 * h * h)
    tail = 0.5 * poly * t * e
    cdf = jnp.where(h >= 0, 1.0 - tail, tail)
    return h * cdf, cdf + h * (e * 0.3989422804014327)


def head_mask(v, head):
    lane = lax.broadcasted_iota(jnp.int32, v.shape, 1)
    return jnp.where((lane >= HEAD_DIM) == (head == 1), v, jnp.zeros_like(v))


def turn(u, c, s1, s2):
    return u * c + pltpu.roll(u, WIDTH - 8, 1) * s1 + pltpu.roll(u, 8, 1) * s2


def turn_back(w, c, s1, s2):
    return w * c + pltpu.roll(w * s2, WIDTH - 8, 1) + pltpu.roll(w * s1, 8, 1)


def allowed(i, seg_col, seg_row):
    keys = (i + 1) * CHUNK
    shape = (CHUNK, keys)
    q_at = lax.broadcasted_iota(jnp.int32, shape, 0) + i * CHUNK
    k_at = lax.broadcasted_iota(jnp.int32, shape, 1)
    same = seg_col[i * CHUNK : keys, :] == seg_row[:, :keys]
    return same & (k_at <= q_at)


def placed_half(first, row):
    none = jnp.zeros_like(row)
    return jnp.where(
        first, jnp.concatenate([row, none], axis=1), jnp.concatenate([none, row], axis=1)
    )


def store_parts(first, rows, value, keep, send):
    low, high = value[:, :HALF].astype(BF16), value[:, HALF:].astype(BF16)

    @pl.when(first)
    def _():
        keep[rows, :] = low
        send[rows, :] = high

    @pl.when(jnp.logical_not(first))
    def _():
        keep[rows, :] = high
        send[rows, :] = low


def forward_rows(x_of, w, sm, bq, be, tabs, normed, mixed, q, k, v, active, slope, stats=None):
    for i in range(ROWS // CHUNK):
        rows = slice(i * CHUNK, (i + 1) * CHUNK)
        xhat, rstd = normalised(x_of(rows))
        if stats:
            stats[0][rows, :], stats[1][rows, :] = xhat, rstd
        normed[rows, :] = (xhat * sm[0:1, :] + sm[2:3, :]).astype(BF16)
        mixed[rows, :] = (xhat * sm[1:2, :] + sm[3:4, :]).astype(BF16)
        joint = nn(normed[rows, :], w[:, :QKV]) + bq[...]
        c, s1, s2 = tabs[0, rows, :], tabs[1, rows, :], tabs[2, rows, :]
        q[rows, :] = turn(joint[:, :WIDTH], c, s1, s2).astype(BF16)
        k[rows, :] = turn(joint[:, WIDTH : 2 * WIDTH], c, s1, s2).astype(BF16)
        v[rows, :] = joint[:, 2 * WIDTH :].astype(BF16)
        hidden = nn(mixed[rows, :], w[:, COL_E:COL_O]) + be[...]
        act, dact = gelu_both(hidden)
        active[rows, :] = act.astype(BF16)
        slope[rows, :] = dact.astype(slope.dtype)


def attend(q, k, v, seg_col, seg_row, att, lse):
    for i in range(ROWS // CHUNK):
        rows = slice(i * CHUNK, (i + 1) * CHUNK)
        keys = slice(0, (i + 1) * CHUNK)
        mask = allowed(i, seg_col[...], seg_row[...])
        out, tops = None, []
        for head in range(2):
            s = nt(head_mask(q[rows, :], head) * 0.125, k[keys, :])
            s = jnp.where(mask, s, -1e30)
            top = jnp.max(s, axis=1, keepdims=True)
            e = jnp.exp(s - top)
            total = jnp.sum(e, axis=1, keepdims=True)
            probs = (e * (1.0 / total)).astype(BF16)
            part = nn(probs, head_mask(v[keys, :], head))
            out = part if out is None else out + part
            tops.append(top + jnp.log(total))
        att[rows, :] = out.astype(BF16)
        lane = lax.broadcasted_iota(jnp.int32, (CHUNK, WIDTH), 1)
        lse[rows, :] = jnp.where(lane < HEAD_DIM, tops[0], tops[1])


def branch_out(first, w, att, active, keep, send):
    for i in range(ROWS // CHUNK):
        rows = slice(i * CHUNK, (i + 1) * CHUNK)
        branch = nt(att[rows, :], w[:, COL_O:COL_S]) + nt(active[rows, :], w[:, COL_S:])
        store_parts(first, rows, branch, keep, send)


def backward_rows(
    first, stats_of, gy_of, w, sm, tabs, seg_col, seg_row, q, k, v, lse, slope,
    gatt, gk, gv, gq, gjoint, ghid, keep, send, sums,
):
    for i in range(ROWS // CHUNK):
        rows = slice(i * CHUNK, (i + 1) * CHUNK)
        gy = gy_of(rows)
        gatt[rows, :] = nn(gy, w[:, COL_O:COL_S]).astype(BF16)
        gact = nn(gy, w[:, COL_S:])
        ghid[rows, :] = (gact * slope[rows, :].astype(F32)).astype(BF16)
    gk[...] = jnp.zeros_like(gk)
    gv[...] = jnp.zeros_like(gv)
    for i in range(ROWS // CHUNK):
        rows = slice(i * CHUNK, (i + 1) * CHUNK)
        keys = slice(0, (i + 1) * CHUNK)
        mask = allowed(i, seg_col[...], seg_row[...])
        out = None
        for head in range(2):
            qh = head_mask(q[rows, :], head) * 0.125
            gh = head_mask(gatt[rows, :], head)
            s = nt(qh, k[keys, :])
            at = head * HEAD_DIM
            probs = jnp.where(mask, jnp.exp(s - lse[rows, at : at + 1]), 0.0)
            gp = nt(gh, v[keys, :])
            dot = jnp.sum(probs * gp, axis=1, keepdims=True)
            gs = (probs * (gp - dot)).astype(BF16)
            part = nn(gs, head_mask(k[keys, :], head) * 0.125)
            out = part if out is None else out + part
            gk[keys, :] += tn(gs, qh)
            gv[keys, :] += tn(probs.astype(BF16), gh)
        gq[rows, :] = out
    total = [None] * 7
    for i in range(ROWS // CHUNK):
        rows = slice(i * CHUNK, (i + 1) * CHUNK)
        c, s1, s2 = tabs[0, rows, :], tabs[1, rows, :], tabs[2, rows, :]
        gjoint[rows, :WIDTH] = turn_back(gq[rows, :], c, s1, s2).astype(BF16)
        gjoint[rows, WIDTH : 2 * WIDTH] = turn_back(gk[rows, :], c, s1, s2).astype(BF16)
        gjoint[rows, 2 * WIDTH :] = gv[rows, :].astype(BF16)
        gj, gh = gjoint[rows, :], ghid[rows, :]
        gn = nt(gj, w[:, :QKV])
        gm = nt(gh, w[:, COL_E:COL_O])
        xhat, rstd = stats_of(rows)
        h = gn * sm[0:1, :] + gm * sm[1:2, :]
        gx = h - jnp.mean(h, axis=1, keepdims=True)
        gx = (gx - xhat * jnp.mean(h * xhat, axis=1, keepdims=True)) * rstd
        store_parts(first, rows, gx, keep, send)
        found = (
            jnp.sum(gn * xhat, axis=0, keepdims=True),
            jnp.sum(gm * xhat, axis=0, keepdims=True),
            jnp.sum(gn, axis=0, keepdims=True),
            jnp.sum(gm, axis=0, keepdims=True),
            jnp.sum(gy_of(rows).astype(F32), axis=0, keepdims=True),
            placed_half(first, jnp.sum(gh.astype(F32), axis=0, keepdims=True)),
            jnp.concatenate(
                [jnp.sum(gj.astype(F32), axis=0, keepdims=True), jnp.zeros((1, MODEL - QKV), F32)],
                axis=1,
            ),
        )
        total = [a if t is None else t + a for t, a in zip(total, found)]
    for n, t in enumerate(total):
        sums[n : n + 1, :] = t
    sums[7:8, :] = jnp.zeros((1, MODEL), F32)


def join(first, out, a0, a1, b0, b1):
    step = HALF // 2

    @pl.when(first)
    def _():
        for n, part in enumerate((a0, a1, b0, b1)):
            out[:, n * step : (n + 1) * step] = part[...]

    @pl.when(jnp.logical_not(first))
    def _():
        for n, part in enumerate((b0, b1, a0, a1)):
            out[:, n * step : (n + 1) * step] = part[...]


def first_forward(
    core, x, w, sm, bq, be, tabs, seg_col, seg_row,
    keep, send, normed, mixed, q, k, v, att, lse, active, slope, zero,
):
    first = core[0] == 0
    zero[...] = jnp.zeros_like(zero)
    forward_rows(
        lambda rows: x[rows, :].astype(F32), w, sm, bq, be, tabs, normed, mixed, q, k, v, active, slope
    )
    attend(q, k, v, seg_col, seg_row, att, lse)
    branch_out(first, w, att, active, keep, send)


def both_ways(
    core, xa0, xa1, xb0, xb1, gy, w, sm, bq, be, tabs, seg_col, seg_row,
    keep_y, send_y, keep_g, send_g, normed, mixed, att, active, gjoint, ghid, sums, zero,
    x, q, k, v, lse, slope, gatt, gk, gv, gq, xhat, rstd,
):
    first = core[0] == 0
    zero[...] = jnp.zeros_like(zero)
    join(first, x, xa0, xa1, xb0, xb1)
    x_of = lambda rows: x[rows, :].astype(F32)
    stats = (xhat, rstd)
    forward_rows(x_of, w, sm, bq, be, tabs, normed, mixed, q, k, v, active, slope, stats)
    attend(q, k, v, seg_col, seg_row, att, lse)
    backward_rows(
        first, lambda rows: (xhat[rows, :], rstd[rows, :]), lambda rows: gy[rows, :], w, sm, tabs,
        seg_col, seg_row, q, k, v, lse, slope, gatt, gk, gv, gq, gjoint, ghid, keep_g, send_g, sums,
    )
    branch_out(first, w, att, active, keep_y, send_y)


def first_backward(
    core, x, ga0, ga1, gb0, gb1, w, sm, tabs, seg_col, seg_row, q, k, v, lse, slope,
    keep_g, send_g, gjoint, ghid, gy, sums, zero,
    gatt, gk, gv, gq,
):
    first = core[0] == 0
    zero[...] = jnp.zeros_like(zero)
    join(first, gy, ga0, ga1, gb0, gb1)
    backward_rows(
        first, lambda rows: normalised(x[rows, :].astype(F32)), lambda rows: gy[rows, :], w, sm, tabs,
        seg_col, seg_row, q, k, v, lse, slope, gatt, gk, gv, gq, gjoint, ghid, keep_g, send_g, sums,
    )


def weight_grads(n0, n1, m0, m1, g0, g1, j0, j1, h0, h1, a0, a1, c0, c1, out):
    out[:, :QKV] = (tn(n0[...], j0[...]) + tn(n1[...], j1[...])).astype(BF16)
    out[:, COL_E:COL_O] = (tn(m0[...], h0[...]) + tn(m1[...], h1[...])).astype(BF16)
    sides = [jnp.concatenate([a[...], c[...]], axis=1) for a, c in ((a0, c0), (a1, c1))]
    out[:, COL_O:COLS] = (tn(g0[...], sides[0]) + tn(g1[...], sides[1])).astype(BF16)


def owner_order(first, row):
    shape = (QKV, HALF)
    at = lax.broadcasted_iota(jnp.int32, shape, 0)
    col = lax.broadcasted_iota(jnp.int32, shape, 1)
    part = (col // 16) % 4
    wanted = jnp.where(part < 3, part * WIDTH + (col // 64) * 16 + col % 16, -1)
    moved = nn(row.astype(BF16), jnp.where(at == wanted, 1.0, 0.0).astype(BF16))
    return placed_half(first, moved)


def row_grads(core, s00, s01, s10, s11, rows):
    for n, (a, b) in enumerate(((s00, s01), (s10, s11))):
        total = a[...] + b[...]
        rows[8 * n : 8 * n + 8, :] = total
        moved = owner_order(core[0] == 0, total[:, :QKV])
        rows[8 * n + 6 : 8 * n + 7, :] = moved[6:7, :]


def sum_tiles(arrived, *refs):
    out, held, sems = refs[-3:]
    parts = held.shape[0]
    step = held.shape[2]
    copies = []
    for i in range(parts):
        rows = pl.ds(i * step, step)
        copies.append(pltpu.make_async_copy(arrived.at[:, rows, :], held.at[i], sems.at[i]))
        copies[i].start()
    for i in range(parts):
        copies[i].wait()
        total = held[i, 0].astype(F32)
        for n in range(1, held.shape[1]):
            total = total + held[i, n].astype(F32)
        out[i * step : (i + 1) * step, :] = total


def sum_tiles_call(arrived, after=()):
    peers, rows, cols = arrived.shape
    parts = 4
    return pl.pallas_call(
        sum_tiles,
        in_specs=[pl.BlockSpec(memory_space=pltpu.HBM)]
        + [pl.BlockSpec(memory_space=pl.ANY)] * len(after),
        out_specs=pl.BlockSpec(memory_space=pltpu.VMEM),
        out_shape=shaped(rows, cols, dtype=F32),
        scratch_shapes=[
            pltpu.VMEM((parts, peers, rows // parts, cols), BF16),
            pltpu.SemaphoreType.DMA((parts,)),
        ],
        compiler_params=pltpu.CompilerParams(vmem_limit_bytes=60 * 2**20),
        name="sum_tiles",
    )(arrived, *after)


def write_out(core, sum0, got0, sum1, got1, joint, expand, output, shrink, hid, bias):
    def write(low, high, at):
        for t in range(3):
            joint[t, :, :WIDTH] = low[:, t * WIDTH : (t + 1) * WIDTH]
            joint[t, :, WIDTH:] = high[:, t * WIDTH : (t + 1) * WIDTH]
        for out, start, end in ((expand, COL_E, COL_O), (output, COL_O, COL_S), (shrink, COL_S, COLS)):
            out[:, : end - start] = low[:, start:end]
            out[:, end - start :] = high[:, start:end]
        rows = (sum0[:, COLS:] + got0[:, COLS:]).T
        hid[...] = rows[at + 5 : at + 6, :]
        for t in range(3):
            bias[t : t + 1, :] = rows[at + 6 : at + 7, 16 * t : 16 * t + 16]

    @pl.when(core[0] == 0)
    def _():
        write(sum0, got0, 0)

    @pl.when(core[0] != 0)
    def _():
        write(got1, sum1, 8)


def write_boundary(core, gx, y, other, out):
    @pl.when(core[0] == 0)
    def _():
        out[:, :, :HALF] = gx[...]
        out[:, :, HALF:] = other[...]

    @pl.when(core[0] != 0)
    def _():
        out[:, :, :HALF] = other[...]
        out[:, :, HALF:] = y[...]


def shaped(*dims, dtype=BF16):
    return jax.ShapeDtypeStruct(dims, dtype)


def call(kernel, n_in, outs, scratch, flops, name, after=()):
    whole = pl.BlockSpec(memory_space=pltpu.VMEM)

    def body(*refs):
        kernel(*refs[:n_in], *refs[n_in + len(after) :])

    made = pl.pallas_call(
        body,
        in_specs=[pl.BlockSpec(memory_space=pltpu.SMEM)]
        + [whole] * (n_in - 1)
        + [pl.BlockSpec(memory_space=pl.ANY)] * len(after),
        out_specs=[whole] * len(outs),
        out_shape=outs,
        scratch_shapes=scratch,
        compiler_params=pltpu.CompilerParams(vmem_limit_bytes=60 * 2**20),
        cost_estimate=pl.CostEstimate(flops=flops, bytes_accessed=8 * 2**20, transcendentals=2**20),
        name=name,
    )
    return lambda *args: made(*args, *after)


ZERO = shaped(1, HALF // 2, dtype=F32)


def tall(width, dtype=BF16):
    return shaped(ROWS, width, dtype=dtype)


def forward_call(*args, after=()):
    outs = [tall(HALF), tall(HALF), tall(MODEL), tall(MODEL)]
    outs += [tall(WIDTH)] * 4 + [tall(WIDTH, F32), tall(INNER), tall(INNER), ZERO]
    return call(first_forward, len(args), outs, [], 2**31, "layer_forward", after)(*args)


def both_call(*args, after=()):
    outs = [tall(HALF)] * 4 + [tall(MODEL)] * 2 + [tall(WIDTH), tall(INNER), tall(QKV), tall(INNER)]
    outs += [shaped(8, MODEL, dtype=F32), ZERO]
    scratch = [pltpu.VMEM((ROWS, MODEL), BF16)] + [pltpu.VMEM((ROWS, WIDTH), BF16)] * 3
    scratch += [pltpu.VMEM((ROWS, WIDTH), F32), pltpu.VMEM((ROWS, INNER), F32)]
    scratch += [pltpu.VMEM((ROWS, WIDTH), BF16)] + [pltpu.VMEM((ROWS, WIDTH), F32)] * 3
    scratch += [pltpu.VMEM((ROWS, MODEL), F32), pltpu.VMEM((ROWS, 1), F32)]
    return call(both_ways, len(args), outs, scratch, 2**32, "layer_both", after)(*args)


def backward_call(*args, after=()):
    outs = [tall(HALF)] * 2 + [tall(QKV), tall(INNER), tall(MODEL), shaped(8, MODEL, dtype=F32), ZERO]
    scratch = [pltpu.VMEM((ROWS, WIDTH), BF16)] + [pltpu.VMEM((ROWS, WIDTH), F32)] * 3
    return call(first_backward, len(args), outs, scratch, 2**31, "layer_backward", after)(*args)


def grads_call(*args, sums=(), after=()):
    blocks = 4
    step = MODEL // blocks
    extra = 128 if sums else 0
    cut = pl.BlockSpec((ROWS, step), lambda i: (0, i))
    rest = [pl.BlockSpec(a.shape, lambda i: (0, 0)) for a in (*args[6:], *sums[1:])]
    n_in = len(args)
    n_all = n_in + len(sums) + len(after)

    def body(*refs):
        first = len(sums[:1])
        out, token, *rows = refs[n_all:]
        weight_grads(*refs[first : first + n_in], out)
        token[...] = jnp.zeros_like(token)
        if sums:
            rows = rows[0]

            @pl.when(pl.program_id(0) == 0)
            def _():
                rows[...] = jnp.zeros_like(rows)
                row_grads(refs[0], *refs[1 + n_in : 5 + n_in], rows)

            at = pl.multiple_of(pl.program_id(0) * step, step)
            out[:, COLS:] = rows[:, pl.ds(at, step)].T.astype(BF16)

    return pl.pallas_call(
        body,
        grid=(blocks,),
        in_specs=[pl.BlockSpec(memory_space=pltpu.SMEM)] * len(sums[:1])
        + [cut] * 6
        + rest
        + [pl.BlockSpec(memory_space=pl.ANY)] * len(after),
        out_specs=[
            pl.BlockSpec((step, COLS + extra), lambda i: (i, 0)),
            pl.BlockSpec(ZERO.shape, lambda i: (0, 0)),
        ],
        out_shape=[pltpu.HBM((MODEL, COLS + extra), BF16), ZERO],
        scratch_shapes=[pltpu.VMEM((128, MODEL), F32)] if sums else [],
        compiler_params=pltpu.CompilerParams(vmem_limit_bytes=60 * 2**20),
        cost_estimate=pl.CostEstimate(flops=2**32, bytes_accessed=2**23, transcendentals=0),
        name="weight_grads",
    )(*sums[:1], *args, *sums[1:], *after)


def gate(x, *after):
    anywhere = pl.BlockSpec(memory_space=pl.ANY)
    return pl.pallas_call(
        lambda *refs: None,
        in_specs=[anywhere] * (1 + len(after)),
        out_specs=anywhere,
        out_shape=shaped(*x.shape, dtype=x.dtype),
        input_output_aliases={0: 0},
        name="gate",
    )(x, *after)


def assemble(place, own, before, behind, far0, far1, out0, out1, *parts):
    step = own.shape[1]
    ring = ROWS // step

    def put(out, value, distance):
        at = lax.rem(place[0] + distance, ring) * step
        out[pl.ds(pl.multiple_of(at, step), step), :] = value

    for n, (out, far) in enumerate(((out0, far0), (out1, far1))):
        put(out, own[n], 0)
        put(out, before[n], ring - 1)
        put(out, behind[n], 1)
        put(out, far[...], 2)

    quarter = HALF // 2
    for core in range(2):

        @pl.when(place[1] == core)
        def _():
            for n, part in enumerate(parts):
                at = core * HALF + (n % 2) * quarter
                part[...] = (out0 if n < 2 else out1)[:, at : at + quarter]


def around_ring(x, by):
    ring = lax.axis_size("tensor")
    return lax.ppermute(x, "tensor", [(i, (i + by) % ring) for i in range(ring)])


def gathered_rows(x, place):
    before, behind = around_ring(x, 1), around_ring(x, -1)
    far0, far1 = around_ring(before[0], 1), around_ring(behind[1], -1)
    outs = [tall(MODEL)] * 2 + [tall(HALF // 2)] * 4
    args = (place, x, before, behind, far0, far1)
    out0, out1, *parts = call(assemble, 6, outs, [], 2**20, "assemble")(*args)
    return [out0, out1], [parts[:2], parts[2:]]


def add_blocks(offset, place, k0, g0, k1, g1, keep, send):
    step = keep.shape[2]
    ring = ROWS // step
    first = jnp.where(place[0] % 2 == offset, 1, ring - 1)
    for out, which in ((keep, (0, ring - first)), (send, (first, 2))):
        for n, distance in enumerate(which):
            at = lax.rem(place[0] + distance, ring) * step
            rows = pl.ds(pl.multiple_of(at, step), step)
            out[n, 0] = (k0[rows, :].astype(F32) + g0[rows, :].astype(F32)).astype(BF16)
            out[n, 1] = (k1[rows, :].astype(F32) + g1[rows, :].astype(F32)).astype(BF16)


def add_blocks_call(offset, place, keeps, gots):
    outs = [shaped(2, 2, ROWS // lax.axis_size("tensor"), HALF)] * 2
    args = (place, keeps[0], gots[0], keeps[1], gots[1])
    return call(functools.partial(add_blocks, offset), 5, outs, [], 2**20, "add_blocks")(*args)


def swap(x):
    return lax.ppermute(x, "pipe", [(0, 1), (1, 0)])


def along_ring(x, axis, offset, stride=1, side=4):
    pairs = []
    for g in range(lax.axis_size(axis)):
        at = (g // stride) % side
        to = (at + 1) % side if at % 2 == offset else (at - 1) % side
        pairs.append((g, g + (to - at) * stride))
    return lax.ppermute(x, axis, pairs)


def added(a, b, row=None):
    total = a.astype(F32) + b.astype(F32)
    return (total if row is None else total + row).astype(BF16)


def halves(a):
    return [a[:, : HALF // 2], a[:, HALF // 2 :]]


class SumOverTensor:
    def __init__(self, keep, send):
        self.chip = halves(added(keep, swap(send)))

    def second(self, zero=None):
        self.pair = [added(a, along_ring(a, "tensor", n), zero) for n, a in enumerate(self.chip)]

    def finish(self, base, rows, zero=None):
        mine = []
        for n, (a, b) in enumerate(zip(self.pair, base)):
            total = a.astype(F32) + along_ring(a, "tensor", 1 - n).astype(F32) + b.astype(F32)
            for row in (rows and rows[n], zero):
                total = total if row is None else total + row
            mine.append(total.astype(BF16))
        return (*mine, *[swap(a) for a in mine])


def summed_blocks(keeps, sends, place, offset, after):
    gots = [swap(gate(s, after)) for s in sends]
    keep, send = add_blocks_call(offset, place, keeps, gots)
    half = added(keep, along_ring(send, "tensor", offset))
    return half[0].astype(F32) + along_ring(half[1], "tensor", 1 - offset).astype(F32)


def rotary_tables(segment_row):
    places = jnp.arange(ROWS, dtype=jnp.int32)
    before = jnp.sum((segment_row[None, :] < segment_row[:, None]).astype(jnp.int32), axis=1)
    positions = (places - before).astype(F32)
    half_rot = ROTARY // 2
    lane = jnp.arange(WIDTH, dtype=jnp.int32)[None, :] % HEAD_DIM
    inverse = 10000.0 ** (-(lane % half_rot).astype(F32) * 2.0 / ROTARY)
    angles = positions[:, None] * inverse
    cosine, sine = jnp.cos(angles), jnp.sin(angles)
    c = jnp.where(lane < ROTARY, cosine, 1.0)
    s1 = jnp.where(lane < half_rot, -sine, 0.0)
    s2 = jnp.where((lane >= half_rot) & (lane < ROTARY), sine, 0.0)
    return jnp.stack([c, s1, s2])


def shards(
    inputs, upstream, segments, joint_weight, joint_bias, output_weight, expand_weight,
    expand_bias, shrink_weight, norm_gains, shift_rows,
):
    dp = lax.axis_size("dp")
    tensor = lax.axis_size("tensor")
    core = lax.axis_index("pipe")
    first = core == 0
    core_arg = core.astype(jnp.int32).reshape(1)
    micros = inputs.shape[0]
    own_d = MODEL // dp

    def pick(a, b):
        return jnp.where(first, a, b)

    def packed(h):
        return jnp.concatenate(
            [
                joint_weight[0][:, :, h * WIDTH : (h + 1) * WIDTH].reshape(own_d, QKV),
                expand_weight[0][:, h * INNER : (h + 1) * INNER],
                output_weight[0][h * WIDTH : (h + 1) * WIDTH].T,
                shrink_weight[0][h * INNER : (h + 1) * INNER].T,
            ],
            axis=1,
        )

    with jax.named_scope("weights"):
        pack_a, pack_b = packed(0), packed(1)
        stay = pick(pack_a, pack_b)
        came = swap(pick(pack_b, pack_a))
        w0 = lax.all_gather(pick(stay, came), "dp", axis=0, tiled=True)
        w1 = lax.all_gather(pick(came, stay), "dp", axis=0, tiled=True)

    with jax.named_scope("small_parameters"):
        bias_row = jnp.pad(joint_bias[0, :, 0, :].reshape(1, -1), ((0, 0), (0, own_d - 3 * 16)))
        small = jnp.concatenate([norm_gains[0], shift_rows[0], expand_bias[0], bias_row], axis=0)
        copies = jnp.broadcast_to(small, (2 * dp, *small.shape))
        small = lax.all_to_all(copies, ("pipe", "dp"), split_axis=0, concat_axis=0, tiled=True)
        small = small.reshape(2, dp, 8, own_d).astype(F32)
        rows = small.transpose(0, 2, 1, 3).reshape(2, 8, MODEL)
        be = [pick(rows[n, 6:7, :INNER], rows[n, 6:7, INNER:]) for n in range(2)]
        bq_all = small[:, :, 7, :48].reshape(2, dp, 3, 16).transpose(0, 2, 1, 3).reshape(2, 3, 256)
        bq = [
            pick(bq_all[n, :, :WIDTH], bq_all[n, :, WIDTH:]).reshape(1, QKV) for n in range(2)
        ]
        shift_own = [pick(rows[n, :, :HALF], rows[n, :, HALF:]) for n in range(2)]

    place = lax.axis_index("tensor").astype(jnp.int32).reshape(1)
    with jax.named_scope("activations_in"):
        both_places = jnp.concatenate([place, core_arg])
        x0, x0_half = gathered_rows(inputs, both_places)
        gy1, gy1_half = gathered_rows(upstream, both_places)

    with jax.named_scope("tables"):
        tabs = [rotary_tables(segments[m]) for m in range(micros)]
        seg_col = [segments[m].reshape(ROWS, 1) for m in range(micros)]
        seg_row = [segments[m].reshape(1, ROWS) for m in range(micros)]

    kept, sums0 = [], []
    after = (*tabs, *gy1)
    for m in range(micros):
        with jax.named_scope("first_layer"):
            keep, send, *saved, zero = forward_call(
                core_arg, x0[m], w0, rows[0], bq[0], be[0], tabs[m], seg_col[m], seg_row[m], after=after
            )
            if m:
                sums0[0].second(zero)
                send = gate(send, *sums0[0].pair)
            sums0.append(SumOverTensor(keep, send))
            after = tuple(sums0[m].chip)
            kept.append(saved)
    sums0[1].second()

    x1, made1, y_parts, sums1 = [], [], [], []
    shift = halves(shift_own[0][4:5] + shift_own[0][5:6])
    for m in range(micros):
        with jax.named_scope("second_layer"):
            if m == 0:
                x1.append(sums0[0].finish(x0_half[0], shift))
                after = tuple(sums0[1].pair)
            else:
                after = tuple(sums1[0].chip)
            keep_y, send_y, keep_g, send_g, *made, zero = both_call(
                core_arg, *x1[m], gy1[m], w1, rows[1], bq[1], be[1], tabs[m], seg_col[m], seg_row[m],
                after=after,
            )
            if m == 0:
                x1.append(sums0[1].finish(x0_half[1], shift, zero))
            else:
                sums1[0].second(zero)
                send_g = gate(send_g, *sums1[0].pair)
            sums1.append(SumOverTensor(keep_g, send_g))
            y_parts.append((keep_y, send_y))
            made1.append(made)

    def pairs(made, n):
        return [made[m][n] for m in range(micros)]

    with jax.named_scope("second_layer_grads"):
        args = []
        for n in (0, 1, None, 4, 5, 2, 3):
            args += gy1 if n is None else pairs(made1, n)
        grads1, zero = grads_call(*args, after=(*sums1[1].chip, *sums1[0].pair))
        g0 = [sums1[0].finish(gy1_half[0], None, zero)]
        sums1[1].second(zero)
        tiles1 = gate(grads1.reshape(dp, own_d, -1), *g0[0][:2])
        arrived1 = lax.all_to_all(tiles1, "dp", split_axis=0, concat_axis=0, tiled=True)

    made0, g_parts = [], []
    after = tuple(sums1[1].pair)
    for m in range(micros):
        with jax.named_scope("first_layer_back"):
            if m:
                g0.append(sums1[m].finish(gy1_half[m], None, zero))
            normed, mixed, q, k, v, att, lse, active, slope = kept[m]
            keep_g, send_g, gjoint, ghid, gy, sums, zero = backward_call(
                core_arg, x0[m], *g0[m], w0, rows[0], tabs[m], seg_col[m], seg_row[m],
                q, k, v, lse, slope, after=after,
            )
            after = (sums,)
            g_parts.append((keep_g, send_g))
            made0.append((normed, mixed, att, active, gjoint, ghid, sums, gy))

    with jax.named_scope("first_layer_grads"):
        args = []
        for n in (0, 1, 7, 4, 5, 2, 3):
            args += pairs(made0, n)
        sums = (core_arg, made0[0][6], made0[1][6], made1[0][6], made1[1][6])
        grads0, _ = grads_call(*args, sums=sums)
        tiles0 = gate(grads0.reshape(dp, own_d, -1), arrived1)
        arrived0 = lax.all_to_all(tiles0, "dp", split_axis=0, concat_axis=0, tiled=True)

    with jax.named_scope("boundary"):

        def own_rows(parts):
            step = ROWS // tensor
            return jnp.stack(
                [
                    lax.dynamic_slice_in_dim(jnp.concatenate(a[:2], axis=1), place[0] * step, step, 0)
                    for a in parts
                ]
            ).astype(F32)

        gx_all = summed_blocks(*zip(*g_parts), place, 0, tiles0) + own_rows(g0)
        y_all = summed_blocks(*zip(*y_parts), place, 1, tiles0) + own_rows(x1)
        y_all = y_all + (shift_own[1][4:5] + shift_own[1][5:6])
        other = swap(pick(y_all, gx_all))
        outs = [shaped(2, ROWS // tensor, MODEL, dtype=F32)]
        args = (core_arg, gx_all, y_all, other)
        boundary = call(write_boundary, 4, outs, [], 2**20, "write_boundary")(*args)[0][None]

    with jax.named_scope("outputs"):
        sum1 = sum_tiles_call(arrived1, (tiles0,))
        got1 = lax.ppermute(sum1, "pipe", [(0, 1)])
        sum0 = sum_tiles_call(arrived0, (other, got1))
        got0 = swap(sum0)
        both = sum0[:, COLS:] + got0[:, COLS:]
        total = pick(both[:, :4], both[:, 8:12]).T
        for offset in (0, 1):
            total = total + along_ring(total, "tensor", offset)
        gy_sum = pick(sum0[:, COLS + 4], sum0[:, COLS + 12])
        outs = [(3, own_d, 2 * WIDTH), (own_d, 2 * INNER), (own_d, 2 * WIDTH), (own_d, 2 * INNER)]
        outs += [(1, own_d), (3, 16)]
        outs = [shaped(*dims, dtype=F32) for dims in outs]
        args = (core_arg, sum0, got0, sum1, got1)
        made = call(write_out, 5, outs, [], 2**20, "write_out")(*args)
        gains = total[None, 0:2]
        shift = jnp.stack([total[2], total[3], gy_sum, gy_sum])[None]
        joint = made[0].transpose(1, 0, 2)[None]
        expand = made[1][None]
        output, shrink = made[2].T[None], made[3].T[None]
        expand_bias_grad = made[4].reshape(1, 1, own_d)
        joint_bias_grad = made[5].reshape(1, 3, 1, 16)

    return (
        boundary,
        joint,
        joint_bias_grad,
        output,
        expand,
        expand_bias_grad,
        shrink,
        gains,
        shift,
    )


def solution(mesh):
    placed = (
        P(None, ("dp", "tensor"), None),
        P(None, ("dp", "tensor"), None),
        P(None, "dp"),
        P("pipe", "dp", None, "tensor"),
        P("pipe", None, "tensor", "dp"),
        P("pipe", "tensor", "dp"),
        P("pipe", "dp", "tensor"),
        P("pipe", "tensor", "dp"),
        P("pipe", "tensor", "dp"),
        P("pipe", None, "dp"),
        P("pipe", None, "dp"),
    )
    return jax.shard_map(
        shards,
        mesh=mesh,
        in_specs=placed,
        out_specs=(
            P("pipe", None, ("dp", "tensor"), None),
            P("pipe", "dp", None, "tensor"),
            P("pipe", None, "tensor", "dp"),
            P("pipe", "tensor", "dp"),
            P("pipe", "dp", "tensor"),
            P("pipe", "tensor", "dp"),
            P("pipe", "tensor", "dp"),
            P("pipe", None, "dp"),
            P("pipe", None, "dp"),
        ),
        check_vma=False,
    )
```
